32 devices in a mesh: dp: 8 (over z, x), seq: 4 (over y, core).
Axes of the slice: x: 2, y: 2, z: 4, core: 2. Of those that a mesh axis runs over, the one named last changes fastest.
Arguments:
- states: float32 [32, 256, 768], P('dp', 'seq'), may hold values from -6 to 6
- item_halves: int32 [32], P('dp'), may hold values from 0 to 1, as said below
- ln1_gain: float32 [2, 768], P(None, ('dp', 'seq')), may hold values from 0.1 to 1.9
- qkv_weight: float32 [2, 768, 2304], P(None, ('dp', 'seq')), may hold values from -0.21875 to 0.21875
- out_weight: float32 [2, 768, 768], P(None, ('dp', 'seq')), may hold values from -1.75 to 1.75
- ln2_gain: float32 [2, 768], P(None, ('dp', 'seq')), may hold values from 0.1 to 1.9
- up_weight: float32 [2, 768, 3072], P(None, ('dp', 'seq')), may hold values from -0.21875 to 0.21875
- down_weight: float32 [2, 3072, 768], P(None, ('dp', 'seq')), may hold values from -0.109375 to 0.109375
- cotangent: float32 [32, 256, 768], P('dp', 'seq'), may hold values from -6 to 6
Outputs:
- outputs: float32 [32, 256, 768], P('dp', 'seq')
- grad_states: float32 [32, 256, 768], P('dp', 'seq')
- grad_ln1_gain: float32 [2, 768], P(None, ('dp', 'seq'))
- grad_qkv_weight: float32 [2, 768, 2304], P(None, ('dp', 'seq'))
- grad_out_weight: float32 [2, 768, 768], P(None, ('dp', 'seq'))
- grad_ln2_gain: float32 [2, 768], P(None, ('dp', 'seq'))
- grad_up_weight: float32 [2, 768, 3072], P(None, ('dp', 'seq'))
- grad_down_weight: float32 [2, 3072, 768], P(None, ('dp', 'seq'))
The draws below stay inside these ranges and needn't reach their ends.
Inputs may be any that keep to these rules, and one draw needn't show every extreme that they name: `item_halves`: 1 marks a block of 256 positions holding two items of 128 tokens each, 0 a block holding one item of 256 tokens; each aligned run of 4 blocks holds at least one block of each kind.
All inputs are finite; a program needn't handle non-finite values.
Results may differ from the reference program's by a relative error of at most 0.02.
The reference program's roundings to bfloat16 on the way count: a program that leaves them out, or rounds other values in their place, can miss the bound.
Values may be sent and summed in bfloat16 or wider, within the bound.
No kernel may reach another device: no remote copies, remote signals or barrier semaphores. Data moves between devices by JAX's collectives and lax.ppermute only.
A program may use at most 256 MiB of HBM per device.

```python
import jax
import jax.numpy as jnp
from jax import lax

D = 768
HEADS = 12
HEAD_DIM = 64
FF = 3072
LAYERS = 2
SPAN = 256
BLK_GROUP = 4
BLOCKS = 32


def draw_item_halves(key, part):
    key = jax.random.fold_in(key, 11)
    key_flags, key_choice = jax.random.split(key)
    groups = BLOCKS // BLK_GROUP
    block_flags = jax.random.randint(key_flags, (groups, BLK_GROUP), 0, 2)
    chosen = jax.random.randint(key_choice, (groups, 1), 0, BLK_GROUP)
    column = jnp.arange(BLK_GROUP)[None, :]
    block_flags = jnp.where(column == chosen, 0, block_flags)
    block_flags = jnp.where(column == (chosen + 1) % BLK_GROUP, 1, block_flags)
    return block_flags.reshape(BLOCKS).astype(jnp.int32)


def level_of(rng, dims, cuts, smallest, top_value):
    loudness, own = 1.0, jax.random.fold_in(rng, 6)
    for axis_at, shards_of in cuts:
        steps = jnp.exp(jax.random.uniform(jax.random.fold_in(own, axis_at), (shards_of,), jnp.float32, smallest / len(cuts), top_value / len(cuts)))
        loudness = loudness * jnp.repeat(steps, dims[axis_at] // shards_of).reshape([-1 if axis == axis_at else 1 for axis in range(len(dims))])
    return loudness


def normal_values(stream_key, extent, width, reach, cuts=(), kind=jnp.bfloat16):
    loudness = level_of(stream_key, extent, cuts, -0.22, 0.18) if cuts else 1.0
    array = jax.random.normal(stream_key, extent, jnp.float32) * width * loudness
    return jnp.minimum(jnp.maximum(array, -reach), reach).astype(kind)


def setup_inputs(seed: int = 0) -> dict:
    arg_keys = jax.random.split(jax.random.key(seed), 10)
    return {
        "states": normal_values(arg_keys[0], (BLOCKS, SPAN, D), 1.0, 6.0, ((0, 8), (1, 4)), jnp.float32),
        "item_halves": draw_item_halves(jax.random.fold_in(arg_keys[9], 71), 0),
        "ln1_gain": jnp.clip(1.0 + 0.18 * jax.random.normal(arg_keys[2], (LAYERS, D), jnp.float32), 0.1, 1.9),
        "qkv_weight": normal_values(arg_keys[3], (LAYERS, D, 3 * D), D ** -0.5, 0.21875, ((1, 32),), jnp.float32),
        "out_weight": normal_values(arg_keys[4], (LAYERS, D, D), (4 * D // SPAN) ** -0.5, 1.75, ((1, 32),), jnp.float32),
        "ln2_gain": jnp.clip(1.0 + 0.18 * jax.random.normal(arg_keys[5], (LAYERS, D), jnp.float32), 0.1, 1.9),
        "up_weight": normal_values(arg_keys[6], (LAYERS, D, FF), D ** -0.5, 0.21875, ((1, 32),), jnp.float32),
        "down_weight": normal_values(arg_keys[7], (LAYERS, FF, D), FF ** -0.5, 0.109375, ((1, 32),), jnp.float32),
        "cotangent": normal_values(arg_keys[8], (BLOCKS, SPAN, D), 1.0, 6.0, ((0, 8), (1, 4)), jnp.float32),
    }


@jax.custom_vjp
def low(v):
    return lax.optimization_barrier(v.astype(jnp.bfloat16)).astype(jnp.float32)

@jax.custom_vjp
def low_back(v):
    return v

def low_keep(v):
    return (low(v), None)

def low_pass(kept, grad):
    return (grad,)

def back_keep(v):
    return (v, None)

def back_low(kept, grad):
    return (low(grad),)
low.defvjp(low_keep, low_pass)
low_back.defvjp(back_keep, back_low)
HIGHEST = lax.Precision.HIGHEST

def normalize(values_in):
    average = lax.optimization_barrier(jnp.mean(values_in, -1, keepdims=True))
    centered = values_in - average
    variance = lax.optimization_barrier(jnp.mean(centered * centered, -1, keepdims=True))
    return centered * lax.rsqrt(variance + 1e-05)

def attend(queries, key_heads, value_heads, item_halves):
    length = queries.shape[1]
    scores = jnp.einsum('bqhe,bkhe->bhqk', queries, key_heads, precision=HIGHEST) * HEAD_DIM ** (-0.5)
    scores = low_back(scores)
    position = jnp.arange(length)
    same_half = position[:, None] // (length // 2) == position[None, :] // (length // 2)
    allowed = jnp.logical_or(item_halves[:, None, None] == 0, same_half[None])[:, None]
    attention = jax.nn.softmax(jnp.where(allowed, scores, -1e+30), axis=-1)
    return jnp.einsum('bhqk,bkhe->bqhe', low(attention), value_heads, precision=HIGHEST)

def layer(residual, item_halves, gain_one, w_qkv, w_out, gain_two, w_up, w_down):
    blocks = residual.shape[0]
    hidden_one = low(normalize(residual) * low(gain_one))
    mixed_qkv = jnp.einsum('bsd,de->bse', hidden_one, low(w_qkv), precision=HIGHEST)
    mixed_qkv = low(low_back(mixed_qkv))
    heads = mixed_qkv.reshape(blocks, SPAN, 3, HEADS, HEAD_DIM)
    attended = attend(heads[:, :, 0], heads[:, :, 1], heads[:, :, 2], item_halves)
    attended = low(low_back(attended.reshape(blocks, SPAN, D)))
    branch = low_back(jnp.einsum('bsd,de->bse', attended, low(w_out), precision=HIGHEST))
    middle = residual + branch
    hidden_two = low(normalize(middle) * low(gain_two))
    pre_act = low_back(jnp.einsum('bsd,df->bsf', hidden_two, low(w_up), precision=HIGHEST))
    activated = low(jax.nn.gelu(pre_act, approximate=False))
    return middle + low_back(jnp.einsum('bsf,fd->bsd', activated, low(w_down), precision=HIGHEST))

def forward(weight_set, residual, item_halves):
    current = residual
    for layer_index in range(LAYERS):
        current = layer(current, item_halves, *[member[layer_index] for member in weight_set])
    return current

def reference(states, item_halves, ln1_gain, qkv_weight, out_weight, ln2_gain, up_weight, down_weight, cotangent):
    weight_set = (ln1_gain, qkv_weight, out_weight, ln2_gain, up_weight, down_weight)
    groups = BLOCKS // BLK_GROUP

    def one_group(totals, pieces):
        group_states, group_halves, group_cot = pieces

        def local_forward(weights_in, states_in):
            return forward(weights_in, states_in, group_halves)
        result, pullback = jax.vjp(local_forward, weight_set, group_states)
        grad_weights, grad_input = pullback(group_cot)
        totals = tuple((running + increment for running, increment in zip(totals, grad_weights)))
        return (totals, (result, grad_input))
    zeros_init = tuple((jnp.zeros_like(member) for member in weight_set))
    pieces = (states.reshape(groups, BLK_GROUP, SPAN, D), item_halves.reshape(groups, BLK_GROUP).astype(jnp.int32), cotangent.reshape(groups, BLK_GROUP, SPAN, D))
    totals, (results, grad_inputs) = lax.scan(one_group, zeros_init, pieces)
    return (results.reshape(BLOCKS, SPAN, D), grad_inputs.reshape(BLOCKS, SPAN, D), totals[0], totals[1], totals[2], totals[3], totals[4], totals[5])
```

```python
import jax
import jax.numpy as jnp
from jax import lax
from jax.experimental import pallas as pl
from jax.experimental.pallas import tpu as pltpu
from jax.sharding import PartitionSpec as P

HEAD_DIM = 64
EPSILON = 1e-05
BF = jnp.bfloat16
F32 = jnp.float32
LINES = ("dp", "seq")
WIDE = 384
DEEP = 192
GAIN_ROWS = 16
VMEM = pl.BlockSpec(memory_space=pltpu.VMEM)
SMEM = pl.BlockSpec(memory_space=pltpu.SMEM)
HBM = pl.BlockSpec(memory_space=pl.ANY)


def call(body, ins, outs, specs, out_specs, scratch, flops, size, limit=58):
    return pl.pallas_call(
        body,
        out_shape=outs,
        in_specs=specs,
        out_specs=out_specs,
        scratch_shapes=scratch,
        cost_estimate=pl.CostEstimate(
            flops=flops, bytes_accessed=6 * size, transcendentals=0
        ),
        compiler_params=pltpu.CompilerParams(vmem_limit_bytes=limit * 1024 * 1024),
    )(*ins)


def shape(dims, dtype):
    return jax.ShapeDtypeStruct(dims, dtype)


def mat(a, b):
    return jnp.dot(a, b, preferred_element_type=F32)


def mat_t(a, b):
    return lax.dot_general(a, b, (((1,), (1,)), ((), ())), preferred_element_type=F32)


def t_mat(a, b):
    return lax.dot_general(a, b, (((0,), (0,)), ((), ())), preferred_element_type=F32)


def normed(v):
    average = jnp.mean(v, -1, keepdims=True)
    centered = v - average
    variance = jnp.mean(centered * centered, -1, keepdims=True)
    root = lax.rsqrt(variance + EPSILON)
    return centered * root, root


def norm_back(n, root, g):
    return root * (
        g - jnp.mean(g, -1, keepdims=True) - n * jnp.mean(g * n, -1, keepdims=True)
    )


def bell(u):
    return 0.5 * (1.0 + lax.erf(u * 0.7071067811865476))


def place(pieces, where_to, cuts):
    count = len(pieces)

    def body(to, *refs):
        for k in range(count):
            for (start, rows), out in zip(cuts, refs[count:]):
                out[to[k]] = refs[k][start : start + rows]

    one = pieces[0]
    return call(
        body,
        [where_to, *pieces],
        [shape((count, rows, one.shape[1]), one.dtype) for _, rows in cuts],
        [SMEM] + [VMEM] * count,
        [VMEM] * len(cuts),
        [],
        0,
        2 * count * one.size * one.dtype.itemsize,
        limit=16,
    )


def combine(meta, arrays, outs, tasks, after=()):
    count = len(arrays)
    terms = [(rows, term) for _, _, rows, sources in tasks for term in sources]

    def body(meta, *refs):
        ins, results, held = refs[:count], refs[count : count + len(outs)], refs[count + len(outs) : -1]
        sems = refs[-1]
        copies = [
            pltpu.make_async_copy(view(meta, ins[place_of]), held[k], sems.at[k])
            for k, (_, (place_of, view)) in enumerate(terms)
        ]
        start_all(copies)
        k = 0
        for result, first, rows, sources in tasks:
            wait_all(copies[k : k + len(sources)])
            step = 64 if rows % 64 == 0 else 16

            def some(r, _, k=k, result=result, first=first, step=step, sources=sources):
                at = pl.multiple_of(r * step, 16)
                total = sum(held[k + j][pl.ds(at, step)].astype(F32) for j in range(len(sources)))
                to = pl.multiple_of(first + at, 16)
                results[result][pl.ds(to, step)] = total.astype(results[result].dtype)
                return 0

            lax.fori_loop(0, rows // step, some, 0)
            k += len(sources)

    arrays = [tie(arrays[0], *after), *arrays[1:]]
    return call(
        body,
        [meta, *arrays],
        [shape((rows, WIDE), kind) for rows, kind in outs],
        [SMEM] + [HBM] * count,
        [VMEM] * len(outs),
        [pltpu.VMEM((rows, WIDE), arrays[term[0]].dtype) for rows, term in terms]
        + [pltpu.SemaphoreType.DMA((len(terms),))],
        0,
        60_000_000,
    )


class Tasks:
    def __init__(self, outs):
        self.arrays, self.tasks, self.rows, self.kinds = [], [], [0] * outs, [BF] * outs

    def add(self, out, rows, *terms):
        sources = []
        for array, view in terms:
            known = [k for k, v in enumerate(self.arrays) if v is array]
            if not known:
                self.arrays.append(array)
            sources.append((known[0] if known else len(self.arrays) - 1, view))
        first = self.rows[out]
        self.tasks.append((out, first, rows, sources))
        self.rows[out] += rows
        return first

    def run(self, meta, after=()):
        return combine(meta, self.arrays, list(zip(self.rows, self.kinds)), self.tasks, after)


def chip_row(meta, i):
    return (meta[0] ^ (i & 1)) * 2 + (meta[1] ^ (i >> 1))


def columns(meta, side, half, q):
    start = (meta[2] ^ side) * half + WIDE * q
    return pl.ds(pl.multiple_of(start, 128), WIDE)


def piece_at(pieces, i, start, rows):
    if len(pieces) == 2:
        half = start // (DEEP // 2)
        return pieces[half].at[i, :, pl.ds(start - half * (DEEP // 2), rows), :]
    if i == 3 and len(pieces) == 5:
        cut = pieces[3].shape[1]
        if start >= cut:
            return pieces[4].at[:, pl.ds(start - cut, rows), :]
    return pieces[i].at[:, pl.ds(start, rows), :]


def chunked(meta, sides, target, sems, first, chunks, to_pieces=False, split=1):
    half = target.shape[-1] // 2
    rows = target.shape[2]
    step = rows // split
    whole = not isinstance(sides, (list, tuple))
    copies = []
    for side in range(2):
        for i in range(4):
            for q in range(chunks):
                for k in range(split):
                    start = first + rows * q + step * k
                    if whole:
                        a = sides.at[:, i, side, pl.ds(start, step), :]
                        place_of, lanes = i, pl.ds(side * half + WIDE * q, WIDE)
                    else:
                        a = piece_at(sides[side], i, start, step)
                        place_of, lanes = chip_row(meta, i), columns(meta, side, half, q)
                    b = target.at[:, place_of, pl.ds(step * k, step), lanes]
                    pair = (b, a) if to_pieces else (a, b)
                    copies.append(pltpu.make_async_copy(*pair, sems.at[len(copies)]))
    return copies


def pieces_of_refs(refs):
    count = len(refs)
    return refs[0] if count == 1 else (refs[: count // 2], refs[count // 2 :])


def start_all(copies):
    for copy in copies:
        copy.start()


def wait_all(copies):
    for copy in copies:
        copy.wait()


def attention_bias(flag, length):
    row = lax.broadcasted_iota(jnp.int32, (length, length), 0) // (length // 2)
    column = lax.broadcasted_iota(jnp.int32, (length, length), 1) // (length // 2)
    return jnp.where(jnp.logical_or(row == column, flag == 0), 0.0, -1e30)


def probabilities(queries, keys, bias):
    s = mat_t(queries, keys) * HEAD_DIM ** (-0.5) + bias
    e = jnp.exp(s - jnp.max(s, -1, keepdims=True))
    return e * (1.0 / jnp.sum(e, -1, keepdims=True))


def head_lanes():
    return lax.broadcasted_iota(jnp.int32, (1, 2 * HEAD_DIM), 1) // HEAD_DIM


def only(lanes, j, v):
    return jnp.where(lanes == j, v, jnp.zeros_like(v))


def tile(ref, t, width):
    z, xy, rows, _ = ref.shape
    return ref[:, :, :, t * width : (t + 1) * width].reshape(z * xy * rows, width)


def attend_forward(meta, x, gain, pieces):
    count = len(pieces)
    length, width = x.shape
    pairs = width // (2 * HEAD_DIM)

    def body(meta, x_ref, gain_ref, *refs):
        src = pieces_of_refs(refs[:count])
        qkv_ref, o_ref, m_ref, wqkv, wo, sems_a, sems_b = refs[count:]
        load_a = chunked(meta, src, wqkv, sems_a, 0, 3)
        load_b = chunked(meta, src, wo, sems_b, width * 3 // 16, 1)
        start_all(load_a)
        start_all(load_b)
        bias = attention_bias(meta[3], length)
        n, _ = normed(x_ref[...])
        hidden = (n * gain_ref[...]).astype(BF)
        wait_all(load_a)
        for t in range(3):
            qkv_ref[:, t * width : (t + 1) * width] = mat(hidden, tile(wqkv, t, width)).astype(BF)
        lanes = head_lanes()

        def pair(p, _):
            take = lambda part: qkv_ref[
                :, pl.ds(pl.multiple_of(part * width + p * 2 * HEAD_DIM, 128), 2 * HEAD_DIM)
            ]
            q, k, v = take(0), take(1), take(2)
            outs = [
                mat(probabilities(only(lanes, j, q), k, bias).astype(BF), v) for j in range(2)
            ]
            o_ref[:, pl.ds(pl.multiple_of(p * 2 * HEAD_DIM, 128), 2 * HEAD_DIM)] = jnp.where(
                lanes == 0, outs[0], outs[1]
            ).astype(BF)
            return 0

        lax.fori_loop(0, pairs, pair, 0)
        wait_all(load_b)
        m_ref[...] = x_ref[...] + mat(o_ref[...], tile(wo, 0, width))

    return call(
        body,
        [meta, x, gain, *pieces],
        (shape((length, 3 * width), BF), shape((length, width), BF), shape((length, width), F32)),
        [SMEM, VMEM, VMEM] + [HBM] * count,
        (VMEM,) * 3,
        [
            pltpu.VMEM((4, 4, width // 16, 3 * width), BF),
            pltpu.VMEM((4, 4, width // 16, width), BF),
            pltpu.SemaphoreType.DMA((24,)),
            pltpu.SemaphoreType.DMA((8,)),
        ],
        2 * length * width * width * 4 + 4 * length * length * width * 2,
        36_000_000,
    )


def feed_forward(meta, m, gain, pieces):
    count = len(pieces)
    length, width = m.shape
    wide = 4 * width

    def body(meta, m_ref, gain_ref, *refs):
        src = pieces_of_refs(refs[:count])
        u_ref, a_ref, y_ref, wu, wd, sems_a, sems_b = refs[count:]
        load_a = chunked(meta, src, wu, sems_a, 0, 4)
        load_b = chunked(meta, src, wd, sems_b, width // 4, 1)
        start_all(load_a)
        start_all(load_b)
        n, _ = normed(m_ref[...])
        hidden = (n * gain_ref[...]).astype(BF)
        wait_all(load_a)
        wait_all(load_b)
        total = m_ref[...]
        for t in range(4):
            u = mat(hidden, tile(wu, t, width))
            u_ref[:, t * width : (t + 1) * width] = u
            a = (u * bell(u)).astype(BF)
            a_ref[:, t * width : (t + 1) * width] = a
            total = total + mat(a, wd[t].reshape(width, width))
        y_ref[...] = total

    return call(
        body,
        [meta, m, gain, *pieces],
        (shape((length, wide), F32), shape((length, wide), BF), shape((length, width), F32)),
        [SMEM, VMEM, VMEM] + [HBM] * count,
        (VMEM,) * 3,
        [
            pltpu.VMEM((4, 4, width // 16, wide), BF),
            pltpu.VMEM((4, 4, width // 4, width), BF),
            pltpu.SemaphoreType.DMA((32,)),
            pltpu.SemaphoreType.DMA((8,)),
        ],
        2 * length * width * wide * 2,
        26_000_000,
    )


def piece_shapes(rows):
    return (shape((4, 4, rows, WIDE), BF),) * 4


def whole_shape():
    return shape((4, 4, 2, 2 * DEEP, WIDE), BF)


def down_backward(meta, dy, a):
    length, width = dy.shape

    def body(meta, dy_ref, a_ref, *refs):
        *outs, stage, sems = refs
        low = dy_ref[...].astype(BF)
        for t in range(4):
            stage[t] = (
                t_mat(a_ref[:, t * width : (t + 1) * width], low)
                .astype(BF)
                .reshape(4, width // 4, width)
            )
        copies = chunked(meta, (outs[:2], outs[2:]), stage, sems, 0, 1, True, 2)
        start_all(copies)
        wait_all(copies)

    outs = piece_shapes(DEEP // 2)
    return call(
        body,
        [meta, dy, a],
        outs,
        [SMEM, VMEM, VMEM],
        (HBM,) * len(outs),
        [pltpu.VMEM((4, 4, width // 4, width), BF), pltpu.SemaphoreType.DMA((16,))],
        8 * length * width * width,
        13_000_000,
    )


def feed_backward(meta, dy, m, u, gain, pieces):
    count = len(pieces)
    length, width = m.shape
    wide = 4 * width

    def body(meta, dy_ref, m_ref, u_ref, gain_ref, *refs):
        src = pieces_of_refs(refs[:count])
        dm_ref, gg_ref, *outs = refs[count:-5]
        wu, wd, stage, sems_a, sems_b = refs[-5:]
        outs = outs[:2], outs[2:]
        load_a = chunked(meta, src, wu, sems_a, 0, 4)
        load_b = chunked(meta, src, wd, sems_b, width // 4, 1)
        start_all(load_b)
        start_all(load_a)
        n, root = normed(m_ref[...])
        gain = gain_ref[...]
        hidden_t = (n * gain).astype(BF).T
        low = dy_ref[...].astype(BF)
        wait_all(load_b)
        wait_all(load_a)
        dh = jnp.zeros((length, width), F32)
        for t in range(4):
            da = mat_t(low, wd[t].reshape(width, width))
            u = u_ref[:, t * width : (t + 1) * width]
            slope = bell(u) + u * (jnp.exp(-0.5 * u * u) * 0.3989422804014327)
            du = (da * slope).astype(BF)
            stage[:, :, :, t * width : (t + 1) * width] = (
                mat(hidden_t, du).astype(BF).reshape(4, 4, width // 16, width)
            )
            dh = dh + mat_t(du, tile(wu, t, width))
        store = chunked(meta, outs, stage, sems_a, 0, 4, True)
        start_all(store)
        gg_ref[...] = jnp.sum(dh * n, 0, keepdims=True)
        dm_ref[...] = dy_ref[...] + norm_back(n, root, dh * gain)
        wait_all(store)

    return call(
        body,
        [meta, dy, m, u, gain, *pieces],
        (shape((length, width), F32), shape((1, width), F32)) + piece_shapes(DEEP // 2),
        [SMEM] + [VMEM] * 4 + [HBM] * count,
        (VMEM, VMEM) + (HBM,) * 4,
        [
            pltpu.VMEM((4, 4, width // 16, wide), BF),
            pltpu.VMEM((4, 4, width // 4, width), BF),
            pltpu.VMEM((4, 4, width // 16, wide), BF),
            pltpu.SemaphoreType.DMA((32,)),
            pltpu.SemaphoreType.DMA((8,)),
        ],
        2 * length * width * wide * 3,
        40_000_000,
    )


def feed_both(meta, m, dy, gain, pieces):
    length, width = m.shape
    wide = 4 * width
    count = len(pieces)

    def body(meta, m_ref, dy_ref, gain_ref, *refs):
        src = pieces_of_refs(refs[:count])
        y_ref, dm_ref, gg_ref, whole = refs[count : count + 4]
        wu, wd, a_ref, slope_ref, stage_u, stage_d, sems_a, sems_b, sems_c, sems_d = refs[count + 4 :]
        load_a = chunked(meta, src, wu, sems_a, 0, 4)
        load_b = chunked(meta, src, wd, sems_b, width // 4, 1)
        start_all(load_a)
        start_all(load_b)
        n, root = normed(m_ref[...])
        gain = gain_ref[...]
        hidden = (n * gain).astype(BF)
        hidden_t = (n * gain).astype(BF).T
        low = dy_ref[...].astype(BF)
        wait_all(load_a)
        for t in range(4):
            u = mat(hidden, tile(wu, t, width))
            share = bell(u)
            a = (u * share).astype(BF)
            a_ref[:, t * width : (t + 1) * width] = a
            slope_ref[:, t * width : (t + 1) * width] = share + u * (
                jnp.exp(-0.5 * u * u) * 0.3989422804014327
            )
            stage_d[t] = t_mat(a, low).astype(BF).reshape(4, width // 4, width)
        store_d = chunked(meta, whole, stage_d, sems_d, DEEP, 1, True)
        start_all(store_d)
        wait_all(load_b)
        dh = jnp.zeros((length, width), F32)
        for t in range(4):
            da = mat_t(low, wd[t].reshape(width, width))
            du = (da * slope_ref[:, t * width : (t + 1) * width]).astype(BF)
            stage_u[:, :, :, t * width : (t + 1) * width] = (
                mat(hidden_t, du).astype(BF).reshape(4, 4, width // 16, width)
            )
            dh = dh + mat_t(du, tile(wu, t, width))
        store_u = chunked(meta, whole, stage_u, sems_c, 0, 4, True)
        start_all(store_u)
        gg_ref[...] = jnp.sum(dh * n, 0, keepdims=True)
        dm_ref[...] = dy_ref[...] + norm_back(n, root, dh * gain)
        total = m_ref[...]
        for t in range(4):
            total = total + mat(a_ref[:, t * width : (t + 1) * width], wd[t].reshape(width, width))
        y_ref[...] = total
        wait_all(store_d)
        wait_all(store_u)

    return call(
        body,
        [meta, m, dy, gain, *pieces],
        (
            shape((length, width), F32),
            shape((length, width), F32),
            shape((1, width), F32),
            whole_shape(),
        ),
        [SMEM] + [VMEM] * 3 + [HBM] * count,
        (VMEM, VMEM, VMEM, HBM),
        [
            pltpu.VMEM((4, 4, width // 16, wide), BF),
            pltpu.VMEM((4, 4, width // 4, width), BF),
            pltpu.VMEM((length, wide), BF),
            pltpu.VMEM((length, wide), F32),
            pltpu.VMEM((4, 4, width // 16, wide), BF),
            pltpu.VMEM((4, 4, width // 4, width), BF),
            pltpu.SemaphoreType.DMA((32,)),
            pltpu.SemaphoreType.DMA((8,)),
            pltpu.SemaphoreType.DMA((32,)),
            pltpu.SemaphoreType.DMA((8,)),
        ],
        2 * length * width * wide * 6,
        60_000_000,
    )


def gain_rows(stage, one, two):
    width = one.shape[1]
    share = width // 16
    row = lax.broadcasted_iota(jnp.int32, (GAIN_ROWS, width), 0)
    both = jnp.where(row == 0, one, jnp.where(row == 1, two, 0.0))
    tall = jnp.broadcast_to(both[None], (16, GAIN_ROWS, width)).reshape(16 * GAIN_ROWS, width)
    chip = lax.broadcasted_iota(jnp.int32, tall.shape, 0) // GAIN_ROWS
    feature = lax.broadcasted_iota(jnp.int32, tall.shape, 1)
    tall = jnp.where(feature // share == chip, tall, 0.0).astype(BF)
    feature = lax.broadcasted_iota(jnp.int32, (width, 128), 0)
    lane = lax.broadcasted_iota(jnp.int32, (width, 128), 1)
    pick = jnp.where(feature % share == lane, 1.0, 0.0).astype(BF)
    stage[...] = jnp.zeros(stage.shape, BF)
    stage[:, :, :, :128] = mat(tall, pick).astype(BF).reshape(4, 4, GAIN_ROWS, 128)


def attend_backward(meta, dm, x, qkv, o, gain, gg_two, pieces):
    count = len(pieces)
    length, width = x.shape
    pairs = width // (2 * HEAD_DIM)
    scale = HEAD_DIM ** (-0.5)

    def body(meta, dm_ref, x_ref, qkv_ref, o_ref, gain_ref, gg_two_ref, *refs):
        src = pieces_of_refs(refs[:count])
        dx_ref = refs[count]
        outs = refs[count + 1 : count + 3], refs[count + 3 : count + 5]
        wqkv, wo, stage, stage_o, stage_g, do_ref, dqkv, sems_a, sems_b, sems_c = refs[count + 5 :]
        load_b = chunked(meta, src, wo, sems_b, width * 3 // 16, 1)
        load_a = chunked(meta, src, wqkv, sems_a, 0, 3)
        start_all(load_b)
        start_all(load_a)
        bias = attention_bias(meta[3], length)
        low = dm_ref[...].astype(BF)
        stage_o[...] = t_mat(o_ref[...], low).astype(BF).reshape(4, 4, width // 16, width)
        wait_all(load_b)
        do_ref[...] = mat_t(low, tile(wo, 0, width)).astype(BF)
        store_b = chunked(meta, outs, stage_o, sems_b, width * 3 // 16, 1, True)
        start_all(store_b)
        lanes = head_lanes()

        def pair(p, _):
            at = lambda part: pl.ds(
                pl.multiple_of(part * width + p * 2 * HEAD_DIM, 128), 2 * HEAD_DIM
            )
            q, k, v = qkv_ref[:, at(0)], qkv_ref[:, at(1)], qkv_ref[:, at(2)]
            d = do_ref[:, at(0)]
            dq, dk, dv = [], [], []
            for j in range(2):
                soft = probabilities(only(lanes, j, q), k, bias)
                dp = mat_t(only(lanes, j, d), v)
                ds = (soft * (dp - jnp.sum(dp * soft, -1, keepdims=True))).astype(BF)
                dv.append(t_mat(soft.astype(BF), d))
                dq.append(mat(ds, k) * scale)
                dk.append(t_mat(ds, q) * scale)
            for part, two in enumerate((dq, dk, dv)):
                dqkv[:, at(part)] = jnp.where(lanes == 0, two[0], two[1]).astype(BF)
            return 0

        lax.fori_loop(0, pairs, pair, 0)
        n, root = normed(x_ref[...])
        gain = gain_ref[...]
        hidden_t = (n * gain).astype(BF).T
        wait_all(load_a)
        dh = jnp.zeros((length, width), F32)
        for t in range(3):
            d = dqkv[:, t * width : (t + 1) * width]
            stage[:, :, :, t * width : (t + 1) * width] = (
                mat(hidden_t, d).astype(BF).reshape(4, 4, width // 16, width)
            )
            dh = dh + mat_t(d, tile(wqkv, t, width))
        store_a = chunked(meta, outs, stage, sems_a, 0, 3, True)
        start_all(store_a)
        gain_rows(stage_g, jnp.sum(dh * n, 0, keepdims=True), gg_two_ref[...])
        store_c = [
            pltpu.make_async_copy(
                stage_g.at[:, chip_row(meta, i)],
                outs[side][half].at[i, :, pl.ds(DEEP // 2, GAIN_ROWS), :],
                sems_c.at[8 * half + 4 * side + i],
            )
            for half in range(2)
            for side in range(2)
            for i in range(4)
        ]
        start_all(store_c)
        dx_ref[...] = dm_ref[...] + norm_back(n, root, dh * gain)
        wait_all(store_a)
        wait_all(store_b)
        wait_all(store_c)

    return call(
        body,
        [meta, dm, x, qkv, o, gain, gg_two, *pieces],
        (shape((length, width), F32),) + piece_shapes(DEEP // 2 + GAIN_ROWS),
        [SMEM] + [VMEM] * 6 + [HBM] * count,
        (VMEM,) + (HBM,) * 4,
        [
            pltpu.VMEM((4, 4, width // 16, 3 * width), BF),
            pltpu.VMEM((4, 4, width // 16, width), BF),
            pltpu.VMEM((4, 4, width // 16, 3 * width), BF),
            pltpu.VMEM((4, 4, width // 16, width), BF),
            pltpu.VMEM((4, 4, GAIN_ROWS, WIDE), BF),
            pltpu.VMEM((length, width), BF),
            pltpu.VMEM((length, 3 * width), BF),
            pltpu.SemaphoreType.DMA((24,)),
            pltpu.SemaphoreType.DMA((8,)),
            pltpu.SemaphoreType.DMA((16,)),
        ],
        2 * length * width * width * 8 + 2 * length * length * width * 10,
        52_000_000,
    )


def index_of(v, i):
    return lax.dynamic_index_in_dim(v, i, 0, keepdims=False)


class Grid:
    def __init__(self):
        dp, seq = lax.axis_index("dp"), lax.axis_index("seq")
        self.z, self.x, self.y, self.c = dp // 2, dp % 2, seq // 2, seq % 2
        places = [(z, x, y, c) for z in range(4) for x in range(2) for y in range(2) for c in range(2)]
        flat = lambda z, x, y, c: (z * 2 + x) * 4 + y * 2 + c
        to = lambda move: [(flat(*p), flat(*move(*p))) for p in places]
        self.perm_c = to(lambda z, x, y, c: (z, x, y, 1 - c))
        self.perm_x = to(lambda z, x, y, c: (z, 1 - x, y, c))
        self.perm_y = to(lambda z, x, y, c: (z, x, 1 - y, c))
        self.perm_z = [to(lambda z, x, y, c, k=k: (z ^ k, x, y, c)) for k in range(4)]

    def over_c(self, v):
        return lax.ppermute(v, LINES, self.perm_c)

    def over_x(self, v):
        return lax.ppermute(v, LINES, self.perm_x)

    def over_y(self, v):
        return lax.ppermute(v, LINES, self.perm_y)

    def over_z(self, v, k):
        return lax.ppermute(v, LINES, self.perm_z[k])

    def planes(self, block, before=(), after=()):
        block = tie(block, *before)
        parts = [tie(block, *after)] + [self.over_z(block, k) for k in (1, 2, 3)]
        order = jnp.stack([self.z ^ k for k in range(4)]).astype(jnp.int32)
        return place(parts, order, [(0, block.shape[0])])[0]


class Gathering:
    def __init__(self, grid, own, cut):
        self.grid, self.own, self.cut = grid, own, cut

    def first(self, *after):
        own = tie(self.own, *after)
        self.by_x, self.by_y = self.grid.over_x(own), self.grid.over_y(own)
        return [self.by_x, self.by_y]

    def second(self, *after):
        a, b = tie(self.by_x, *after), tie(self.by_y, *after)
        self.both = [self.grid.over_y(a[:, : self.cut]), self.grid.over_x(b[:, self.cut :])]
        return self.both

    def pieces(self, *after):
        here = [self.own, self.by_x, self.by_y, *(tie(v, *after) for v in self.both)]
        return here + [self.grid.over_c(v) for v in here]


class Reduction:
    def __init__(self, grid, *pieces):
        flat = lambda v: v.reshape(4, -1, WIDE)
        self.mine = [flat(v) for v in pieces[:2]]
        self.came = [flat(grid.over_c(v)) for v in pieces[2:]]
        self.rows = self.mine[0].shape[1]

    def part(self, i, half):
        view = lambda meta, ref: ref.at[i]
        return (self.mine[half], view), (self.came[half], view)

    def at_plane(self, half, plane, count):
        rows = self.rows // 4

        def inside(first):
            return lambda meta, ref: ref.at[pl.ds(pl.multiple_of(first + plane(meta) * rows, 16), count)]

        def own(meta, ref):
            return ref.at[0, pl.ds(pl.multiple_of(plane(meta) * rows, 16), count)]

        cells = [self.straight[half], self.last[half]]
        return [(self.mine[half], own), (self.came[half], own)] + [(v, inside(first)) for v, first in cells]

    def counts(self):
        return DEEP // 2, self.rows // 4


def cell(v, first, rows):
    return v, lambda meta, ref: ref.at[pl.ds(first, rows)]


def step(grid, meta, after, seconds, firsts):
    tasks = Tasks(2)
    ends = []
    for r in seconds:
        for half in (0, 1):
            terms = r.part(1 + half, half) + (cell(*r.diagonal[half], r.rows),)
            ends.append((r, half, "last", 1 - half, tasks.add(1 - half, r.rows, *terms)))
    for r in firsts:
        for half in (0, 1):
            rows = r.rows
            ends.append((r, half, "diagonal", half, tasks.add(half, rows, *r.part(3, half))))
            ends.append((r, half, "straight", half, tasks.add(half, rows, *r.part(2 - half, half))))
    sent = tasks.run(meta, after)
    came = [grid.over_y(sent[0]), grid.over_x(sent[1])]
    for r, half, name, way, first in ends:
        if not hasattr(r, name):
            setattr(r, name, [None, None])
        getattr(r, name)[half] = (came[way], first)
    return sent, came


class Planes:
    def __init__(self, grid, meta, *reductions, at_once=False, after=()):
        self.grid, self.meta = grid, meta
        self.depth = sum(sum(r.counts()) for r in reductions)
        z = lambda meta: meta[4]
        if at_once:
            planes = [[lambda meta, k=k: z(meta) ^ k] for k in range(4)]
        else:
            planes = [[lambda meta, k=k, q=q: (z(meta) // 2 ^ k) * 2 + q for q in range(2)] for k in range(2)]
        tasks = Tasks(len(planes))
        tasks.kinds[0] = F32
        for out, group in enumerate(planes):
            for plane in group:
                for r in reductions:
                    for half in (0, 1):
                        tasks.add(out, r.counts()[half], *r.at_plane(half, plane, r.counts()[half]))
        self.kept, *sent = tasks.run(meta, after)
        self.sent = sent
        self.came = [grid.over_z(v, k) for v, k in zip(sent, (1, 2, 3) if at_once else (2,))]

    def second(self, *after):
        rows = self.depth
        tasks = Tasks(2)
        tasks.kinds[0] = F32
        for out in (0, 1):
            view = lambda meta, ref, out=out: ref.at[
                pl.ds(pl.multiple_of((meta[4] % 2 ^ out) * rows, 16), rows)
            ]
            tasks.add(out, rows, (self.kept, view), (self.came[0], view))
        self.kept, sent = tasks.run(self.meta, after)
        self.came = [self.grid.over_z(sent, 1)]

    def sums(self, layout, *after):
        return own_and_other(self.grid, self.meta, layout, tie(self.kept, *after), *self.came)


def own_and_other(grid, meta, layout, kept, *came):
    leave = sum(chunks * rows // 2 for _, chunks, rows in layout)
    count = len(came)

    def body(meta, kept, *refs):
        came, total, out = refs[:count], refs[count], refs[count + 1]
        total[...] = sum((v[...].astype(F32) for v in came), kept[...].astype(F32))
        at = 0
        for first, chunks, rows in layout:
            half = rows // 2
            for q in range(chunks):
                start = first + rows * q + half * (1 - meta[2])
                out[at : at + half] = total[pl.ds(pl.multiple_of(start, 8), half)]
                at += half

    total, out = call(
        body,
        [meta, kept, *came],
        [shape(kept.shape, F32), shape((leave, WIDE), F32)],
        [SMEM] + [VMEM] * (1 + count),
        [VMEM] * 2,
        [],
        0,
        5_000_000,
        limit=16,
    )
    return total, grid.over_c(out)


def tie(v, *after):
    return lax.optimization_barrier((v, *after))[0] if after else v


def seq_swaps(pieces_of, cuts):
    me, count = lax.axis_index("seq"), lax.axis_size("seq")
    kept = [pieces_of(me)]
    for r in range(1, count):
        kept.append(lax.ppermute(pieces_of(me ^ r), "seq", [(s, s ^ r) for s in range(count)]))
    order = jnp.stack([me ^ r for r in range(count)]).astype(jnp.int32)
    return lambda *after: place([tie(kept[0], *after), *kept[1:]], order, cuts)


def swap_all(grid, v, cuts):
    y, c = grid.y, grid.c
    pairs = v.reshape(2, 2, *v.shape[1:])
    stay = index_of(pairs, y)
    came = grid.over_y(index_of(pairs, 1 - y))
    other = grid.over_c(jnp.stack([index_of(stay, 1 - c), index_of(came, 1 - c)]))
    order = jnp.stack([y * 2 + c, (1 - y) * 2 + c, y * 2 + 1 - c, (1 - y) * 2 + 1 - c]).astype(jnp.int32)
    own = index_of(stay, c)
    return lambda *after: place(
        [tie(own, *after), index_of(came, c), other[0], other[1]], order, cuts
    )


def to_blocks(*arrays):
    quarter, width = arrays[0].shape[1:]
    cuts = [(quarter * k, quarter) for k in range(len(arrays))]
    end = seq_swaps(lambda s: jnp.concatenate([index_of(v, s) for v in arrays]), cuts)
    return lambda *after: [v.reshape(-1, width) for v in end(*after)]


def from_block(v, quarter):
    parts = v.reshape(-1, quarter, v.shape[-1])
    end = seq_swaps(lambda s: index_of(parts, s), [(0, quarter)])
    return lambda *after: end(*after)[0]


def both_halves(matrix):
    rows, wide = matrix.shape
    return matrix.reshape(rows, 2, wide // 2 // WIDE, WIDE).transpose(1, 2, 0, 3)


def lower_gains(ln1_gain, ln2_gain):
    return jnp.stack([ln1_gain, ln2_gain]).astype(BF)


def own_chunks(masters, core):
    views = []
    for l in range(masters[0].shape[0]):
        for ref, chunks in zip(masters, (3, 1, 4, 1)):
            for q in range(chunks):
                start = core * (ref.shape[2] // 2) + WIDE * q
                views.append(ref[l, :, pl.ds(pl.multiple_of(start, 128), WIDE)])
    return views


def chip_blocks(grid, meta, ln1_gain, ln2_gain, masters):
    layers, rows = masters[0].shape[:2]
    total = layers * 4 * 4 * rows * 3 // 4

    def leave(meta, one, two, *refs):
        ins, out = refs[:4], refs[4]
        start = 0
        for v in own_chunks(ins, 1 - meta[2]):
            out[start : start + v.shape[0]] = v
            start += v.shape[0]
        out[start : start + 8] = jnp.zeros((8, WIDE), F32)
        out[start : start + layers, :rows] = one[...]
        out[start + layers : start + 2 * layers, :rows] = two[...]

    size = sum(v.size for v in masters) * 8
    sent = call(
        leave,
        [meta, ln1_gain, ln2_gain, *masters],
        shape((total + 8, WIDE), F32),
        [SMEM] + [VMEM] * 6,
        VMEM,
        [],
        0,
        size,
        limit=16,
    )
    came = grid.over_c(sent)

    def merge(meta, sent, came, *refs):
        ins, outs, stage = refs[:4], refs[4:-1], refs[-1]
        core = meta[2]
        start = 0
        for v in own_chunks(ins, core):
            depth = v.shape[0]
            stage[pl.ds(pl.multiple_of(2 * start + core * depth, 8), depth)] = v
            stage[pl.ds(pl.multiple_of(2 * start + (1 - core) * depth, 8), depth)] = came[start : start + depth]
            start += depth
        stage[pl.ds(pl.multiple_of(2 * start + core * 8, 8), 8)] = sent[start : start + 8]
        stage[pl.ds(pl.multiple_of(2 * start + (1 - core) * 8, 8), 8)] = came[start : start + 8]
        first = 0
        for j, out in enumerate(outs):
            depth = DEEP * (1 + j % 2)
            out[:depth] = stage[first : first + depth].astype(BF)
            first += depth
        outs[0][DEEP:] = stage[first:].astype(BF)

    outs = [
        shape((DEEP * (1 + j % 2) + (GAIN_ROWS if j == 0 else 0), WIDE), BF) for j in range(2 * layers)
    ]
    return call(
        merge,
        [meta, sent, came, *masters],
        outs,
        [SMEM] + [VMEM] * 6,
        [VMEM] * len(outs),
        [pltpu.VMEM((2 * total + GAIN_ROWS, WIDE), F32)],
        0,
        size,
        limit=20,
    )


def finish(meta, sums, rows, width):
    layers = len(sums)

    def body(meta, *refs):
        count = 4 * layers
        ins, (one, two, *outs) = refs[:count], refs[count:]
        core = meta[2]
        for l in range(layers):
            feed, came, attn, came_attn = ins[4 * l : 4 * l + 4]

            def put(out, q, total, first, depth, came, at):
                half = out.shape[2] // 2
                columns = lambda c: pl.ds(pl.multiple_of(c * half + WIDE * q, 128), WIDE)
                out[l, :, columns(core)] = total[pl.ds(pl.multiple_of(first + core * depth, 8), depth)]
                out[l, :, columns(1 - core)] = came[at : at + depth]

            put(outs[3], 0, feed, DEEP, 4 * rows, came, 4 * rows)
            for q in range(4):
                put(outs[2], q, feed, 2 * rows * q, rows, came, q * rows)
            for q in range(3):
                put(outs[0], q, attn, 2 * rows * q, rows, came_attn, q * rows)
            put(outs[1], 0, attn, 6 * rows, rows, came_attn, 3 * rows)
            for g, out in enumerate((one, two)):
                both = attn[DEEP + g : DEEP + g + 1, : 2 * rows]
                out[l : l + 1] = jnp.where(core == 0, both[:, :rows], both[:, rows:])

    gain = shape((layers, rows), F32)
    outs = [gain, gain] + [
        shape((layers, r, w), F32)
        for r, w in ((rows, 3 * width), (rows, width), (rows, 4 * width), (4 * rows, width))
    ]
    flat = [v for l in range(layers) for v in sums[l]]
    one, two, qkv, out, up, down = call(
        body,
        [meta, *flat],
        outs,
        [SMEM] + [VMEM] * len(flat),
        [VMEM] * len(outs),
        [],
        0,
        8 * sum(v.size for v in flat),
        limit=20,
    )
    return one, qkv, out, two, up, down


def whole_gains(grid, gathering, layers, rows):
    g = gathering
    diagonal = g.both[1][:, -GAIN_ROWS:]
    tails = jnp.stack([v[:, -GAIN_ROWS:, :rows] for v in (g.own, g.by_x, g.by_y, diagonal)])
    tails = tails.reshape(2, 2, 4, 2, 8, rows)[:, :, :, :, : 2 * layers]
    tails = jnp.where(grid.y == 0, tails, tails[::-1])
    tails = jnp.where(grid.x == 0, tails, tails[:, ::-1])
    return tails.transpose(4, 2, 1, 0, 3, 5).reshape(2, layers, -1)


def pieces_of_whole(matrices):
    parts = []
    for whole in matrices:
        rows, wide = whole.shape
        parts.append(
            whole.reshape(4, 4, rows // 16, 2, wide // 2 // WIDE, WIDE).transpose(3, 1, 0, 4, 2, 5)
            .reshape(2, 4, 4, -1, WIDE)
        )
    stacked = jnp.concatenate(parts, 3)
    order = [(i & 1) * 2 + (i >> 1) for i in range(4)]
    return [stacked[side, order[i]] for side in range(2) for i in range(4)]


def whole_of_pieces(mine0, mine1, other0, other1, widths):
    cut = DEEP // 2
    sides = (mine0, mine1), (other0, other1)
    both = [jnp.concatenate([a[:, :, :cut], b[:, :, :cut]], 2) for a, b in sides]
    stacked = jnp.stack(both)
    stacked = jnp.stack([stacked[:, i] for i in (0, 2, 1, 3)], 1)
    outs, start = [], 0
    for rows, wide in widths:
        depth, chunks = rows // 16, wide // 2 // WIDE
        part = stacked[:, :, :, start : start + depth * chunks]
        start += depth * chunks
        outs.append(
            part.reshape(2, 4, 4, chunks, depth, WIDE).transpose(2, 1, 4, 0, 3, 5).reshape(rows, wide)
        )
    return outs


def per_device(
    states,
    item_halves,
    ln1_gain,
    qkv_weight,
    out_weight,
    ln2_gain,
    up_weight,
    down_weight,
    cotangent,
):
    masters = (qkv_weight, out_weight, up_weight, down_weight)
    layers, gain_shard = ln1_gain.shape
    quarter, width = states.shape[1:]
    near = lax.axis_size("dp") == 8 and lax.axis_size("seq") == 4 and layers == 2
    gains = lower_gains(ln1_gain, ln2_gain)
    flag = index_of(item_halves, lax.axis_index("seq"))
    if near:
        return by_permutes(states, flag, ln1_gain, ln2_gain, masters, cotangent, quarter)
    zero = jnp.zeros((), jnp.int32)
    meta = jnp.stack([zero, zero, zero, flag]).astype(jnp.int32)
    x, grad = to_blocks(states, cotangent)()
    gains = lax.all_gather(gains, LINES, axis=2, tiled=True).astype(F32)
    kept = []
    for l in range(layers):
        qkv, out, up, down = (
            lax.all_gather(v[l].astype(BF), LINES, axis=0, tiled=True) for v in masters
        )
        attn, feed = pieces_of_whole([qkv, out]), pieces_of_whole([up, down])
        qkv, o, m = attend_forward(meta, x, gains[0, l][None], attn)
        u, a, y = feed_forward(meta, m, gains[1, l][None], feed)
        kept.append((x, qkv, o, m, u, a, attn, feed))
        x = y
    outputs = x
    results = [None] * layers
    for l in reversed(range(layers)):
        x, qkv, o, m, u, a, attn, feed = kept[l]
        down_pieces = down_backward(meta, grad, a)
        dm, gg_two, *up_pieces = feed_backward(meta, grad, m, u, gains[1, l][None], feed)
        grad, *attn_pieces = attend_backward(meta, dm, x, qkv, o, gains[0, l][None], gg_two, attn)
        wholes = (
            whole_of_pieces(*attn_pieces, ((width, 3 * width), (width, width)))
            + whole_of_pieces(*up_pieces, ((width, 4 * width),))
            + whole_of_pieces(*down_pieces, ((4 * width, width),))
        )
        gain_sums = attn_pieces[0][:, :, DEEP // 2 :, : width // 16]
        gain_sums = jnp.stack([gain_sums[i] for i in (0, 2, 1, 3)]).transpose(2, 1, 0, 3).reshape(GAIN_ROWS, width)
        sums = [
            lax.psum_scatter(v.astype(F32), LINES, scatter_dimension=0, tiled=True) for v in wholes
        ]
        gain_sums = lax.psum(gain_sums[:2].astype(F32), LINES)
        owner = lax.axis_index(LINES) * gain_shard
        results[l] = (lax.dynamic_slice_in_dim(gain_sums, owner, gain_shard, 1), *sums)
    return collect(from_block(outputs, quarter)(), from_block(grad, quarter)(), results)


def collect(outputs, grad_states, results):
    gains, qkv, out, up, down = (jnp.stack([r[k] for r in results]) for k in range(5))
    return outputs, grad_states, gains[:, 0], qkv, out, gains[:, 1], up, down


def by_permutes(states, flag, ln1_gain, ln2_gain, masters, cotangent, quarter):
    grid = Grid()
    meta = jnp.stack([grid.x, grid.y, grid.c, flag, grid.z]).astype(jnp.int32)
    layers, rows = masters[0].shape[:2]
    width = states.shape[2]
    blocks = chip_blocks(grid, meta, ln1_gain, ln2_gain, masters)
    come = swap_all(
        grid,
        jnp.concatenate([tie(states, blocks[0]), cotangent], 1),
        [(0, quarter), (quarter, quarter)],
    )
    feed1 = lax.all_gather(blocks[3], LINES, axis=0, tiled=True)
    feed1 = [feed1.reshape(4, 4, 2, 2 * DEEP, WIDE)]
    own = grid.planes(blocks[0])
    attn0 = Gathering(grid, own, DEEP // 2)
    attn0.first()
    own = grid.planes(blocks[1], (own,), (attn0.by_x, attn0.by_y))
    attn0.second()
    x, grad = (v.reshape(-1, width) for v in come(*attn0.both))
    feed0 = Gathering(grid, own, DEEP)
    feed0.first(*attn0.both)
    gains = whole_gains(grid, attn0, layers, rows).astype(F32)
    attn0 = attn0.pieces()
    qkv0, o0, m0 = attend_forward(meta, x, gains[0, 0][None], attn0)
    own = grid.planes(blocks[2], (own,), (m0,))
    feed0.second(m0)
    attn1 = Gathering(grid, own, DEEP // 2)
    attn1.first(feed0.by_x, feed0.by_y)
    attn1.second()
    feed0 = feed0.pieces()
    u0, a0, x1 = feed_forward(meta, tie(m0, attn1.by_x, attn1.by_y), gains[1, 0][None], feed0)
    attn1 = attn1.pieces(x1)
    qkv1, o1, m1 = attend_forward(meta, x1, gains[0, 1][None], attn1)
    y, dm, gg_two, whole = feed_both(meta, m1, grad, gains[1, 1][None], feed1)
    whole = lax.psum_scatter(whole.reshape(-1, WIDE), LINES, scatter_dimension=0, tiled=True)
    grad, *pieces = attend_backward(meta, dm, x1, qkv1, o1, gains[0, 1][None], gg_two, attn1)
    attn1 = Reduction(grid, *pieces)
    down_pieces = down_backward(meta, grad, a0)
    down0 = Reduction(grid, *down_pieces)
    ready, came1 = step(grid, meta, (down_pieces[0],), (), (attn1,))
    dm, gg_two, *pieces = feed_backward(
        meta, tie(grad, down_pieces[0], *ready), m0, u0, gains[1, 0][None], feed0
    )
    up0 = Reduction(grid, *pieces)
    ready, came2 = step(grid, meta, (dm, *came1), (attn1,), (down0,))
    dm = tie(dm, *ready)
    grad, *pieces = attend_backward(meta, dm, x, qkv0, o0, gains[0, 0][None], gg_two, attn0)
    attn0 = Reduction(grid, *pieces)
    sent, came3 = step(grid, meta, (grad, *came2), (down0,), (up0,))
    planes_attn1 = Planes(grid, meta, attn1, at_once=True, after=sent)
    sent, came4 = step(grid, meta, (*attn0.came, *came3), (up0,), (attn0,))
    sent, came5 = step(grid, meta, (*planes_attn1.came, *came4), (attn0,), ())
    feed = ((0, 4, 2 * rows), (DEEP, 1, DEEP))
    attend = ((0, 4, 2 * rows),)
    both = (*feed, (2 * DEEP, 4, 2 * rows))
    sums_attn1 = planes_attn1.sums(attend, *sent)
    planes0 = Planes(grid, meta, up0, down0, attn0, at_once=True)
    results = jnp.concatenate([v.reshape(4, quarter, width) for v in (tie(y, *planes0.sent), grad)], 1)
    results = swap_all(grid, results, [(0, quarter), (quarter, quarter)])
    outputs, grad_states = results(*planes0.came)
    sums1 = own_and_other(grid, meta, feed, tie(whole, *planes0.sent))
    total, came = planes0.sums(both)
    cut = 2 * DEEP
    sums0 = (total[:cut], came[: cut // 2], total[cut:], came[cut // 2 :])
    return outputs, grad_states, *finish(meta, (sums0, (*sums1, *sums_attn1)), rows, width)


def solution(mesh):
    rows = P(None, LINES, None)
    tokens = P("dp", "seq", None)
    gain = P(None, LINES)
    return jax.shard_map(
        per_device,
        mesh=mesh,
        in_specs=(tokens, P("dp"), gain, rows, rows, gain, rows, rows, tokens),
        out_specs=(tokens, tokens, gain, rows, rows, gain, rows, rows),
        check_vma=False,
    )
```

```python
import jax
import jax.numpy as jnp
from jax import lax
from jax.experimental import pallas as pl
from jax.experimental.pallas import tpu as pltpu
from jax.sharding import PartitionSpec as P

HEAD_DIM = 64
EPSILON = 1e-05
BF = jnp.bfloat16
F32 = jnp.float32
LINES = ("dp", "seq")
WIDE = 384
DEEP = 192
GAIN_ROWS = 16
VMEM = pl.BlockSpec(memory_space=pltpu.VMEM)
SMEM = pl.BlockSpec(memory_space=pltpu.SMEM)
HBM = pl.BlockSpec(memory_space=pl.ANY)


def call(body, ins, outs, specs, out_specs, scratch, flops, size, limit=58):
    return pl.pallas_call(
        body,
        out_shape=outs,
        in_specs=specs,
        out_specs=out_specs,
        scratch_shapes=scratch,
        cost_estimate=pl.CostEstimate(
            flops=flops, bytes_accessed=6 * size, transcendentals=0
        ),
        compiler_params=pltpu.CompilerParams(vmem_limit_bytes=limit * 1024 * 1024),
    )(*ins)


def shape(dims, dtype):
    return jax.ShapeDtypeStruct(dims, dtype)


def mat(a, b):
    return jnp.dot(a, b, preferred_element_type=F32)


def mat_t(a, b):
    return lax.dot_general(a, b, (((1,), (1,)), ((), ())), preferred_element_type=F32)


def t_mat(a, b):
    return lax.dot_general(a, b, (((0,), (0,)), ((), ())), preferred_element_type=F32)


def normed(v):
    average = jnp.mean(v, -1, keepdims=True)
    centered = v - average
    variance = jnp.mean(centered * centered, -1, keepdims=True)
    root = lax.rsqrt(variance + EPSILON)
    return centered * root, root


def norm_back(n, root, g):
    return root * (
        g - jnp.mean(g, -1, keepdims=True) - n * jnp.mean(g * n, -1, keepdims=True)
    )


def bell(u):
    return 0.5 * (1.0 + lax.erf(u * 0.7071067811865476))


def place(pieces, where_to, cuts):
    count = len(pieces)

    def body(to, *refs):
        for k in range(count):
            for (start, rows), out in zip(cuts, refs[count:]):
                out[to[k]] = refs[k][start : start + rows]

    one = pieces[0]
    return call(
        body,
        [where_to, *pieces],
        [shape((count, rows, one.shape[1]), one.dtype) for _, rows in cuts],
        [SMEM] + [VMEM] * count,
        [VMEM] * len(cuts),
        [],
        0,
        2 * count * one.size * one.dtype.itemsize,
        limit=16,
    )


def combine(meta, arrays, outs, tasks, after=()):
    count = len(arrays)
    terms = [(rows, term) for _, _, rows, sources in tasks for term in sources]

    def body(meta, *refs):
        ins, results, held = refs[:count], refs[count : count + len(outs)], refs[count + len(outs) : -1]
        sems = refs[-1]
        copies = [
            pltpu.make_async_copy(view(meta, ins[place_of]), held[k], sems.at[k])
            for k, (_, (place_of, view)) in enumerate(terms)
        ]
        start_all(copies)
        k = 0
        for result, first, rows, sources in tasks:
            wait_all(copies[k : k + len(sources)])
            step = 64 if rows % 64 == 0 else 16

            def some(r, _, k=k, result=result, first=first, step=step, sources=sources):
                at = pl.multiple_of(r * step, 16)
                total = sum(held[k + j][pl.ds(at, step)].astype(F32) for j in range(len(sources)))
                to = pl.multiple_of(first + at, 16)
                results[result][pl.ds(to, step)] = total.astype(results[result].dtype)
                return 0

            lax.fori_loop(0, rows // step, some, 0)
            k += len(sources)

    arrays = [tie(arrays[0], *after), *arrays[1:]]
    return call(
        body,
        [meta, *arrays],
        [shape((rows, WIDE), kind) for rows, kind in outs],
        [SMEM] + [HBM] * count,
        [VMEM] * len(outs),
        [pltpu.VMEM((rows, WIDE), arrays[term[0]].dtype) for rows, term in terms]
        + [pltpu.SemaphoreType.DMA((len(terms),))],
        0,
        60_000_000,
    )


class Tasks:
    def __init__(self, outs):
        self.arrays, self.tasks, self.rows, self.kinds = [], [], [0] * outs, [BF] * outs

    def add(self, out, rows, *terms):
        sources = []
        for array, view in terms:
            known = [k for k, v in enumerate(self.arrays) if v is array]
            if not known:
                self.arrays.append(array)
            sources.append((known[0] if known else len(self.arrays) - 1, view))
        first = self.rows[out]
        self.tasks.append((out, first, rows, sources))
        self.rows[out] += rows
        return first

    def run(self, meta, after=()):
        return combine(meta, self.arrays, list(zip(self.rows, self.kinds)), self.tasks, after)


def chip_row(meta, i):
    return (meta[0] ^ (i & 1)) * 2 + (meta[1] ^ (i >> 1))


def columns(meta, side, half, q):
    start = (meta[2] ^ side) * half + WIDE * q
    return pl.ds(pl.multiple_of(start, 128), WIDE)


def place_in(count, half, i):
    if count == 1:
        return 0, 4 * half + i
    if count == 2:
        return (0, 2 * half + (0 if i == 3 else 1)) if i in (3, 2 - half) else (1, 2 * half + (1 if i == 0 else 0))
    if i == 3 or i == 2 - half:
        return half, 0 if i == 3 else 1
    return 2, 2 * half + (1 if i == 0 else 0)


def piece_at(pieces, i, start, rows):
    if len(pieces) < 4:
        half = start // (DEEP // 2)
        array, at = place_in(len(pieces), half, i)
        return pieces[array].at[at, :, pl.ds(start - half * (DEEP // 2), rows), :]
    if i == 3 and len(pieces) == 5:
        cut = pieces[3].shape[1]
        if start >= cut:
            return pieces[4].at[:, pl.ds(start - cut, rows), :]
    return pieces[i].at[:, pl.ds(start, rows), :]


def chunked(meta, sides, target, sems, first, chunks, to_pieces=False, split=1):
    half = target.shape[-1] // 2
    rows = target.shape[2]
    step = rows // split
    whole = not isinstance(sides, (list, tuple))
    copies = []
    for side in range(2):
        for i in range(4):
            for q in range(chunks):
                for k in range(split):
                    start = first + rows * q + step * k
                    if whole:
                        a = sides.at[:, i, side, pl.ds(start, step), :]
                        place_of, lanes = i, pl.ds(side * half + WIDE * q, WIDE)
                    else:
                        a = piece_at(sides[side], i, start, step)
                        place_of, lanes = chip_row(meta, i), columns(meta, side, half, q)
                    b = target.at[:, place_of, pl.ds(step * k, step), lanes]
                    pair = (b, a) if to_pieces else (a, b)
                    copies.append(pltpu.make_async_copy(*pair, sems.at[len(copies)]))
    return copies


def pieces_of_refs(refs):
    count = len(refs)
    return refs[0] if count == 1 else (refs[: count // 2], refs[count // 2 :])


def start_all(copies):
    for copy in copies:
        copy.start()


def wait_all(copies):
    for copy in copies:
        copy.wait()


def attention_bias(flag, length):
    row = lax.broadcasted_iota(jnp.int32, (length, length), 0) // (length // 2)
    column = lax.broadcasted_iota(jnp.int32, (length, length), 1) // (length // 2)
    return jnp.where(jnp.logical_or(row == column, flag == 0), 0.0, -1e30)


def probabilities(queries, keys, bias):
    s = mat_t(queries, keys) * HEAD_DIM ** (-0.5) + bias
    e = jnp.exp(s - jnp.max(s, -1, keepdims=True))
    return e * (1.0 / jnp.sum(e, -1, keepdims=True))


def head_lanes():
    return lax.broadcasted_iota(jnp.int32, (1, 2 * HEAD_DIM), 1) // HEAD_DIM


def only(lanes, j, v):
    return jnp.where(lanes == j, v, jnp.zeros_like(v))


def tile(ref, t, width):
    z, xy, rows, _ = ref.shape
    return ref[:, :, :, t * width : (t + 1) * width].reshape(z * xy * rows, width)


def attend_forward(meta, x, gain, pieces):
    count = len(pieces)
    length, width = x.shape
    pairs = width // (2 * HEAD_DIM)

    def body(meta, x_ref, gain_ref, *refs):
        src = pieces_of_refs(refs[:count])
        qkv_ref, o_ref, m_ref, wqkv, wo, sems_a, sems_b = refs[count:]
        load_a = chunked(meta, src, wqkv, sems_a, 0, 3)
        load_b = chunked(meta, src, wo, sems_b, width * 3 // 16, 1)
        start_all(load_a)
        start_all(load_b)
        bias = attention_bias(meta[3], length)
        n, _ = normed(x_ref[...])
        hidden = (n * gain_ref[...]).astype(BF)
        wait_all(load_a)
        for t in range(3):
            qkv_ref[:, t * width : (t + 1) * width] = mat(hidden, tile(wqkv, t, width)).astype(BF)
        lanes = head_lanes()

        def pair(p, _):
            take = lambda part: qkv_ref[
                :, pl.ds(pl.multiple_of(part * width + p * 2 * HEAD_DIM, 128), 2 * HEAD_DIM)
            ]
            q, k, v = take(0), take(1), take(2)
            outs = [
                mat(probabilities(only(lanes, j, q), k, bias).astype(BF), v) for j in range(2)
            ]
            o_ref[:, pl.ds(pl.multiple_of(p * 2 * HEAD_DIM, 128), 2 * HEAD_DIM)] = jnp.where(
                lanes == 0, outs[0], outs[1]
            ).astype(BF)
            return 0

        lax.fori_loop(0, pairs, pair, 0, unroll=True)
        wait_all(load_b)
        m_ref[...] = x_ref[...] + mat(o_ref[...], tile(wo, 0, width))

    return call(
        body,
        [meta, x, gain, *pieces],
        (shape((length, 3 * width), BF), shape((length, width), BF), shape((length, width), F32)),
        [SMEM, VMEM, VMEM] + [HBM] * count,
        (VMEM,) * 3,
        [
            pltpu.VMEM((4, 4, width // 16, 3 * width), BF),
            pltpu.VMEM((4, 4, width // 16, width), BF),
            pltpu.SemaphoreType.DMA((24,)),
            pltpu.SemaphoreType.DMA((8,)),
        ],
        2 * length * width * width * 4 + 4 * length * length * width * 2,
        36_000_000,
    )


def feed_forward(meta, m, gain, pieces):
    count = len(pieces)
    length, width = m.shape
    wide = 4 * width

    def body(meta, m_ref, gain_ref, *refs):
        src = pieces_of_refs(refs[:count])
        u_ref, a_ref, y_ref, wu, wd, sems_a, sems_b = refs[count:]
        load_a = chunked(meta, src, wu, sems_a, 0, 4)
        load_b = chunked(meta, src, wd, sems_b, width // 4, 1)
        start_all(load_a)
        start_all(load_b)
        n, _ = normed(m_ref[...])
        hidden = (n * gain_ref[...]).astype(BF)
        wait_all(load_a)
        wait_all(load_b)
        total = m_ref[...]
        for t in range(4):
            u = mat(hidden, tile(wu, t, width))
            u_ref[:, t * width : (t + 1) * width] = u
            a = (u * bell(u)).astype(BF)
            a_ref[:, t * width : (t + 1) * width] = a
            total = total + mat(a, wd[t].reshape(width, width))
        y_ref[...] = total

    return call(
        body,
        [meta, m, gain, *pieces],
        (shape((length, wide), F32), shape((length, wide), BF), shape((length, width), F32)),
        [SMEM, VMEM, VMEM] + [HBM] * count,
        (VMEM,) * 3,
        [
            pltpu.VMEM((4, 4, width // 16, wide), BF),
            pltpu.VMEM((4, 4, width // 4, width), BF),
            pltpu.SemaphoreType.DMA((32,)),
            pltpu.SemaphoreType.DMA((8,)),
        ],
        2 * length * width * wide * 2,
        26_000_000,
    )


def piece_shapes(rows, parts):
    part = lambda count: shape((count, 4, rows, WIDE), BF)
    others = {1: (part(8),), 2: (part(4), part(4)), 3: (part(2), part(2), part(4))}
    return (part(8),) + others[parts]


def whole_shape():
    return shape((4, 4, 2, 2 * DEEP, WIDE), BF)


def down_backward(meta, dy, a):
    length, width = dy.shape

    def body(meta, dy_ref, a_ref, *refs):
        *outs, stage, sems = refs
        low = dy_ref[...].astype(BF)
        for t in range(4):
            stage[t] = (
                t_mat(a_ref[:, t * width : (t + 1) * width], low)
                .astype(BF)
                .reshape(4, width // 4, width)
            )
        copies = chunked(meta, (outs[:1], outs[1:]), stage, sems, 0, 1, True, 2)
        start_all(copies)
        wait_all(copies)

    outs = piece_shapes(DEEP // 2, 1)
    return call(
        body,
        [meta, dy, a],
        outs,
        [SMEM, VMEM, VMEM],
        (HBM,) * 2,
        [pltpu.VMEM((4, 4, width // 4, width), BF), pltpu.SemaphoreType.DMA((16,))],
        8 * length * width * width,
        13_000_000,
    )


def feed_backward(meta, dy, m, u, gain, pieces):
    count = len(pieces)
    length, width = m.shape
    wide = 4 * width

    def body(meta, dy_ref, m_ref, u_ref, gain_ref, *refs):
        src = pieces_of_refs(refs[:count])
        dm_ref, gg_ref, *outs = refs[count:-5]
        wu, wd, stage, sems_a, sems_b = refs[-5:]
        outs = outs[:1], outs[1:]
        load_a = chunked(meta, src, wu, sems_a, 0, 4)
        load_b = chunked(meta, src, wd, sems_b, width // 4, 1)
        start_all(load_b)
        start_all(load_a)
        n, root = normed(m_ref[...])
        gain = gain_ref[...]
        hidden_t = (n * gain).astype(BF).T
        low = dy_ref[...].astype(BF)
        wait_all(load_b)
        wait_all(load_a)
        dh = jnp.zeros((length, width), F32)
        for t in range(4):
            da = mat_t(low, wd[t].reshape(width, width))
            u = u_ref[:, t * width : (t + 1) * width]
            slope = bell(u) + u * (jnp.exp(-0.5 * u * u) * 0.3989422804014327)
            du = (da * slope).astype(BF)
            stage[:, :, :, t * width : (t + 1) * width] = (
                mat(hidden_t, du).astype(BF).reshape(4, 4, width // 16, width)
            )
            dh = dh + mat_t(du, tile(wu, t, width))
        store = chunked(meta, outs, stage, sems_a, 0, 4, True)
        start_all(store)
        gg_ref[...] = jnp.sum(dh * n, 0, keepdims=True)
        dm_ref[...] = dy_ref[...] + norm_back(n, root, dh * gain)
        wait_all(store)

    return call(
        body,
        [meta, dy, m, u, gain, *pieces],
        (shape((length, width), F32), shape((1, width), F32)) + piece_shapes(DEEP // 2, 2),
        [SMEM] + [VMEM] * 4 + [HBM] * count,
        (VMEM, VMEM) + (HBM,) * 3,
        [
            pltpu.VMEM((4, 4, width // 16, wide), BF),
            pltpu.VMEM((4, 4, width // 4, width), BF),
            pltpu.VMEM((4, 4, width // 16, wide), BF),
            pltpu.SemaphoreType.DMA((32,)),
            pltpu.SemaphoreType.DMA((8,)),
        ],
        2 * length * width * wide * 3,
        40_000_000,
    )


def feed_both(meta, m, dy, gain, pieces):
    length, width = m.shape
    wide = 4 * width
    count = len(pieces)

    def body(meta, m_ref, dy_ref, gain_ref, *refs):
        src = pieces_of_refs(refs[:count])
        y_ref, dm_ref, gg_ref, whole = refs[count : count + 4]
        wu, wd, a_ref, slope_ref, stage_u, stage_d, sems_a, sems_b, sems_c, sems_d = refs[count + 4 :]
        load_a = chunked(meta, src, wu, sems_a, 0, 4)
        load_b = chunked(meta, src, wd, sems_b, width // 4, 1)
        start_all(load_a)
        start_all(load_b)
        n, root = normed(m_ref[...])
        gain = gain_ref[...]
        hidden = (n * gain).astype(BF)
        hidden_t = (n * gain).astype(BF).T
        low = dy_ref[...].astype(BF)
        wait_all(load_a)
        for t in range(4):
            u = mat(hidden, tile(wu, t, width))
            share = bell(u)
            a = (u * share).astype(BF)
            a_ref[:, t * width : (t + 1) * width] = a
            slope_ref[:, t * width : (t + 1) * width] = share + u * (
                jnp.exp(-0.5 * u * u) * 0.3989422804014327
            )
            stage_d[t] = t_mat(a, low).astype(BF).reshape(4, width // 4, width)
        store_d = chunked(meta, whole, stage_d, sems_d, DEEP, 1, True)
        start_all(store_d)
        wait_all(load_b)
        dh = jnp.zeros((length, width), F32)
        for t in range(4):
            da = mat_t(low, wd[t].reshape(width, width))
            du = (da * slope_ref[:, t * width : (t + 1) * width]).astype(BF)
            stage_u[:, :, :, t * width : (t + 1) * width] = (
                mat(hidden_t, du).astype(BF).reshape(4, 4, width // 16, width)
            )
            dh = dh + mat_t(du, tile(wu, t, width))
        store_u = chunked(meta, whole, stage_u, sems_c, 0, 4, True)
        start_all(store_u)
        gg_ref[...] = jnp.sum(dh * n, 0, keepdims=True)
        dm_ref[...] = dy_ref[...] + norm_back(n, root, dh * gain)
        total = m_ref[...]
        for t in range(4):
            total = total + mat(a_ref[:, t * width : (t + 1) * width], wd[t].reshape(width, width))
        y_ref[...] = total
        wait_all(store_d)
        wait_all(store_u)

    return call(
        body,
        [meta, m, dy, gain, *pieces],
        (
            shape((length, width), F32),
            shape((length, width), F32),
            shape((1, width), F32),
            whole_shape(),
        ),
        [SMEM] + [VMEM] * 3 + [HBM] * count,
        (VMEM, VMEM, VMEM, HBM),
        [
            pltpu.VMEM((4, 4, width // 16, wide), BF),
            pltpu.VMEM((4, 4, width // 4, width), BF),
            pltpu.VMEM((length, wide), BF),
            pltpu.VMEM((length, wide), F32),
            pltpu.VMEM((4, 4, width // 16, wide), BF),
            pltpu.VMEM((4, 4, width // 4, width), BF),
            pltpu.SemaphoreType.DMA((32,)),
            pltpu.SemaphoreType.DMA((8,)),
            pltpu.SemaphoreType.DMA((32,)),
            pltpu.SemaphoreType.DMA((8,)),
        ],
        2 * length * width * wide * 6,
        60_000_000,
    )


def gain_place(pieces, half, i):
    array, at = place_in(len(pieces), half, i)
    return pieces[array].at[at, :, pl.ds(DEEP // 2, GAIN_ROWS), :]


def gain_rows(stage, one, two):
    width = one.shape[1]
    share = width // 16
    row = lax.broadcasted_iota(jnp.int32, (GAIN_ROWS, width), 0)
    both = jnp.where(row == 0, one, jnp.where(row == 1, two, 0.0))
    tall = jnp.broadcast_to(both[None], (16, GAIN_ROWS, width)).reshape(16 * GAIN_ROWS, width)
    chip = lax.broadcasted_iota(jnp.int32, tall.shape, 0) // GAIN_ROWS
    feature = lax.broadcasted_iota(jnp.int32, tall.shape, 1)
    tall = jnp.where(feature // share == chip, tall, 0.0).astype(BF)
    feature = lax.broadcasted_iota(jnp.int32, (width, 128), 0)
    lane = lax.broadcasted_iota(jnp.int32, (width, 128), 1)
    pick = jnp.where(feature % share == lane, 1.0, 0.0).astype(BF)
    stage[...] = jnp.zeros(stage.shape, BF)
    stage[:, :, :, :128] = mat(tall, pick).astype(BF).reshape(4, 4, GAIN_ROWS, 128)


def attend_backward(meta, dm, x, qkv, o, gain, gg_two, pieces):
    count = len(pieces)
    length, width = x.shape
    pairs = width // (2 * HEAD_DIM)
    scale = HEAD_DIM ** (-0.5)

    def body(meta, dm_ref, x_ref, qkv_ref, o_ref, gain_ref, gg_two_ref, *refs):
        src = pieces_of_refs(refs[:count])
        dx_ref = refs[count]
        outs = refs[count + 1 : count + 2], refs[count + 2 : count + 5]
        wqkv, wo, stage, stage_o, stage_g, do_ref, dqkv, sems_a, sems_b, sems_c = refs[count + 5 :]
        load_b = chunked(meta, src, wo, sems_b, width * 3 // 16, 1)
        load_a = chunked(meta, src, wqkv, sems_a, 0, 3)
        start_all(load_b)
        start_all(load_a)
        bias = attention_bias(meta[3], length)
        low = dm_ref[...].astype(BF)
        stage_o[...] = t_mat(o_ref[...], low).astype(BF).reshape(4, 4, width // 16, width)
        wait_all(load_b)
        do_ref[...] = mat_t(low, tile(wo, 0, width)).astype(BF)
        store_b = chunked(meta, outs, stage_o, sems_b, width * 3 // 16, 1, True)
        start_all(store_b)
        lanes = head_lanes()

        def pair(p, _):
            at = lambda part: pl.ds(
                pl.multiple_of(part * width + p * 2 * HEAD_DIM, 128), 2 * HEAD_DIM
            )
            q, k, v = qkv_ref[:, at(0)], qkv_ref[:, at(1)], qkv_ref[:, at(2)]
            d = do_ref[:, at(0)]
            dq, dk, dv = [], [], []
            for j in range(2):
                soft = probabilities(only(lanes, j, q), k, bias)
                dp = mat_t(only(lanes, j, d), v)
                ds = (soft * (dp - jnp.sum(dp * soft, -1, keepdims=True))).astype(BF)
                dv.append(t_mat(soft.astype(BF), d))
                dq.append(mat(ds, k) * scale)
                dk.append(t_mat(ds, q) * scale)
            for part, two in enumerate((dq, dk, dv)):
                dqkv[:, at(part)] = jnp.where(lanes == 0, two[0], two[1]).astype(BF)
            return 0

        lax.fori_loop(0, pairs, pair, 0, unroll=2)
        n, root = normed(x_ref[...])
        gain = gain_ref[...]
        hidden_t = (n * gain).astype(BF).T
        wait_all(load_a)
        dh = jnp.zeros((length, width), F32)
        for t in range(3):
            d = dqkv[:, t * width : (t + 1) * width]
            stage[:, :, :, t * width : (t + 1) * width] = (
                mat(hidden_t, d).astype(BF).reshape(4, 4, width // 16, width)
            )
            dh = dh + mat_t(d, tile(wqkv, t, width))
        store_a = chunked(meta, outs, stage, sems_a, 0, 3, True)
        start_all(store_a)
        gain_rows(stage_g, jnp.sum(dh * n, 0, keepdims=True), gg_two_ref[...])
        store_c = [
            pltpu.make_async_copy(
                stage_g.at[:, chip_row(meta, i)],
                gain_place(outs[side], half, i),
                sems_c.at[8 * half + 4 * side + i],
            )
            for half in range(2)
            for side in range(2)
            for i in range(4)
        ]
        start_all(store_c)
        dx_ref[...] = dm_ref[...] + norm_back(n, root, dh * gain)
        wait_all(store_a)
        wait_all(store_b)
        wait_all(store_c)

    return call(
        body,
        [meta, dm, x, qkv, o, gain, gg_two, *pieces],
        (shape((length, width), F32),) + piece_shapes(DEEP // 2 + GAIN_ROWS, 3),
        [SMEM] + [VMEM] * 6 + [HBM] * count,
        (VMEM,) + (HBM,) * 4,
        [
            pltpu.VMEM((4, 4, width // 16, 3 * width), BF),
            pltpu.VMEM((4, 4, width // 16, width), BF),
            pltpu.VMEM((4, 4, width // 16, 3 * width), BF),
            pltpu.VMEM((4, 4, width // 16, width), BF),
            pltpu.VMEM((4, 4, GAIN_ROWS, WIDE), BF),
            pltpu.VMEM((length, width), BF),
            pltpu.VMEM((length, 3 * width), BF),
            pltpu.SemaphoreType.DMA((24,)),
            pltpu.SemaphoreType.DMA((8,)),
            pltpu.SemaphoreType.DMA((16,)),
        ],
        2 * length * width * width * 8 + 2 * length * length * width * 10,
        52_000_000,
    )


def index_of(v, i):
    return lax.dynamic_index_in_dim(v, i, 0, keepdims=False)


class Grid:
    def __init__(self):
        dp, seq = lax.axis_index("dp"), lax.axis_index("seq")
        self.z, self.x, self.y, self.c = dp // 2, dp % 2, seq // 2, seq % 2
        places = [(z, x, y, c) for z in range(4) for x in range(2) for y in range(2) for c in range(2)]
        flat = lambda z, x, y, c: (z * 2 + x) * 4 + y * 2 + c
        to = lambda move: [(flat(*p), flat(*move(*p))) for p in places]
        self.perm_c = to(lambda z, x, y, c: (z, x, y, 1 - c))
        self.perm_x = to(lambda z, x, y, c: (z, 1 - x, y, c))
        self.perm_y = to(lambda z, x, y, c: (z, x, 1 - y, c))
        self.perm_z = [to(lambda z, x, y, c, k=k: (z ^ k, x, y, c)) for k in range(4)]

    def over_c(self, v):
        return lax.ppermute(v, LINES, self.perm_c)

    def over_x(self, v):
        return lax.ppermute(v, LINES, self.perm_x)

    def over_y(self, v):
        return lax.ppermute(v, LINES, self.perm_y)

    def over_z(self, v, k):
        return lax.ppermute(v, LINES, self.perm_z[k])

    def planes(self, block, before=(), after=()):
        block = tie(block, *before)
        parts = [tie(block, *after)] + [self.over_z(block, k) for k in (1, 2, 3)]
        order = jnp.stack([self.z ^ k for k in range(4)]).astype(jnp.int32)
        return place(parts, order, [(0, block.shape[0])])[0]


class Gathering:
    def __init__(self, grid, own, cut):
        self.grid, self.own, self.cut = grid, own, cut

    def first(self, *after):
        own = tie(self.own, *after)
        self.by_x, self.by_y = self.grid.over_x(own), self.grid.over_y(own)
        return [self.by_x, self.by_y]

    def second(self, *after):
        a, b = tie(self.by_x, *after), tie(self.by_y, *after)
        self.both = [self.grid.over_y(a[:, : self.cut]), self.grid.over_x(b[:, self.cut :])]
        return self.both

    def pieces(self, *after):
        here = [self.own, self.by_x, self.by_y, *(tie(v, *after) for v in self.both)]
        return here + [self.grid.over_c(v) for v in here]


class Reduction:
    def __init__(self, grid, *pieces):
        flat = lambda v: v.reshape(v.shape[0], -1, WIDE)
        self.mine = flat(pieces[0])
        self.came = [flat(grid.over_c(v)) for v in pieces[1:]]
        self.rows = self.mine.shape[1]

    def other(self, i, half, *rest):
        array, at = place_in(len(self.came), half, i)
        return self.came[array], lambda meta, ref: ref.at[(at, *[f(meta) for f in rest])]

    def part(self, i, half):
        return (self.mine, lambda meta, ref: ref.at[4 * half + i]), self.other(i, half)

    def at_plane(self, half, plane, count):
        rows = self.rows // 4

        def inside(first):
            return lambda meta, ref: ref.at[pl.ds(pl.multiple_of(first + plane(meta) * rows, 16), count)]

        def at(meta):
            return pl.ds(pl.multiple_of(plane(meta) * rows, 16), count)

        def own(meta, ref):
            return ref.at[4 * half, at(meta)]

        cells = [self.straight[half], self.last[half]]
        return [(self.mine, own), self.other(0, half, at)] + [(v, inside(first)) for v, first in cells]

    def counts(self):
        return DEEP // 2, self.rows // 4


def cell(v, first, rows):
    return v, lambda meta, ref: ref.at[pl.ds(first, rows)]


def step(grid, meta, after, seconds, firsts):
    tasks = Tasks(2)
    ends = []
    for r in seconds:
        for half in (0, 1):
            terms = r.part(1 + half, half) + (cell(*r.diagonal[half], r.rows),)
            ends.append((r, half, "last", 1 - half, tasks.add(1 - half, r.rows, *terms)))
    for r in firsts:
        for half in (0, 1):
            rows = r.rows
            ends.append((r, half, "diagonal", half, tasks.add(half, rows, *r.part(3, half))))
            ends.append((r, half, "straight", half, tasks.add(half, rows, *r.part(2 - half, half))))
    sent = tasks.run(meta, after)
    came = [grid.over_y(sent[0]), grid.over_x(sent[1])]
    for r, half, name, way, first in ends:
        if not hasattr(r, name):
            setattr(r, name, [None, None])
        getattr(r, name)[half] = (came[way], first)
    return sent, came


class Planes:
    def __init__(self, grid, meta, *reductions, at_once=False, after=()):
        self.grid, self.meta = grid, meta
        self.depth = sum(sum(r.counts()) for r in reductions)
        z = lambda meta: meta[4]
        if at_once:
            planes = [[lambda meta, k=k: z(meta) ^ k] for k in range(4)]
        else:
            planes = [[lambda meta, k=k, q=q: (z(meta) // 2 ^ k) * 2 + q for q in range(2)] for k in range(2)]
        tasks = Tasks(len(planes))
        tasks.kinds[0] = F32
        for out, group in enumerate(planes):
            for plane in group:
                for r in reductions:
                    for half in (0, 1):
                        tasks.add(out, r.counts()[half], *r.at_plane(half, plane, r.counts()[half]))
        self.kept, *sent = tasks.run(meta, after)
        self.sent = sent
        self.came = [grid.over_z(v, k) for v, k in zip(sent, (1, 2, 3) if at_once else (2,))]

    def second(self, *after):
        rows = self.depth
        tasks = Tasks(2)
        tasks.kinds[0] = F32
        for out in (0, 1):
            view = lambda meta, ref, out=out: ref.at[
                pl.ds(pl.multiple_of((meta[4] % 2 ^ out) * rows, 16), rows)
            ]
            tasks.add(out, rows, (self.kept, view), (self.came[0], view))
        self.kept, sent = tasks.run(self.meta, after)
        self.came = [self.grid.over_z(sent, 1)]

    def sums(self, layout, *after):
        return own_and_other(self.grid, self.meta, layout, tie(self.kept, *after), *self.came)


def own_and_other(grid, meta, layout, kept, *came):
    leave = sum(chunks * rows // 2 for _, chunks, rows in layout)
    count = len(came)

    def body(meta, kept, *refs):
        came, total, out = refs[:count], refs[count], refs[count + 1]
        total[...] = sum((v[...].astype(F32) for v in came), kept[...].astype(F32))
        at = 0
        for first, chunks, rows in layout:
            half = rows // 2
            for q in range(chunks):
                start = first + rows * q + half * (1 - meta[2])
                out[at : at + half] = total[pl.ds(pl.multiple_of(start, 8), half)]
                at += half

    total, out = call(
        body,
        [meta, kept, *came],
        [shape(kept.shape, F32), shape((leave, WIDE), F32)],
        [SMEM] + [VMEM] * (1 + count),
        [VMEM] * 2,
        [],
        0,
        5_000_000,
        limit=16,
    )
    return total, grid.over_c(out)


def tie(v, *after):
    return lax.optimization_barrier((v, *after))[0] if after else v


def seq_swaps(pieces_of, cuts):
    me, count = lax.axis_index("seq"), lax.axis_size("seq")
    kept = [pieces_of(me)]
    for r in range(1, count):
        kept.append(lax.ppermute(pieces_of(me ^ r), "seq", [(s, s ^ r) for s in range(count)]))
    order = jnp.stack([me ^ r for r in range(count)]).astype(jnp.int32)
    return lambda *after: place([tie(kept[0], *after), *kept[1:]], order, cuts)


def swap_all(grid, v, cuts):
    y, c = grid.y, grid.c
    pairs = v.reshape(2, 2, *v.shape[1:])
    stay = index_of(pairs, y)
    came = grid.over_y(index_of(pairs, 1 - y))
    other = grid.over_c(jnp.stack([index_of(stay, 1 - c), index_of(came, 1 - c)]))
    order = jnp.stack([y * 2 + c, (1 - y) * 2 + c, y * 2 + 1 - c, (1 - y) * 2 + 1 - c]).astype(jnp.int32)
    own = index_of(stay, c)
    return lambda *after: place(
        [tie(own, *after), index_of(came, c), other[0], other[1]], order, cuts
    )


def to_blocks(*arrays):
    quarter, width = arrays[0].shape[1:]
    cuts = [(quarter * k, quarter) for k in range(len(arrays))]
    end = seq_swaps(lambda s: jnp.concatenate([index_of(v, s) for v in arrays]), cuts)
    return lambda *after: [v.reshape(-1, width) for v in end(*after)]


def from_block(v, quarter):
    parts = v.reshape(-1, quarter, v.shape[-1])
    end = seq_swaps(lambda s: index_of(parts, s), [(0, quarter)])
    return lambda *after: end(*after)[0]


def both_halves(matrix):
    rows, wide = matrix.shape
    return matrix.reshape(rows, 2, wide // 2 // WIDE, WIDE).transpose(1, 2, 0, 3)


def lower_gains(ln1_gain, ln2_gain):
    return jnp.stack([ln1_gain, ln2_gain]).astype(BF)


def own_chunks(masters, core):
    views = []
    for l in range(masters[0].shape[0]):
        for ref, chunks in zip(masters, (3, 1, 4, 1)):
            for q in range(chunks):
                start = core * (ref.shape[2] // 2) + WIDE * q
                views.append(ref[l, :, pl.ds(pl.multiple_of(start, 128), WIDE)])
    return views


def chip_blocks(grid, meta, ln1_gain, ln2_gain, masters):
    layers, rows = masters[0].shape[:2]
    total = layers * 4 * 4 * rows * 3 // 4

    def leave(meta, one, two, *refs):
        ins, out = refs[:4], refs[4]
        start = 0
        for v in own_chunks(ins, 1 - meta[2]):
            out[start : start + v.shape[0]] = v
            start += v.shape[0]
        out[start : start + 8] = jnp.zeros((8, WIDE), F32)
        out[start : start + layers, :rows] = one[...]
        out[start + layers : start + 2 * layers, :rows] = two[...]

    size = sum(v.size for v in masters) * 8
    sent = call(
        leave,
        [meta, ln1_gain, ln2_gain, *masters],
        shape((total + 8, WIDE), F32),
        [SMEM] + [VMEM] * 6,
        VMEM,
        [],
        0,
        size,
        limit=16,
    )
    came = grid.over_c(sent)

    def merge(meta, sent, came, *refs):
        ins, outs, stage = refs[:4], refs[4:-1], refs[-1]
        core = meta[2]
        start = 0
        for v in own_chunks(ins, core):
            depth = v.shape[0]
            stage[pl.ds(pl.multiple_of(2 * start + core * depth, 8), depth)] = v
            stage[pl.ds(pl.multiple_of(2 * start + (1 - core) * depth, 8), depth)] = came[start : start + depth]
            start += depth
        stage[pl.ds(pl.multiple_of(2 * start + core * 8, 8), 8)] = sent[start : start + 8]
        stage[pl.ds(pl.multiple_of(2 * start + (1 - core) * 8, 8), 8)] = came[start : start + 8]
        first = 0
        for j, out in enumerate(outs):
            depth = DEEP * (1 + j % 2)
            out[:depth] = stage[first : first + depth].astype(BF)
            first += depth
        outs[0][DEEP:] = stage[first:].astype(BF)

    outs = [
        shape((DEEP * (1 + j % 2) + (GAIN_ROWS if j == 0 else 0), WIDE), BF) for j in range(2 * layers)
    ]
    return call(
        merge,
        [meta, sent, came, *masters],
        outs,
        [SMEM] + [VMEM] * 6,
        [VMEM] * len(outs),
        [pltpu.VMEM((2 * total + GAIN_ROWS, WIDE), F32)],
        0,
        size,
        limit=20,
    )


def finish(meta, sums, rows, width):
    layers = len(sums)

    def body(meta, *refs):
        count = 4 * layers
        ins, (one, two, *outs) = refs[:count], refs[count:]
        core = meta[2]
        for l in range(layers):
            feed, came, attn, came_attn = ins[4 * l : 4 * l + 4]

            def put(out, q, total, first, depth, came, at):
                half = out.shape[2] // 2
                columns = lambda c: pl.ds(pl.multiple_of(c * half + WIDE * q, 128), WIDE)
                out[l, :, columns(core)] = total[pl.ds(pl.multiple_of(first + core * depth, 8), depth)]
                out[l, :, columns(1 - core)] = came[at : at + depth]

            put(outs[3], 0, feed, DEEP, 4 * rows, came, 4 * rows)
            for q in range(4):
                put(outs[2], q, feed, 2 * rows * q, rows, came, q * rows)
            for q in range(3):
                put(outs[0], q, attn, 2 * rows * q, rows, came_attn, q * rows)
            put(outs[1], 0, attn, 6 * rows, rows, came_attn, 3 * rows)
            for g, out in enumerate((one, two)):
                both = attn[DEEP + g : DEEP + g + 1, : 2 * rows]
                out[l : l + 1] = jnp.where(core == 0, both[:, :rows], both[:, rows:])

    gain = shape((layers, rows), F32)
    outs = [gain, gain] + [
        shape((layers, r, w), F32)
        for r, w in ((rows, 3 * width), (rows, width), (rows, 4 * width), (4 * rows, width))
    ]
    flat = [v for l in range(layers) for v in sums[l]]
    one, two, qkv, out, up, down = call(
        body,
        [meta, *flat],
        outs,
        [SMEM] + [VMEM] * len(flat),
        [VMEM] * len(outs),
        [],
        0,
        8 * sum(v.size for v in flat),
        limit=20,
    )
    return one, qkv, out, two, up, down


def whole_gains(grid, gathering, layers, rows):
    g = gathering
    diagonal = g.both[1][:, -GAIN_ROWS:]
    tails = jnp.stack([v[:, -GAIN_ROWS:, :rows] for v in (g.own, g.by_x, g.by_y, diagonal)])
    tails = tails.reshape(2, 2, 4, 2, 8, rows)[:, :, :, :, : 2 * layers]
    tails = jnp.where(grid.y == 0, tails, tails[::-1])
    tails = jnp.where(grid.x == 0, tails, tails[:, ::-1])
    return tails.transpose(4, 2, 1, 0, 3, 5).reshape(2, layers, -1)


def pieces_of_whole(matrices):
    parts = []
    for whole in matrices:
        rows, wide = whole.shape
        parts.append(
            whole.reshape(4, 4, rows // 16, 2, wide // 2 // WIDE, WIDE).transpose(3, 1, 0, 4, 2, 5)
            .reshape(2, 4, 4, -1, WIDE)
        )
    stacked = jnp.concatenate(parts, 3)
    order = [(i & 1) * 2 + (i >> 1) for i in range(4)]
    return [stacked[side, order[i]] for side in range(2) for i in range(4)]


def whole_of_pieces(*pieces, widths):
    cut = DEEP // 2
    sides = []
    for arrays in (pieces[:1], pieces[1:]):
        places = [[place_in(len(arrays), half, i) for i in range(4)] for half in (0, 1)]
        sides.append([jnp.stack([arrays[array][at] for array, at in row]) for row in places])
    both = [jnp.concatenate([a[:, :, :cut], b[:, :, :cut]], 2) for a, b in sides]
    stacked = jnp.stack(both)
    stacked = jnp.stack([stacked[:, i] for i in (0, 2, 1, 3)], 1)
    outs, start = [], 0
    for rows, wide in widths:
        depth, chunks = rows // 16, wide // 2 // WIDE
        part = stacked[:, :, :, start : start + depth * chunks]
        start += depth * chunks
        outs.append(
            part.reshape(2, 4, 4, chunks, depth, WIDE).transpose(2, 1, 4, 0, 3, 5).reshape(rows, wide)
        )
    return outs


def per_device(
    states,
    item_halves,
    ln1_gain,
    qkv_weight,
    out_weight,
    ln2_gain,
    up_weight,
    down_weight,
    cotangent,
):
    masters = (qkv_weight, out_weight, up_weight, down_weight)
    layers, gain_shard = ln1_gain.shape
    quarter, width = states.shape[1:]
    near = lax.axis_size("dp") == 8 and lax.axis_size("seq") == 4 and layers == 2
    gains = lower_gains(ln1_gain, ln2_gain)
    flag = index_of(item_halves, lax.axis_index("seq"))
    if near:
        return by_permutes(states, flag, ln1_gain, ln2_gain, masters, cotangent, quarter)
    zero = jnp.zeros((), jnp.int32)
    meta = jnp.stack([zero, zero, zero, flag]).astype(jnp.int32)
    x, grad = to_blocks(states, cotangent)()
    gains = lax.all_gather(gains, LINES, axis=2, tiled=True).astype(F32)
    kept = []
    for l in range(layers):
        qkv, out, up, down = (
            lax.all_gather(v[l].astype(BF), LINES, axis=0, tiled=True) for v in masters
        )
        attn, feed = pieces_of_whole([qkv, out]), pieces_of_whole([up, down])
        qkv, o, m = attend_forward(meta, x, gains[0, l][None], attn)
        u, a, y = feed_forward(meta, m, gains[1, l][None], feed)
        kept.append((x, qkv, o, m, u, a, attn, feed))
        x = y
    outputs = x
    results = [None] * layers
    for l in reversed(range(layers)):
        x, qkv, o, m, u, a, attn, feed = kept[l]
        down_pieces = down_backward(meta, grad, a)
        dm, gg_two, *up_pieces = feed_backward(meta, grad, m, u, gains[1, l][None], feed)
        grad, *attn_pieces = attend_backward(meta, dm, x, qkv, o, gains[0, l][None], gg_two, attn)
        wholes = (
            whole_of_pieces(*attn_pieces, widths=((width, 3 * width), (width, width)))
            + whole_of_pieces(*up_pieces, widths=((width, 4 * width),))
            + whole_of_pieces(*down_pieces, widths=((4 * width, width),))
        )
        gain_sums = attn_pieces[0][:4, :, DEEP // 2 :, : width // 16]
        gain_sums = jnp.stack([gain_sums[i] for i in (0, 2, 1, 3)]).transpose(2, 1, 0, 3).reshape(GAIN_ROWS, width)
        sums = [
            lax.psum_scatter(v.astype(F32), LINES, scatter_dimension=0, tiled=True) for v in wholes
        ]
        gain_sums = lax.psum(gain_sums[:2].astype(F32), LINES)
        owner = lax.axis_index(LINES) * gain_shard
        results[l] = (lax.dynamic_slice_in_dim(gain_sums, owner, gain_shard, 1), *sums)
    return collect(from_block(outputs, quarter)(), from_block(grad, quarter)(), results)


def collect(outputs, grad_states, results):
    gains, qkv, out, up, down = (jnp.stack([r[k] for r in results]) for k in range(5))
    return outputs, grad_states, gains[:, 0], qkv, out, gains[:, 1], up, down


def by_permutes(states, flag, ln1_gain, ln2_gain, masters, cotangent, quarter):
    grid = Grid()
    meta = jnp.stack([grid.x, grid.y, grid.c, flag, grid.z]).astype(jnp.int32)
    layers, rows = masters[0].shape[:2]
    width = states.shape[2]
    blocks = chip_blocks(grid, meta, ln1_gain, ln2_gain, masters)
    come = swap_all(
        grid,
        jnp.concatenate([tie(states, blocks[0]), cotangent], 1),
        [(0, quarter), (quarter, quarter)],
    )
    feed1 = lax.all_gather(blocks[3], LINES, axis=0, tiled=True)
    feed1 = [feed1.reshape(4, 4, 2, 2 * DEEP, WIDE)]
    own = grid.planes(blocks[0])
    attn0 = Gathering(grid, own, DEEP // 2)
    attn0.first()
    own = grid.planes(blocks[1], (own,), (attn0.by_x, attn0.by_y))
    attn0.second()
    x, grad = (v.reshape(-1, width) for v in come(*attn0.both))
    feed0 = Gathering(grid, own, DEEP)
    feed0.first(*attn0.both)
    gains = whole_gains(grid, attn0, layers, rows).astype(F32)
    attn0 = attn0.pieces()
    qkv0, o0, m0 = attend_forward(meta, x, gains[0, 0][None], attn0)
    own = grid.planes(blocks[2], (own,), (m0,))
    feed0.second(m0, own)
    attn1 = Gathering(grid, own, DEEP // 2)
    attn1.first(feed0.by_x, feed0.by_y)
    attn1.second()
    feed0 = feed0.pieces()
    u0, a0, x1 = feed_forward(meta, tie(m0, attn1.by_x, attn1.by_y), gains[1, 0][None], feed0)
    attn1 = attn1.pieces(x1)
    qkv1, o1, m1 = attend_forward(meta, x1, gains[0, 1][None], attn1)
    y, dm, gg_two, whole = feed_both(meta, m1, grad, gains[1, 1][None], feed1)
    whole = lax.psum_scatter(whole.reshape(-1, WIDE), LINES, scatter_dimension=0, tiled=True)
    grad, *pieces = attend_backward(meta, dm, x1, qkv1, o1, gains[0, 1][None], gg_two, attn1)
    attn1 = Reduction(grid, *pieces)
    down_pieces = down_backward(meta, grad, a0)
    down0 = Reduction(grid, *down_pieces)
    ready, came1 = step(grid, meta, (down_pieces[0],), (), (attn1,))
    dm, gg_two, *pieces = feed_backward(
        meta, tie(grad, down_pieces[0], *ready), m0, u0, gains[1, 0][None], feed0
    )
    up0 = Reduction(grid, *pieces)
    ready, came2 = step(grid, meta, (dm, *came1), (attn1,), (down0,))
    dm = tie(dm, *ready)
    grad, *pieces = attend_backward(meta, dm, x, qkv0, o0, gains[0, 0][None], gg_two, attn0)
    attn0 = Reduction(grid, *pieces)
    sent, came3 = step(grid, meta, (grad, *attn0.came[:2], up0.came[0], *came2), (down0,), (up0, attn0))
    planes_attn1 = Planes(grid, meta, attn1, at_once=True, after=sent)
    sent, came4 = step(grid, meta, (*planes_attn1.came, *came3), (up0, attn0), ())
    feed = ((0, 4, 2 * rows), (DEEP, 1, DEEP))
    attend = ((0, 4, 2 * rows),)
    both = (*feed, (2 * DEEP, 4, 2 * rows))
    sums_attn1 = planes_attn1.sums(attend, *sent)
    planes0 = Planes(grid, meta, up0, down0, attn0, at_once=True)
    results = jnp.concatenate([v.reshape(4, quarter, width) for v in (tie(y, *planes0.sent), grad)], 1)
    results = swap_all(grid, results, [(0, quarter), (quarter, quarter)])
    outputs, grad_states = results(*planes0.came)
    sums1 = own_and_other(grid, meta, feed, tie(whole, *planes0.sent))
    total, came = planes0.sums(both)
    cut = 2 * DEEP
    sums0 = (total[:cut], came[: cut // 2], total[cut:], came[cut // 2 :])
    return outputs, grad_states, *finish(meta, (sums0, (*sums1, *sums_attn1)), rows, width)


def solution(mesh):
    rows = P(None, LINES, None)
    tokens = P("dp", "seq", None)
    gain = P(None, LINES)
    return jax.shard_map(
        per_device,
        mesh=mesh,
        in_specs=(tokens, P("dp"), gain, rows, rows, gain, rows, rows, tokens),
        out_specs=(tokens, tokens, gain, rows, rows, gain, rows, rows),
        check_vma=False,
    )
```

```python
import jax
import jax.numpy as jnp
from jax import lax
from jax.experimental import pallas as pl
from jax.experimental.pallas import tpu as pltpu
from jax.sharding import PartitionSpec as P

HEAD_DIM = 64
EPSILON = 1e-05
BF = jnp.bfloat16
F32 = jnp.float32
LINES = ("dp", "seq")
WIDE = 384
DEEP = 192
GAIN_ROWS = 16
VMEM = pl.BlockSpec(memory_space=pltpu.VMEM)
SMEM = pl.BlockSpec(memory_space=pltpu.SMEM)
HBM = pl.BlockSpec(memory_space=pl.ANY)


def call(body, ins, outs, specs, out_specs, scratch, flops, size, limit=58):
    return pl.pallas_call(
        body,
        out_shape=outs,
        in_specs=specs,
        out_specs=out_specs,
        scratch_shapes=scratch,
        cost_estimate=pl.CostEstimate(
            flops=flops, bytes_accessed=6 * size, transcendentals=0
        ),
        compiler_params=pltpu.CompilerParams(vmem_limit_bytes=limit * 1024 * 1024),
    )(*ins)


def shape(dims, dtype):
    return jax.ShapeDtypeStruct(dims, dtype)


def mat(a, b):
    return jnp.dot(a, b, preferred_element_type=F32)


def mat_t(a, b):
    return lax.dot_general(a, b, (((1,), (1,)), ((), ())), preferred_element_type=F32)


def t_mat(a, b):
    return lax.dot_general(a, b, (((0,), (0,)), ((), ())), preferred_element_type=F32)


def normed(v):
    average = jnp.mean(v, -1, keepdims=True)
    centered = v - average
    variance = jnp.mean(centered * centered, -1, keepdims=True)
    root = lax.rsqrt(variance + EPSILON)
    return centered * root, root


def norm_back(n, root, g):
    return root * (
        g - jnp.mean(g, -1, keepdims=True) - n * jnp.mean(g * n, -1, keepdims=True)
    )


def bell(u):
    return 0.5 * (1.0 + lax.erf(u * 0.7071067811865476))


def place(pieces, where_to, cuts):
    count = len(pieces)

    def body(to, *refs):
        for k in range(count):
            for (start, rows), out in zip(cuts, refs[count:]):
                out[to[k]] = refs[k][start : start + rows]

    one = pieces[0]
    return call(
        body,
        [where_to, *pieces],
        [shape((count, rows, one.shape[1]), one.dtype) for _, rows in cuts],
        [SMEM] + [VMEM] * count,
        [VMEM] * len(cuts),
        [],
        0,
        2 * count * one.size * one.dtype.itemsize,
        limit=16,
    )


def combine(meta, arrays, outs, tasks, after=()):
    count = len(arrays)
    terms = [(rows, term) for _, _, rows, sources in tasks for term in sources]

    def body(meta, *refs):
        ins, results, held = refs[:count], refs[count : count + len(outs)], refs[count + len(outs) : -1]
        sems = refs[-1]
        copies = [
            pltpu.make_async_copy(view(meta, ins[place_of]), held[k], sems.at[k])
            for k, (_, (place_of, view)) in enumerate(terms)
        ]
        start_all(copies)
        k = 0
        for result, first, rows, sources in tasks:
            wait_all(copies[k : k + len(sources)])
            step = 64 if rows % 64 == 0 else 16

            def some(r, _, k=k, result=result, first=first, step=step, sources=sources):
                at = pl.multiple_of(r * step, 16)
                total = sum(held[k + j][pl.ds(at, step)].astype(F32) for j in range(len(sources)))
                to = pl.multiple_of(first + at, 16)
                results[result][pl.ds(to, step)] = total.astype(results[result].dtype)
                return 0

            lax.fori_loop(0, rows // step, some, 0)
            k += len(sources)

    arrays = [tie(arrays[0], *after), *arrays[1:]]
    return call(
        body,
        [meta, *arrays],
        [shape((rows, WIDE), kind) for rows, kind in outs],
        [SMEM] + [HBM] * count,
        [VMEM] * len(outs),
        [pltpu.VMEM((rows, WIDE), arrays[term[0]].dtype) for rows, term in terms]
        + [pltpu.SemaphoreType.DMA((len(terms),))],
        0,
        60_000_000,
    )


class Tasks:
    def __init__(self, outs):
        self.arrays, self.tasks, self.rows, self.kinds = [], [], [0] * outs, [BF] * outs

    def add(self, out, rows, *terms):
        sources = []
        for array, view in terms:
            known = [k for k, v in enumerate(self.arrays) if v is array]
            if not known:
                self.arrays.append(array)
            sources.append((known[0] if known else len(self.arrays) - 1, view))
        first = self.rows[out]
        self.tasks.append((out, first, rows, sources))
        self.rows[out] += rows
        return first

    def run(self, meta, after=()):
        return combine(meta, self.arrays, list(zip(self.rows, self.kinds)), self.tasks, after)


def chip_row(meta, i):
    return (meta[0] ^ (i & 1)) * 2 + (meta[1] ^ (i >> 1))


def columns(meta, side, half, q):
    start = (meta[2] ^ side) * half + WIDE * q
    return pl.ds(pl.multiple_of(start, 128), WIDE)


def place_in(count, half, i):
    if count == 1:
        return 0, 4 * half + i
    if count == 2:
        return (0, 2 * half + (0 if i == 3 else 1)) if i in (3, 2 - half) else (1, 2 * half + (1 if i == 0 else 0))
    if i == 3 or i == 2 - half:
        return half, 0 if i == 3 else 1
    return 2, 2 * half + (1 if i == 0 else 0)


def piece_at(pieces, i, start, rows):
    if len(pieces) < 4:
        half = start // (DEEP // 2)
        array, at = place_in(len(pieces), half, i)
        return pieces[array].at[at, :, pl.ds(start - half * (DEEP // 2), rows), :]
    if i == 3 and len(pieces) == 5:
        cut = pieces[3].shape[1]
        if start >= cut:
            return pieces[4].at[:, pl.ds(start - cut, rows), :]
    return pieces[i].at[:, pl.ds(start, rows), :]


def chunked(meta, sides, target, sems, first, chunks, to_pieces=False, split=1):
    half = target.shape[-1] // 2
    rows = target.shape[2]
    step = rows // split
    whole = not isinstance(sides, (list, tuple))
    copies = []
    for side in range(2):
        for i in range(4):
            for q in range(chunks):
                for k in range(split):
                    start = first + rows * q + step * k
                    if whole:
                        a = sides.at[:, i, side, pl.ds(start, step), :]
                        place_of, lanes = i, pl.ds(side * half + WIDE * q, WIDE)
                    else:
                        a = piece_at(sides[side], i, start, step)
                        place_of, lanes = chip_row(meta, i), columns(meta, side, half, q)
                    b = target.at[:, place_of, pl.ds(step * k, step), lanes]
                    pair = (b, a) if to_pieces else (a, b)
                    copies.append(pltpu.make_async_copy(*pair, sems.at[len(copies)]))
    return copies


def pieces_of_refs(refs):
    count = len(refs)
    return refs[0] if count == 1 else (refs[: count // 2], refs[count // 2 :])


def start_all(copies):
    for copy in copies:
        copy.start()


def wait_all(copies):
    for copy in copies:
        copy.wait()


def attention_bias(flag, length):
    row = lax.broadcasted_iota(jnp.int32, (length, length), 0) // (length // 2)
    column = lax.broadcasted_iota(jnp.int32, (length, length), 1) // (length // 2)
    return jnp.where(jnp.logical_or(row == column, flag == 0), 0.0, -1e30)


def probabilities(queries, keys, bias):
    s = mat_t(queries, keys) * HEAD_DIM ** (-0.5) + bias
    e = jnp.exp(s - jnp.max(s, -1, keepdims=True))
    return e * (1.0 / jnp.sum(e, -1, keepdims=True))


def head_lanes():
    return lax.broadcasted_iota(jnp.int32, (1, 2 * HEAD_DIM), 1) // HEAD_DIM


def only(lanes, j, v):
    return jnp.where(lanes == j, v, jnp.zeros_like(v))


def tile(ref, t, width):
    z, xy, rows, _ = ref.shape
    return ref[:, :, :, t * width : (t + 1) * width].reshape(z * xy * rows, width)


def attend_forward(meta, x, gain, pieces):
    count = len(pieces)
    length, width = x.shape
    pairs = width // (2 * HEAD_DIM)

    def body(meta, x_ref, gain_ref, *refs):
        src = pieces_of_refs(refs[:count])
        qkv_ref, o_ref, m_ref, wqkv, wo, sems_a, sems_b = refs[count:]
        load_a = chunked(meta, src, wqkv, sems_a, 0, 3)
        load_b = chunked(meta, src, wo, sems_b, width * 3 // 16, 1)
        start_all(load_a)
        start_all(load_b)
        bias = attention_bias(meta[3], length)
        n, _ = normed(x_ref[...])
        hidden = (n * gain_ref[...]).astype(BF)
        wait_all(load_a)
        for t in range(3):
            qkv_ref[:, t * width : (t + 1) * width] = mat(hidden, tile(wqkv, t, width)).astype(BF)
        lanes = head_lanes()

        def pair(p, _):
            take = lambda part: qkv_ref[
                :, pl.ds(pl.multiple_of(part * width + p * 2 * HEAD_DIM, 128), 2 * HEAD_DIM)
            ]
            q, k, v = take(0), take(1), take(2)
            outs = [
                mat(probabilities(only(lanes, j, q), k, bias).astype(BF), v) for j in range(2)
            ]
            o_ref[:, pl.ds(pl.multiple_of(p * 2 * HEAD_DIM, 128), 2 * HEAD_DIM)] = jnp.where(
                lanes == 0, outs[0], outs[1]
            ).astype(BF)
            return 0

        lax.fori_loop(0, pairs, pair, 0, unroll=True)
        wait_all(load_b)
        m_ref[...] = x_ref[...] + mat(o_ref[...], tile(wo, 0, width))

    return call(
        body,
        [meta, x, gain, *pieces],
        (shape((length, 3 * width), BF), shape((length, width), BF), shape((length, width), F32)),
        [SMEM, VMEM, VMEM] + [HBM] * count,
        (VMEM,) * 3,
        [
            pltpu.VMEM((4, 4, width // 16, 3 * width), BF),
            pltpu.VMEM((4, 4, width // 16, width), BF),
            pltpu.SemaphoreType.DMA((24,)),
            pltpu.SemaphoreType.DMA((8,)),
        ],
        2 * length * width * width * 4 + 4 * length * length * width * 2,
        36_000_000,
    )


def feed_forward(meta, m, gain, pieces):
    count = len(pieces)
    length, width = m.shape
    wide = 4 * width

    def body(meta, m_ref, gain_ref, *refs):
        src = pieces_of_refs(refs[:count])
        u_ref, a_ref, y_ref, wu, wd, sems_a, sems_b = refs[count:]
        load_a = chunked(meta, src, wu, sems_a, 0, 4)
        load_b = chunked(meta, src, wd, sems_b, width // 4, 1)
        start_all(load_a)
        start_all(load_b)
        n, _ = normed(m_ref[...])
        hidden = (n * gain_ref[...]).astype(BF)
        wait_all(load_a)
        wait_all(load_b)
        total = m_ref[...]
        for t in range(4):
            u = mat(hidden, tile(wu, t, width))
            u_ref[:, t * width : (t + 1) * width] = u
            a = (u * bell(u)).astype(BF)
            a_ref[:, t * width : (t + 1) * width] = a
            total = total + mat(a, wd[t].reshape(width, width))
        y_ref[...] = total

    return call(
        body,
        [meta, m, gain, *pieces],
        (shape((length, wide), F32), shape((length, wide), BF), shape((length, width), F32)),
        [SMEM, VMEM, VMEM] + [HBM] * count,
        (VMEM,) * 3,
        [
            pltpu.VMEM((4, 4, width // 16, wide), BF),
            pltpu.VMEM((4, 4, width // 4, width), BF),
            pltpu.SemaphoreType.DMA((32,)),
            pltpu.SemaphoreType.DMA((8,)),
        ],
        2 * length * width * wide * 2,
        26_000_000,
    )


def piece_shapes(rows, parts):
    part = lambda count: shape((count, 4, rows, WIDE), BF)
    others = {1: (part(8),), 2: (part(4), part(4)), 3: (part(2), part(2), part(4))}
    return (part(8),) + others[parts]


def whole_shape():
    return shape((4, 4, 2, 2 * DEEP, WIDE), BF)


def down_backward(meta, dy, a):
    length, width = dy.shape

    def body(meta, dy_ref, a_ref, *refs):
        *outs, stage, sems = refs
        low = dy_ref[...].astype(BF)
        for t in range(4):
            stage[t] = (
                t_mat(a_ref[:, t * width : (t + 1) * width], low)
                .astype(BF)
                .reshape(4, width // 4, width)
            )
        copies = chunked(meta, (outs[:1], outs[1:]), stage, sems, 0, 1, True, 2)
        start_all(copies)
        wait_all(copies)

    outs = piece_shapes(DEEP // 2, 2)
    return call(
        body,
        [meta, dy, a],
        outs,
        [SMEM, VMEM, VMEM],
        (HBM,) * 3,
        [pltpu.VMEM((4, 4, width // 4, width), BF), pltpu.SemaphoreType.DMA((16,))],
        8 * length * width * width,
        13_000_000,
    )


def feed_backward(meta, dy, m, u, gain, pieces):
    count = len(pieces)
    length, width = m.shape
    wide = 4 * width

    def body(meta, dy_ref, m_ref, u_ref, gain_ref, *refs):
        src = pieces_of_refs(refs[:count])
        dm_ref, gg_ref, *outs = refs[count:-5]
        wu, wd, stage, sems_a, sems_b = refs[-5:]
        outs = outs[:1], outs[1:]
        load_a = chunked(meta, src, wu, sems_a, 0, 4)
        load_b = chunked(meta, src, wd, sems_b, width // 4, 1)
        start_all(load_b)
        start_all(load_a)
        n, root = normed(m_ref[...])
        gain = gain_ref[...]
        hidden_t = (n * gain).astype(BF).T
        low = dy_ref[...].astype(BF)
        wait_all(load_b)
        wait_all(load_a)
        dh = jnp.zeros((length, width), F32)
        for t in range(4):
            da = mat_t(low, wd[t].reshape(width, width))
            u = u_ref[:, t * width : (t + 1) * width]
            slope = bell(u) + u * (jnp.exp(-0.5 * u * u) * 0.3989422804014327)
            du = (da * slope).astype(BF)
            stage[:, :, :, t * width : (t + 1) * width] = (
                mat(hidden_t, du).astype(BF).reshape(4, 4, width // 16, width)
            )
            dh = dh + mat_t(du, tile(wu, t, width))
        store = chunked(meta, outs, stage, sems_a, 0, 4, True)
        start_all(store)
        gg_ref[...] = jnp.sum(dh * n, 0, keepdims=True)
        dm_ref[...] = dy_ref[...] + norm_back(n, root, dh * gain)
        wait_all(store)

    return call(
        body,
        [meta, dy, m, u, gain, *pieces],
        (shape((length, width), F32), shape((1, width), F32)) + piece_shapes(DEEP // 2, 2),
        [SMEM] + [VMEM] * 4 + [HBM] * count,
        (VMEM, VMEM) + (HBM,) * 3,
        [
            pltpu.VMEM((4, 4, width // 16, wide), BF),
            pltpu.VMEM((4, 4, width // 4, width), BF),
            pltpu.VMEM((4, 4, width // 16, wide), BF),
            pltpu.SemaphoreType.DMA((32,)),
            pltpu.SemaphoreType.DMA((8,)),
        ],
        2 * length * width * wide * 3,
        40_000_000,
    )


def feed_both(meta, m, dy, gain, pieces):
    length, width = m.shape
    wide = 4 * width
    count = len(pieces)

    def body(meta, m_ref, dy_ref, gain_ref, *refs):
        src = pieces_of_refs(refs[:count])
        y_ref, dm_ref, gg_ref, whole = refs[count : count + 4]
        wu, wd, a_ref, slope_ref, stage_u, stage_d, sems_a, sems_b, sems_c, sems_d = refs[count + 4 :]
        load_a = chunked(meta, src, wu, sems_a, 0, 4)
        load_b = chunked(meta, src, wd, sems_b, width // 4, 1)
        start_all(load_a)
        start_all(load_b)
        n, root = normed(m_ref[...])
        gain = gain_ref[...]
        hidden = (n * gain).astype(BF)
        hidden_t = (n * gain).astype(BF).T
        low = dy_ref[...].astype(BF)
        wait_all(load_a)
        for t in range(4):
            u = mat(hidden, tile(wu, t, width))
            share = bell(u)
            a = (u * share).astype(BF)
            a_ref[:, t * width : (t + 1) * width] = a
            slope_ref[:, t * width : (t + 1) * width] = share + u * (
                jnp.exp(-0.5 * u * u) * 0.3989422804014327
            )
            stage_d[t] = t_mat(a, low).astype(BF).reshape(4, width // 4, width)
        store_d = chunked(meta, whole, stage_d, sems_d, DEEP, 1, True)
        start_all(store_d)
        wait_all(load_b)
        dh = jnp.zeros((length, width), F32)
        for t in range(4):
            da = mat_t(low, wd[t].reshape(width, width))
            du = (da * slope_ref[:, t * width : (t + 1) * width]).astype(BF)
            stage_u[:, :, :, t * width : (t + 1) * width] = (
                mat(hidden_t, du).astype(BF).reshape(4, 4, width // 16, width)
            )
            dh = dh + mat_t(du, tile(wu, t, width))
        store_u = chunked(meta, whole, stage_u, sems_c, 0, 4, True)
        start_all(store_u)
        gg_ref[...] = jnp.sum(dh * n, 0, keepdims=True)
        dm_ref[...] = dy_ref[...] + norm_back(n, root, dh * gain)
        total = m_ref[...]
        for t in range(4):
            total = total + mat(a_ref[:, t * width : (t + 1) * width], wd[t].reshape(width, width))
        y_ref[...] = total
        wait_all(store_d)
        wait_all(store_u)

    return call(
        body,
        [meta, m, dy, gain, *pieces],
        (
            shape((length, width), F32),
            shape((length, width), F32),
            shape((1, width), F32),
            whole_shape(),
        ),
        [SMEM] + [VMEM] * 3 + [HBM] * count,
        (VMEM, VMEM, VMEM, HBM),
        [
            pltpu.VMEM((4, 4, width // 16, wide), BF),
            pltpu.VMEM((4, 4, width // 4, width), BF),
            pltpu.VMEM((length, wide), BF),
            pltpu.VMEM((length, wide), F32),
            pltpu.VMEM((4, 4, width // 16, wide), BF),
            pltpu.VMEM((4, 4, width // 4, width), BF),
            pltpu.SemaphoreType.DMA((32,)),
            pltpu.SemaphoreType.DMA((8,)),
            pltpu.SemaphoreType.DMA((32,)),
            pltpu.SemaphoreType.DMA((8,)),
        ],
        2 * length * width * wide * 6,
        60_000_000,
    )


def gain_place(pieces, half, i):
    array, at = place_in(len(pieces), half, i)
    return pieces[array].at[at, :, pl.ds(DEEP // 2, GAIN_ROWS), :]


def gain_rows(stage, one, two):
    width = one.shape[1]
    share = width // 16
    row = lax.broadcasted_iota(jnp.int32, (GAIN_ROWS, width), 0)
    both = jnp.where(row == 0, one, jnp.where(row == 1, two, 0.0))
    tall = jnp.broadcast_to(both[None], (16, GAIN_ROWS, width)).reshape(16 * GAIN_ROWS, width)
    chip = lax.broadcasted_iota(jnp.int32, tall.shape, 0) // GAIN_ROWS
    feature = lax.broadcasted_iota(jnp.int32, tall.shape, 1)
    tall = jnp.where(feature // share == chip, tall, 0.0).astype(BF)
    feature = lax.broadcasted_iota(jnp.int32, (width, 128), 0)
    lane = lax.broadcasted_iota(jnp.int32, (width, 128), 1)
    pick = jnp.where(feature % share == lane, 1.0, 0.0).astype(BF)
    stage[...] = jnp.zeros(stage.shape, BF)
    stage[:, :, :, :128] = mat(tall, pick).astype(BF).reshape(4, 4, GAIN_ROWS, 128)


def attend_backward(meta, dm, x, qkv, o, gain, gg_two, pieces):
    count = len(pieces)
    length, width = x.shape
    pairs = width // (2 * HEAD_DIM)
    scale = HEAD_DIM ** (-0.5)

    def body(meta, dm_ref, x_ref, qkv_ref, o_ref, gain_ref, gg_two_ref, *refs):
        src = pieces_of_refs(refs[:count])
        dx_ref = refs[count]
        outs = refs[count + 1 : count + 2], refs[count + 2 : count + 5]
        wqkv, wo, stage, stage_o, stage_g, do_ref, dqkv, sems_a, sems_b, sems_c = refs[count + 5 :]
        load_b = chunked(meta, src, wo, sems_b, width * 3 // 16, 1)
        load_a = chunked(meta, src, wqkv, sems_a, 0, 3)
        start_all(load_b)
        start_all(load_a)
        bias = attention_bias(meta[3], length)
        low = dm_ref[...].astype(BF)
        stage_o[...] = t_mat(o_ref[...], low).astype(BF).reshape(4, 4, width // 16, width)
        wait_all(load_b)
        do_ref[...] = mat_t(low, tile(wo, 0, width)).astype(BF)
        store_b = chunked(meta, outs, stage_o, sems_b, width * 3 // 16, 1, True)
        start_all(store_b)
        lanes = head_lanes()

        def pair(p, _):
            at = lambda part: pl.ds(
                pl.multiple_of(part * width + p * 2 * HEAD_DIM, 128), 2 * HEAD_DIM
            )
            q, k, v = qkv_ref[:, at(0)], qkv_ref[:, at(1)], qkv_ref[:, at(2)]
            d = do_ref[:, at(0)]
            dq, dk, dv = [], [], []
            for j in range(2):
                soft = probabilities(only(lanes, j, q), k, bias)
                dp = mat_t(only(lanes, j, d), v)
                ds = (soft * (dp - jnp.sum(dp * soft, -1, keepdims=True))).astype(BF)
                dv.append(t_mat(soft.astype(BF), d))
                dq.append(mat(ds, k) * scale)
                dk.append(t_mat(ds, q) * scale)
            for part, two in enumerate((dq, dk, dv)):
                dqkv[:, at(part)] = jnp.where(lanes == 0, two[0], two[1]).astype(BF)
            return 0

        lax.fori_loop(0, pairs, pair, 0, unroll=2)
        n, root = normed(x_ref[...])
        gain = gain_ref[...]
        hidden_t = (n * gain).astype(BF).T
        wait_all(load_a)
        dh = jnp.zeros((length, width), F32)
        for t in range(3):
            d = dqkv[:, t * width : (t + 1) * width]
            stage[:, :, :, t * width : (t + 1) * width] = (
                mat(hidden_t, d).astype(BF).reshape(4, 4, width // 16, width)
            )
            dh = dh + mat_t(d, tile(wqkv, t, width))
        store_a = chunked(meta, outs, stage, sems_a, 0, 3, True)
        start_all(store_a)
        gain_rows(stage_g, jnp.sum(dh * n, 0, keepdims=True), gg_two_ref[...])
        store_c = [
            pltpu.make_async_copy(
                stage_g.at[:, chip_row(meta, i)],
                gain_place(outs[side], half, i),
                sems_c.at[8 * half + 4 * side + i],
            )
            for half in range(2)
            for side in range(2)
            for i in range(4)
        ]
        start_all(store_c)
        dx_ref[...] = dm_ref[...] + norm_back(n, root, dh * gain)
        wait_all(store_a)
        wait_all(store_b)
        wait_all(store_c)

    return call(
        body,
        [meta, dm, x, qkv, o, gain, gg_two, *pieces],
        (shape((length, width), F32),) + piece_shapes(DEEP // 2 + GAIN_ROWS, 3),
        [SMEM] + [VMEM] * 6 + [HBM] * count,
        (VMEM,) + (HBM,) * 4,
        [
            pltpu.VMEM((4, 4, width // 16, 3 * width), BF),
            pltpu.VMEM((4, 4, width // 16, width), BF),
            pltpu.VMEM((4, 4, width // 16, 3 * width), BF),
            pltpu.VMEM((4, 4, width // 16, width), BF),
            pltpu.VMEM((4, 4, GAIN_ROWS, WIDE), BF),
            pltpu.VMEM((length, width), BF),
            pltpu.VMEM((length, 3 * width), BF),
            pltpu.SemaphoreType.DMA((24,)),
            pltpu.SemaphoreType.DMA((8,)),
            pltpu.SemaphoreType.DMA((16,)),
        ],
        2 * length * width * width * 8 + 2 * length * length * width * 10,
        52_000_000,
    )


def index_of(v, i):
    return lax.dynamic_index_in_dim(v, i, 0, keepdims=False)


class Grid:
    def __init__(self):
        dp, seq = lax.axis_index("dp"), lax.axis_index("seq")
        self.z, self.x, self.y, self.c = dp // 2, dp % 2, seq // 2, seq % 2
        places = [(z, x, y, c) for z in range(4) for x in range(2) for y in range(2) for c in range(2)]
        flat = lambda z, x, y, c: (z * 2 + x) * 4 + y * 2 + c
        to = lambda move: [(flat(*p), flat(*move(*p))) for p in places]
        self.perm_c = to(lambda z, x, y, c: (z, x, y, 1 - c))
        self.perm_x = to(lambda z, x, y, c: (z, 1 - x, y, c))
        self.perm_y = to(lambda z, x, y, c: (z, x, 1 - y, c))
        self.perm_z = [to(lambda z, x, y, c, k=k: (z ^ k, x, y, c)) for k in range(4)]

    def over_c(self, v):
        return lax.ppermute(v, LINES, self.perm_c)

    def over_x(self, v):
        return lax.ppermute(v, LINES, self.perm_x)

    def over_y(self, v):
        return lax.ppermute(v, LINES, self.perm_y)

    def over_z(self, v, k):
        return lax.ppermute(v, LINES, self.perm_z[k])

    def planes(self, block, before=(), after=()):
        block = tie(block, *before)
        parts = [tie(block, *after)] + [self.over_z(block, k) for k in (1, 2, 3)]
        order = jnp.stack([self.z ^ k for k in range(4)]).astype(jnp.int32)
        return place(parts, order, [(0, block.shape[0])])[0]


class Gathering:
    def __init__(self, grid, own, cut):
        self.grid, self.own, self.cut = grid, own, cut

    def first(self, *after):
        own = tie(self.own, *after)
        self.by_x, self.by_y = self.grid.over_x(own), self.grid.over_y(own)
        return [self.by_x, self.by_y]

    def second(self, *after):
        a, b = tie(self.by_x, *after), tie(self.by_y, *after)
        self.both = [self.grid.over_y(a[:, : self.cut]), self.grid.over_x(b[:, self.cut :])]
        return self.both

    def pieces(self, *after):
        here = [self.own, self.by_x, self.by_y, *(tie(v, *after) for v in self.both)]
        return here + [self.grid.over_c(v) for v in here]


class Reduction:
    def __init__(self, grid, *pieces):
        flat = lambda v: v.reshape(v.shape[0], -1, WIDE)
        self.mine = flat(pieces[0])
        self.came = [flat(grid.over_c(v)) for v in pieces[1:]]
        self.rows = self.mine.shape[1]

    def other(self, i, half, *rest):
        array, at = place_in(len(self.came), half, i)
        return self.came[array], lambda meta, ref: ref.at[(at, *[f(meta) for f in rest])]

    def part(self, i, half):
        return (self.mine, lambda meta, ref: ref.at[4 * half + i]), self.other(i, half)

    def at_plane(self, half, plane, count):
        rows = self.rows // 4

        def inside(first):
            return lambda meta, ref: ref.at[pl.ds(pl.multiple_of(first + plane(meta) * rows, 16), count)]

        def at(meta):
            return pl.ds(pl.multiple_of(plane(meta) * rows, 16), count)

        def own(meta, ref):
            return ref.at[4 * half, at(meta)]

        cells = [self.straight[half], self.last[half]]
        return [(self.mine, own), self.other(0, half, at)] + [(v, inside(first)) for v, first in cells]

    def counts(self):
        return DEEP // 2, self.rows // 4


def cell(v, first, rows):
    return v, lambda meta, ref: ref.at[pl.ds(first, rows)]


def step(grid, meta, after, seconds, firsts):
    tasks = Tasks(2)
    ends = []
    for r in seconds:
        for half in (0, 1):
            terms = r.part(1 + half, half) + (cell(*r.diagonal[half], r.rows),)
            ends.append((r, half, "last", 1 - half, tasks.add(1 - half, r.rows, *terms)))
    for r in firsts:
        for half in (0, 1):
            rows = r.rows
            ends.append((r, half, "diagonal", half, tasks.add(half, rows, *r.part(3, half))))
            ends.append((r, half, "straight", half, tasks.add(half, rows, *r.part(2 - half, half))))
    sent = tasks.run(meta, after)
    came = [grid.over_y(sent[0]), grid.over_x(sent[1])]
    for r, half, name, way, first in ends:
        if not hasattr(r, name):
            setattr(r, name, [None, None])
        getattr(r, name)[half] = (came[way], first)
    return sent, came


class Planes:
    def __init__(self, grid, meta, *reductions, at_once=False, after=()):
        self.grid, self.meta = grid, meta
        self.depth = sum(sum(r.counts()) for r in reductions)
        z = lambda meta: meta[4]
        if at_once:
            planes = [[lambda meta, k=k: z(meta) ^ k] for k in range(4)]
        else:
            planes = [[lambda meta, k=k, q=q: (z(meta) // 2 ^ k) * 2 + q for q in range(2)] for k in range(2)]
        tasks = Tasks(len(planes))
        tasks.kinds[0] = F32
        for out, group in enumerate(planes):
            for plane in group:
                for r in reductions:
                    for half in (0, 1):
                        tasks.add(out, r.counts()[half], *r.at_plane(half, plane, r.counts()[half]))
        self.kept, *sent = tasks.run(meta, after)
        self.sent = sent
        self.came = [grid.over_z(v, k) for v, k in zip(sent, (1, 2, 3) if at_once else (2,))]

    def second(self, *after):
        rows = self.depth
        tasks = Tasks(2)
        tasks.kinds[0] = F32
        for out in (0, 1):
            view = lambda meta, ref, out=out: ref.at[
                pl.ds(pl.multiple_of((meta[4] % 2 ^ out) * rows, 16), rows)
            ]
            tasks.add(out, rows, (self.kept, view), (self.came[0], view))
        self.kept, sent = tasks.run(self.meta, after)
        self.came = [self.grid.over_z(sent, 1)]

    def sums(self, layout, *after):
        return own_and_other(self.grid, self.meta, layout, tie(self.kept, *after), *self.came)


def own_and_other(grid, meta, layout, kept, *came):
    leave = sum(chunks * rows // 2 for _, chunks, rows in layout)
    count = len(came)

    def body(meta, kept, *refs):
        came, total, out = refs[:count], refs[count], refs[count + 1]
        total[...] = sum((v[...].astype(F32) for v in came), kept[...].astype(F32))
        at = 0
        for first, chunks, rows in layout:
            half = rows // 2
            for q in range(chunks):
                start = first + rows * q + half * (1 - meta[2])
                out[at : at + half] = total[pl.ds(pl.multiple_of(start, 8), half)]
                at += half

    total, out = call(
        body,
        [meta, kept, *came],
        [shape(kept.shape, F32), shape((leave, WIDE), F32)],
        [SMEM] + [VMEM] * (1 + count),
        [VMEM] * 2,
        [],
        0,
        5_000_000,
        limit=16,
    )
    return total, grid.over_c(out)


def tie(v, *after):
    return lax.optimization_barrier((v, *after))[0] if after else v


def seq_swaps(pieces_of, cuts):
    me, count = lax.axis_index("seq"), lax.axis_size("seq")
    kept = [pieces_of(me)]
    for r in range(1, count):
        kept.append(lax.ppermute(pieces_of(me ^ r), "seq", [(s, s ^ r) for s in range(count)]))
    order = jnp.stack([me ^ r for r in range(count)]).astype(jnp.int32)
    return lambda *after: place([tie(kept[0], *after), *kept[1:]], order, cuts)


def swap_all(grid, v, cuts):
    y, c = grid.y, grid.c
    pairs = v.reshape(2, 2, *v.shape[1:])
    stay = index_of(pairs, y)
    came = grid.over_y(index_of(pairs, 1 - y))
    other = grid.over_c(jnp.stack([index_of(stay, 1 - c), index_of(came, 1 - c)]))
    order = jnp.stack([y * 2 + c, (1 - y) * 2 + c, y * 2 + 1 - c, (1 - y) * 2 + 1 - c]).astype(jnp.int32)
    own = index_of(stay, c)
    return lambda *after: place(
        [tie(own, *after), index_of(came, c), other[0], other[1]], order, cuts
    )


def to_blocks(*arrays):
    quarter, width = arrays[0].shape[1:]
    cuts = [(quarter * k, quarter) for k in range(len(arrays))]
    end = seq_swaps(lambda s: jnp.concatenate([index_of(v, s) for v in arrays]), cuts)
    return lambda *after: [v.reshape(-1, width) for v in end(*after)]


def from_block(v, quarter):
    parts = v.reshape(-1, quarter, v.shape[-1])
    end = seq_swaps(lambda s: index_of(parts, s), [(0, quarter)])
    return lambda *after: end(*after)[0]


def both_halves(matrix):
    rows, wide = matrix.shape
    return matrix.reshape(rows, 2, wide // 2 // WIDE, WIDE).transpose(1, 2, 0, 3)


def lower_gains(ln1_gain, ln2_gain):
    return jnp.stack([ln1_gain, ln2_gain]).astype(BF)


def own_chunks(masters, core):
    views = []
    for l in range(masters[0].shape[0]):
        for ref, chunks in zip(masters, (3, 1, 4, 1)):
            for q in range(chunks):
                start = core * (ref.shape[2] // 2) + WIDE * q
                views.append(ref[l, :, pl.ds(pl.multiple_of(start, 128), WIDE)])
    return views


def chip_blocks(grid, meta, ln1_gain, ln2_gain, masters):
    layers, rows = masters[0].shape[:2]
    total = layers * 4 * 4 * rows * 3 // 4

    def leave(meta, one, two, *refs):
        ins, out = refs[:4], refs[4]
        start = 0
        for v in own_chunks(ins, 1 - meta[2]):
            out[start : start + v.shape[0]] = v
            start += v.shape[0]
        out[start : start + 8] = jnp.zeros((8, WIDE), F32)
        out[start : start + layers, :rows] = one[...]
        out[start + layers : start + 2 * layers, :rows] = two[...]

    size = sum(v.size for v in masters) * 8
    sent = call(
        leave,
        [meta, ln1_gain, ln2_gain, *masters],
        shape((total + 8, WIDE), F32),
        [SMEM] + [VMEM] * 6,
        VMEM,
        [],
        0,
        size,
        limit=16,
    )
    came = grid.over_c(sent)

    def merge(meta, sent, came, *refs):
        ins, outs, stage = refs[:4], refs[4:-1], refs[-1]
        core = meta[2]
        start = 0
        for v in own_chunks(ins, core):
            depth = v.shape[0]
            stage[pl.ds(pl.multiple_of(2 * start + core * depth, 8), depth)] = v
            stage[pl.ds(pl.multiple_of(2 * start + (1 - core) * depth, 8), depth)] = came[start : start + depth]
            start += depth
        stage[pl.ds(pl.multiple_of(2 * start + core * 8, 8), 8)] = sent[start : start + 8]
        stage[pl.ds(pl.multiple_of(2 * start + (1 - core) * 8, 8), 8)] = came[start : start + 8]
        first = 0
        for j, out in enumerate(outs):
            depth = DEEP * (1 + j % 2)
            out[:depth] = stage[first : first + depth].astype(BF)
            first += depth
        outs[0][DEEP:] = stage[first:].astype(BF)

    outs = [
        shape((DEEP * (1 + j % 2) + (GAIN_ROWS if j == 0 else 0), WIDE), BF) for j in range(2 * layers)
    ]
    return call(
        merge,
        [meta, sent, came, *masters],
        outs,
        [SMEM] + [VMEM] * 6,
        [VMEM] * len(outs),
        [pltpu.VMEM((2 * total + GAIN_ROWS, WIDE), F32)],
        0,
        size,
        limit=20,
    )


def finish(meta, sums, rows, width):
    layers = len(sums)

    def body(meta, *refs):
        count = 4 * layers
        ins, (one, two, *outs) = refs[:count], refs[count:]
        core = meta[2]
        for l in range(layers):
            feed, came, attn, came_attn = ins[4 * l : 4 * l + 4]

            def put(out, q, total, first, depth, came, at):
                half = out.shape[2] // 2
                columns = lambda c: pl.ds(pl.multiple_of(c * half + WIDE * q, 128), WIDE)
                out[l, :, columns(core)] = total[pl.ds(pl.multiple_of(first + core * depth, 8), depth)]
                out[l, :, columns(1 - core)] = came[at : at + depth]

            put(outs[3], 0, feed, DEEP, 4 * rows, came, 4 * rows)
            for q in range(4):
                put(outs[2], q, feed, 2 * rows * q, rows, came, q * rows)
            for q in range(3):
                put(outs[0], q, attn, 2 * rows * q, rows, came_attn, q * rows)
            put(outs[1], 0, attn, 6 * rows, rows, came_attn, 3 * rows)
            for g, out in enumerate((one, two)):
                both = attn[DEEP + g : DEEP + g + 1, : 2 * rows]
                out[l : l + 1] = jnp.where(core == 0, both[:, :rows], both[:, rows:])

    gain = shape((layers, rows), F32)
    outs = [gain, gain] + [
        shape((layers, r, w), F32)
        for r, w in ((rows, 3 * width), (rows, width), (rows, 4 * width), (4 * rows, width))
    ]
    flat = [v for l in range(layers) for v in sums[l]]
    one, two, qkv, out, up, down = call(
        body,
        [meta, *flat],
        outs,
        [SMEM] + [VMEM] * len(flat),
        [VMEM] * len(outs),
        [],
        0,
        8 * sum(v.size for v in flat),
        limit=20,
    )
    return one, qkv, out, two, up, down


def whole_gains(grid, gathering, layers, rows):
    g = gathering
    diagonal = g.both[1][:, -GAIN_ROWS:]
    tails = jnp.stack([v[:, -GAIN_ROWS:, :rows] for v in (g.own, g.by_x, g.by_y, diagonal)])
    tails = tails.reshape(2, 2, 4, 2, 8, rows)[:, :, :, :, : 2 * layers]
    tails = jnp.where(grid.y == 0, tails, tails[::-1])
    tails = jnp.where(grid.x == 0, tails, tails[:, ::-1])
    return tails.transpose(4, 2, 1, 0, 3, 5).reshape(2, layers, -1)


def pieces_of_whole(matrices):
    parts = []
    for whole in matrices:
        rows, wide = whole.shape
        parts.append(
            whole.reshape(4, 4, rows // 16, 2, wide // 2 // WIDE, WIDE).transpose(3, 1, 0, 4, 2, 5)
            .reshape(2, 4, 4, -1, WIDE)
        )
    stacked = jnp.concatenate(parts, 3)
    order = [(i & 1) * 2 + (i >> 1) for i in range(4)]
    return [stacked[side, order[i]] for side in range(2) for i in range(4)]


def whole_of_pieces(*pieces, widths):
    cut = DEEP // 2
    sides = []
    for arrays in (pieces[:1], pieces[1:]):
        places = [[place_in(len(arrays), half, i) for i in range(4)] for half in (0, 1)]
        sides.append([jnp.stack([arrays[array][at] for array, at in row]) for row in places])
    both = [jnp.concatenate([a[:, :, :cut], b[:, :, :cut]], 2) for a, b in sides]
    stacked = jnp.stack(both)
    stacked = jnp.stack([stacked[:, i] for i in (0, 2, 1, 3)], 1)
    outs, start = [], 0
    for rows, wide in widths:
        depth, chunks = rows // 16, wide // 2 // WIDE
        part = stacked[:, :, :, start : start + depth * chunks]
        start += depth * chunks
        outs.append(
            part.reshape(2, 4, 4, chunks, depth, WIDE).transpose(2, 1, 4, 0, 3, 5).reshape(rows, wide)
        )
    return outs


def per_device(
    states,
    item_halves,
    ln1_gain,
    qkv_weight,
    out_weight,
    ln2_gain,
    up_weight,
    down_weight,
    cotangent,
):
    masters = (qkv_weight, out_weight, up_weight, down_weight)
    layers, gain_shard = ln1_gain.shape
    quarter, width = states.shape[1:]
    near = lax.axis_size("dp") == 8 and lax.axis_size("seq") == 4 and layers == 2
    gains = lower_gains(ln1_gain, ln2_gain)
    flag = index_of(item_halves, lax.axis_index("seq"))
    if near:
        return by_permutes(states, flag, ln1_gain, ln2_gain, masters, cotangent, quarter)
    zero = jnp.zeros((), jnp.int32)
    meta = jnp.stack([zero, zero, zero, flag]).astype(jnp.int32)
    x, grad = to_blocks(states, cotangent)()
    gains = lax.all_gather(gains, LINES, axis=2, tiled=True).astype(F32)
    kept = []
    for l in range(layers):
        qkv, out, up, down = (
            lax.all_gather(v[l].astype(BF), LINES, axis=0, tiled=True) for v in masters
        )
        attn, feed = pieces_of_whole([qkv, out]), pieces_of_whole([up, down])
        qkv, o, m = attend_forward(meta, x, gains[0, l][None], attn)
        u, a, y = feed_forward(meta, m, gains[1, l][None], feed)
        kept.append((x, qkv, o, m, u, a, attn, feed))
        x = y
    outputs = x
    results = [None] * layers
    for l in reversed(range(layers)):
        x, qkv, o, m, u, a, attn, feed = kept[l]
        down_pieces = down_backward(meta, grad, a)
        dm, gg_two, *up_pieces = feed_backward(meta, grad, m, u, gains[1, l][None], feed)
        grad, *attn_pieces = attend_backward(meta, dm, x, qkv, o, gains[0, l][None], gg_two, attn)
        wholes = (
            whole_of_pieces(*attn_pieces, widths=((width, 3 * width), (width, width)))
            + whole_of_pieces(*up_pieces, widths=((width, 4 * width),))
            + whole_of_pieces(*down_pieces, widths=((4 * width, width),))
        )
        gain_sums = attn_pieces[0][:4, :, DEEP // 2 :, : width // 16]
        gain_sums = jnp.stack([gain_sums[i] for i in (0, 2, 1, 3)]).transpose(2, 1, 0, 3).reshape(GAIN_ROWS, width)
        sums = [
            lax.psum_scatter(v.astype(F32), LINES, scatter_dimension=0, tiled=True) for v in wholes
        ]
        gain_sums = lax.psum(gain_sums[:2].astype(F32), LINES)
        owner = lax.axis_index(LINES) * gain_shard
        results[l] = (lax.dynamic_slice_in_dim(gain_sums, owner, gain_shard, 1), *sums)
    return collect(from_block(outputs, quarter)(), from_block(grad, quarter)(), results)


def collect(outputs, grad_states, results):
    gains, qkv, out, up, down = (jnp.stack([r[k] for r in results]) for k in range(5))
    return outputs, grad_states, gains[:, 0], qkv, out, gains[:, 1], up, down


def by_permutes(states, flag, ln1_gain, ln2_gain, masters, cotangent, quarter):
    grid = Grid()
    meta = jnp.stack([grid.x, grid.y, grid.c, flag, grid.z]).astype(jnp.int32)
    layers, rows = masters[0].shape[:2]
    width = states.shape[2]
    blocks = chip_blocks(grid, meta, ln1_gain, ln2_gain, masters)
    come = swap_all(
        grid,
        jnp.concatenate([tie(states, blocks[0]), cotangent], 1),
        [(0, quarter), (quarter, quarter)],
    )
    feed1 = lax.all_gather(blocks[3], LINES, axis=0, tiled=True)
    feed1 = [feed1.reshape(4, 4, 2, 2 * DEEP, WIDE)]
    own = grid.planes(blocks[0])
    attn0 = Gathering(grid, own, DEEP // 2)
    attn0.first()
    own = grid.planes(blocks[1], (own,), (attn0.by_x, attn0.by_y))
    attn0.second()
    x, grad = (v.reshape(-1, width) for v in come(*attn0.both))
    feed0 = Gathering(grid, own, DEEP)
    feed0.first(*attn0.both)
    gains = whole_gains(grid, attn0, layers, rows).astype(F32)
    attn0 = attn0.pieces()
    qkv0, o0, m0 = attend_forward(meta, x, gains[0, 0][None], attn0)
    own = grid.planes(blocks[2], (own,), (m0,))
    feed0.second(m0, own)
    attn1 = Gathering(grid, own, DEEP // 2)
    attn1.first(feed0.by_x, feed0.by_y)
    attn1.second()
    feed0 = feed0.pieces()
    u0, a0, x1 = feed_forward(meta, tie(m0, attn1.by_x, attn1.by_y), gains[1, 0][None], feed0)
    attn1 = attn1.pieces(x1)
    qkv1, o1, m1 = attend_forward(meta, x1, gains[0, 1][None], attn1)
    y, dm, gg_two, whole = feed_both(meta, m1, grad, gains[1, 1][None], feed1)
    whole = lax.psum_scatter(whole.reshape(-1, WIDE), LINES, scatter_dimension=0, tiled=True)
    grad, *pieces = attend_backward(meta, dm, x1, qkv1, o1, gains[0, 1][None], gg_two, attn1)
    attn1 = Reduction(grid, *pieces)
    down_pieces = down_backward(meta, grad, a0)
    down0 = Reduction(grid, *down_pieces)
    ready, came1 = step(grid, meta, (down_pieces[0],), (), (attn1,))
    dm, gg_two, *pieces = feed_backward(
        meta, tie(grad, down_pieces[0], *ready), m0, u0, gains[1, 0][None], feed0
    )
    up0 = Reduction(grid, *pieces)
    ready, came2 = step(grid, meta, (dm, *down0.came, *came1), (attn1,), (down0,))
    dm = tie(dm, *ready)
    grad, *pieces = attend_backward(meta, dm, x, qkv0, o0, gains[0, 0][None], gg_two, attn0)
    attn0 = Reduction(grid, *pieces)
    sent, came3 = step(grid, meta, (grad, *attn0.came[:2], up0.came[0], *came2), (down0,), (up0, attn0))
    planes_attn1 = Planes(grid, meta, attn1, at_once=True, after=sent)
    sent, came4 = step(grid, meta, (*planes_attn1.came, *came3), (up0, attn0), ())
    feed = ((0, 4, 2 * rows), (DEEP, 1, DEEP))
    attend = ((0, 4, 2 * rows),)
    both = (*feed, (2 * DEEP, 4, 2 * rows))
    sums_attn1 = planes_attn1.sums(attend, *sent)
    planes0 = Planes(grid, meta, up0, down0, attn0, at_once=True)
    results = jnp.concatenate([v.reshape(4, quarter, width) for v in (tie(y, *planes0.sent), grad)], 1)
    results = swap_all(grid, results, [(0, quarter), (quarter, quarter)])
    outputs, grad_states = results(*planes0.came)
    sums1 = own_and_other(grid, meta, feed, tie(whole, *planes0.sent))
    total, came = planes0.sums(both)
    cut = 2 * DEEP
    sums0 = (total[:cut], came[: cut // 2], total[cut:], came[cut // 2 :])
    return outputs, grad_states, *finish(meta, (sums0, (*sums1, *sums_attn1)), rows, width)


def solution(mesh):
    rows = P(None, LINES, None)
    tokens = P("dp", "seq", None)
    gain = P(None, LINES)
    return jax.shard_map(
        per_device,
        mesh=mesh,
        in_specs=(tokens, P("dp"), gain, rows, rows, gain, rows, rows, tokens),
        out_specs=(tokens, tokens, gain, rows, rows, gain, rows, rows),
        check_vma=False,
    )
```

```python
import jax
import jax.numpy as jnp
from jax import lax
from jax.experimental import pallas as pl
from jax.experimental.pallas import tpu as pltpu
from jax.sharding import PartitionSpec as P

HEAD_DIM = 64
EPSILON = 1e-05
BF = jnp.bfloat16
F32 = jnp.float32
LINES = ("dp", "seq")
WIDE = 384
DEEP = 192
GAIN_ROWS = 16
VMEM = pl.BlockSpec(memory_space=pltpu.VMEM)
SMEM = pl.BlockSpec(memory_space=pltpu.SMEM)
HBM = pl.BlockSpec(memory_space=pl.ANY)


def call(body, ins, outs, specs, out_specs, scratch, flops, size, limit=58):
    return pl.pallas_call(
        body,
        out_shape=outs,
        in_specs=specs,
        out_specs=out_specs,
        scratch_shapes=scratch,
        cost_estimate=pl.CostEstimate(
            flops=flops, bytes_accessed=6 * size, transcendentals=0
        ),
        compiler_params=pltpu.CompilerParams(vmem_limit_bytes=limit * 1024 * 1024),
    )(*ins)


def shape(dims, dtype):
    return jax.ShapeDtypeStruct(dims, dtype)


def mat(a, b):
    return jnp.dot(a, b, preferred_element_type=F32)


def mat_t(a, b):
    return lax.dot_general(a, b, (((1,), (1,)), ((), ())), preferred_element_type=F32)


def t_mat(a, b):
    return lax.dot_general(a, b, (((0,), (0,)), ((), ())), preferred_element_type=F32)


def normed(v):
    average = jnp.mean(v, -1, keepdims=True)
    centered = v - average
    variance = jnp.mean(centered * centered, -1, keepdims=True)
    root = lax.rsqrt(variance + EPSILON)
    return centered * root, root


def norm_back(n, root, g):
    return root * (
        g - jnp.mean(g, -1, keepdims=True) - n * jnp.mean(g * n, -1, keepdims=True)
    )


def bell(u):
    return 0.5 * (1.0 + lax.erf(u * 0.7071067811865476))


def place(pieces, where_to, cuts):
    count = len(pieces)

    def body(to, *refs):
        for k in range(count):
            for (start, rows), out in zip(cuts, refs[count:]):
                out[to[k]] = refs[k][start : start + rows]

    one = pieces[0]
    return call(
        body,
        [where_to, *pieces],
        [shape((count, rows, one.shape[1]), one.dtype) for _, rows in cuts],
        [SMEM] + [VMEM] * count,
        [VMEM] * len(cuts),
        [],
        0,
        2 * count * one.size * one.dtype.itemsize,
        limit=16,
    )


def combine(meta, arrays, outs, tasks, after=()):
    count = len(arrays)
    terms = [(rows, term) for _, _, rows, sources in tasks for term in sources]

    def body(meta, *refs):
        ins, results, held = refs[:count], refs[count : count + len(outs)], refs[count + len(outs) : -1]
        sems = refs[-1]
        copies = [
            pltpu.make_async_copy(view(meta, ins[place_of]), held[k], sems.at[k])
            for k, (_, (place_of, view)) in enumerate(terms)
        ]
        start_all(copies)
        k = 0
        for result, first, rows, sources in tasks:
            wait_all(copies[k : k + len(sources)])
            step = 64 if rows % 64 == 0 else 16

            def some(r, _, k=k, result=result, first=first, step=step, sources=sources):
                at = pl.multiple_of(r * step, 16)
                total = sum(held[k + j][pl.ds(at, step)].astype(F32) for j in range(len(sources)))
                to = pl.multiple_of(first + at, 16)
                results[result][pl.ds(to, step)] = total.astype(results[result].dtype)
                return 0

            lax.fori_loop(0, rows // step, some, 0)
            k += len(sources)

    arrays = [tie(arrays[0], *after), *arrays[1:]]
    return call(
        body,
        [meta, *arrays],
        [shape((rows, WIDE), kind) for rows, kind in outs],
        [SMEM] + [HBM] * count,
        [VMEM] * len(outs),
        [pltpu.VMEM((rows, WIDE), arrays[term[0]].dtype) for rows, term in terms]
        + [pltpu.SemaphoreType.DMA((len(terms),))],
        0,
        60_000_000,
    )


class Tasks:
    def __init__(self, outs):
        self.arrays, self.tasks, self.rows, self.kinds = [], [], [0] * outs, [BF] * outs

    def add(self, out, rows, *terms):
        sources = []
        for array, view in terms:
            known = [k for k, v in enumerate(self.arrays) if v is array]
            if not known:
                self.arrays.append(array)
            sources.append((known[0] if known else len(self.arrays) - 1, view))
        first = self.rows[out]
        self.tasks.append((out, first, rows, sources))
        self.rows[out] += rows
        return first

    def run(self, meta, after=()):
        return combine(meta, self.arrays, list(zip(self.rows, self.kinds)), self.tasks, after)


def chip_row(meta, i):
    return (meta[0] ^ (i & 1)) * 2 + (meta[1] ^ (i >> 1))


def columns(meta, side, half, q):
    start = (meta[2] ^ side) * half + WIDE * q
    return pl.ds(pl.multiple_of(start, 128), WIDE)


def place_in(count, half, i):
    if count == 1:
        return 0, 4 * half + i
    if count == 2:
        return (0, 2 * half + (0 if i == 3 else 1)) if i in (3, 2 - half) else (1, 2 * half + (1 if i == 0 else 0))
    if i == 3 or i == 2 - half:
        return half, 0 if i == 3 else 1
    return 2, 2 * half + (1 if i == 0 else 0)


def piece_at(pieces, i, start, rows):
    if len(pieces) < 4:
        half = start // (DEEP // 2)
        array, at = place_in(len(pieces), half, i)
        return pieces[array].at[at, :, pl.ds(start - half * (DEEP // 2), rows), :]
    if i == 3 and len(pieces) == 5:
        cut = pieces[3].shape[1]
        if start >= cut:
            return pieces[4].at[:, pl.ds(start - cut, rows), :]
    return pieces[i].at[:, pl.ds(start, rows), :]


def chunked(meta, sides, target, sems, first, chunks, to_pieces=False, split=1):
    half = target.shape[-1] // 2
    rows = target.shape[2]
    step = rows // split
    whole = not isinstance(sides, (list, tuple))
    copies = []
    for side in range(2):
        for i in range(4):
            for q in range(chunks):
                for k in range(split):
                    start = first + rows * q + step * k
                    if whole:
                        a = sides.at[:, i, side, pl.ds(start, step), :]
                        place_of, lanes = i, pl.ds(side * half + WIDE * q, WIDE)
                    else:
                        a = piece_at(sides[side], i, start, step)
                        place_of, lanes = chip_row(meta, i), columns(meta, side, half, q)
                    b = target.at[:, place_of, pl.ds(step * k, step), lanes]
                    pair = (b, a) if to_pieces else (a, b)
                    copies.append(pltpu.make_async_copy(*pair, sems.at[len(copies)]))
    return copies


def pieces_of_refs(refs):
    count = len(refs)
    return refs[0] if count == 1 else (refs[: count // 2], refs[count // 2 :])


def start_all(copies):
    for copy in copies:
        copy.start()


def wait_all(copies):
    for copy in copies:
        copy.wait()


def attention_bias(flag, length):
    row = lax.broadcasted_iota(jnp.int32, (length, length), 0) // (length // 2)
    column = lax.broadcasted_iota(jnp.int32, (length, length), 1) // (length // 2)
    return jnp.where(jnp.logical_or(row == column, flag == 0), 0.0, -1e30)


def probabilities(queries, keys, bias):
    s = mat_t(queries, keys) * HEAD_DIM ** (-0.5) + bias
    e = jnp.exp(s - jnp.max(s, -1, keepdims=True))
    return e * (1.0 / jnp.sum(e, -1, keepdims=True))


def head_lanes():
    return lax.broadcasted_iota(jnp.int32, (1, 2 * HEAD_DIM), 1) // HEAD_DIM


def only(lanes, j, v):
    return jnp.where(lanes == j, v, jnp.zeros_like(v))


def tile(ref, t, width):
    z, xy, rows, _ = ref.shape
    return ref[:, :, :, t * width : (t + 1) * width].reshape(z * xy * rows, width)


def attend_forward(meta, x, gain, pieces):
    count = len(pieces)
    length, width = x.shape
    pairs = width // (2 * HEAD_DIM)

    def body(meta, x_ref, gain_ref, *refs):
        src = pieces_of_refs(refs[:count])
        qkv_ref, o_ref, m_ref, wqkv, wo, sems_a, sems_b = refs[count:]
        load_a = chunked(meta, src, wqkv, sems_a, 0, 3)
        load_b = chunked(meta, src, wo, sems_b, width * 3 // 16, 1)
        start_all(load_a)
        start_all(load_b)
        bias = attention_bias(meta[3], length)
        n, _ = normed(x_ref[...])
        hidden = (n * gain_ref[...]).astype(BF)
        wait_all(load_a)
        for t in range(3):
            qkv_ref[:, t * width : (t + 1) * width] = mat(hidden, tile(wqkv, t, width)).astype(BF)
        lanes = head_lanes()

        def pair(p, _):
            take = lambda part: qkv_ref[
                :, pl.ds(pl.multiple_of(part * width + p * 2 * HEAD_DIM, 128), 2 * HEAD_DIM)
            ]
            q, k, v = take(0), take(1), take(2)
            outs = [
                mat(probabilities(only(lanes, j, q), k, bias).astype(BF), v) for j in range(2)
            ]
            o_ref[:, pl.ds(pl.multiple_of(p * 2 * HEAD_DIM, 128), 2 * HEAD_DIM)] = jnp.where(
                lanes == 0, outs[0], outs[1]
            ).astype(BF)
            return 0

        lax.fori_loop(0, pairs, pair, 0, unroll=True)
        wait_all(load_b)
        m_ref[...] = x_ref[...] + mat(o_ref[...], tile(wo, 0, width))

    return call(
        body,
        [meta, x, gain, *pieces],
        (shape((length, 3 * width), BF), shape((length, width), BF), shape((length, width), F32)),
        [SMEM, VMEM, VMEM] + [HBM] * count,
        (VMEM,) * 3,
        [
            pltpu.VMEM((4, 4, width // 16, 3 * width), BF),
            pltpu.VMEM((4, 4, width // 16, width), BF),
            pltpu.SemaphoreType.DMA((24,)),
            pltpu.SemaphoreType.DMA((8,)),
        ],
        2 * length * width * width * 4 + 4 * length * length * width * 2,
        36_000_000,
    )


def feed_forward(meta, m, gain, pieces):
    count = len(pieces)
    length, width = m.shape
    wide = 4 * width

    def body(meta, m_ref, gain_ref, *refs):
        src = pieces_of_refs(refs[:count])
        u_ref, a_ref, y_ref, wu, wd, sems_a, sems_b = refs[count:]
        load_a = chunked(meta, src, wu, sems_a, 0, 4)
        load_b = chunked(meta, src, wd, sems_b, width // 4, 1)
        start_all(load_a)
        start_all(load_b)
        n, _ = normed(m_ref[...])
        hidden = (n * gain_ref[...]).astype(BF)
        wait_all(load_a)
        wait_all(load_b)
        total = m_ref[...]
        for t in range(4):
            u = mat(hidden, tile(wu, t, width))
            u_ref[:, t * width : (t + 1) * width] = u
            a = (u * bell(u)).astype(BF)
            a_ref[:, t * width : (t + 1) * width] = a
            total = total + mat(a, wd[t].reshape(width, width))
        y_ref[...] = total

    return call(
        body,
        [meta, m, gain, *pieces],
        (shape((length, wide), F32), shape((length, wide), BF), shape((length, width), F32)),
        [SMEM, VMEM, VMEM] + [HBM] * count,
        (VMEM,) * 3,
        [
            pltpu.VMEM((4, 4, width // 16, wide), BF),
            pltpu.VMEM((4, 4, width // 4, width), BF),
            pltpu.SemaphoreType.DMA((32,)),
            pltpu.SemaphoreType.DMA((8,)),
        ],
        2 * length * width * wide * 2,
        26_000_000,
    )


def piece_shapes(rows, parts):
    part = lambda count: shape((count, 4, rows, WIDE), BF)
    others = {1: (part(8),), 2: (part(4), part(4)), 3: (part(2), part(2), part(4))}
    return (part(8),) + others[parts]


def whole_shape():
    return shape((4, 4, 2, 2 * DEEP, WIDE), BF)


def down_backward(meta, dy, a):
    length, width = dy.shape

    def body(meta, dy_ref, a_ref, *refs):
        *outs, stage, sems = refs
        low = dy_ref[...].astype(BF)
        for t in range(4):
            stage[t] = (
                t_mat(a_ref[:, t * width : (t + 1) * width], low)
                .astype(BF)
                .reshape(4, width // 4, width)
            )
        copies = chunked(meta, (outs[:1], outs[1:]), stage, sems, 0, 1, True, 2)
        start_all(copies)
        wait_all(copies)

    outs = piece_shapes(DEEP // 2, 2)
    return call(
        body,
        [meta, dy, a],
        outs,
        [SMEM, VMEM, VMEM],
        (HBM,) * 3,
        [pltpu.VMEM((4, 4, width // 4, width), BF), pltpu.SemaphoreType.DMA((16,))],
        8 * length * width * width,
        13_000_000,
    )


def feed_backward(meta, dy, m, u, gain, pieces):
    count = len(pieces)
    length, width = m.shape
    wide = 4 * width

    def body(meta, dy_ref, m_ref, u_ref, gain_ref, *refs):
        src = pieces_of_refs(refs[:count])
        dm_ref, gg_ref, *outs = refs[count:-5]
        wu, wd, stage, sems_a, sems_b = refs[-5:]
        outs = outs[:1], outs[1:]
        load_a = chunked(meta, src, wu, sems_a, 0, 4)
        load_b = chunked(meta, src, wd, sems_b, width // 4, 1)
        start_all(load_b)
        start_all(load_a)
        n, root = normed(m_ref[...])
        gain = gain_ref[...]
        hidden_t = (n * gain).astype(BF).T
        low = dy_ref[...].astype(BF)
        wait_all(load_b)
        wait_all(load_a)
        dh = jnp.zeros((length, width), F32)
        for t in range(4):
            da = mat_t(low, wd[t].reshape(width, width))
            u = u_ref[:, t * width : (t + 1) * width]
            slope = bell(u) + u * (jnp.exp(-0.5 * u * u) * 0.3989422804014327)
            du = (da * slope).astype(BF)
            stage[:, :, :, t * width : (t + 1) * width] = (
                mat(hidden_t, du).astype(BF).reshape(4, 4, width // 16, width)
            )
            dh = dh + mat_t(du, tile(wu, t, width))
        store = chunked(meta, outs, stage, sems_a, 0, 4, True)
        start_all(store)
        gg_ref[...] = jnp.sum(dh * n, 0, keepdims=True)
        dm_ref[...] = dy_ref[...] + norm_back(n, root, dh * gain)
        wait_all(store)

    return call(
        body,
        [meta, dy, m, u, gain, *pieces],
        (shape((length, width), F32), shape((1, width), F32)) + piece_shapes(DEEP // 2, 2),
        [SMEM] + [VMEM] * 4 + [HBM] * count,
        (VMEM, VMEM) + (HBM,) * 3,
        [
            pltpu.VMEM((4, 4, width // 16, wide), BF),
            pltpu.VMEM((4, 4, width // 4, width), BF),
            pltpu.VMEM((4, 4, width // 16, wide), BF),
            pltpu.SemaphoreType.DMA((32,)),
            pltpu.SemaphoreType.DMA((8,)),
        ],
        2 * length * width * wide * 3,
        40_000_000,
    )


def feed_both(meta, m, dy, gain, pieces):
    length, width = m.shape
    wide = 4 * width
    count = len(pieces)

    def body(meta, m_ref, dy_ref, gain_ref, *refs):
        src = pieces_of_refs(refs[:count])
        y_ref, dm_ref, gg_ref, whole = refs[count : count + 4]
        wu, wd, a_ref, slope_ref, stage_u, stage_d, sems_a, sems_b, sems_c, sems_d = refs[count + 4 :]
        load_a = chunked(meta, src, wu, sems_a, 0, 4)
        load_b = chunked(meta, src, wd, sems_b, width // 4, 1)
        start_all(load_a)
        start_all(load_b)
        n, root = normed(m_ref[...])
        gain = gain_ref[...]
        hidden = (n * gain).astype(BF)
        hidden_t = (n * gain).astype(BF).T
        low = dy_ref[...].astype(BF)
        wait_all(load_a)
        for t in range(4):
            u = mat(hidden, tile(wu, t, width))
            share = bell(u)
            a = (u * share).astype(BF)
            a_ref[:, t * width : (t + 1) * width] = a
            slope_ref[:, t * width : (t + 1) * width] = share + u * (
                jnp.exp(-0.5 * u * u) * 0.3989422804014327
            )
            stage_d[t] = t_mat(a, low).astype(BF).reshape(4, width // 4, width)
        store_d = chunked(meta, whole, stage_d, sems_d, DEEP, 1, True)
        start_all(store_d)
        wait_all(load_b)
        dh = jnp.zeros((length, width), F32)
        for t in range(4):
            da = mat_t(low, wd[t].reshape(width, width))
            du = (da * slope_ref[:, t * width : (t + 1) * width]).astype(BF)
            stage_u[:, :, :, t * width : (t + 1) * width] = (
                mat(hidden_t, du).astype(BF).reshape(4, 4, width // 16, width)
            )
            dh = dh + mat_t(du, tile(wu, t, width))
        store_u = chunked(meta, whole, stage_u, sems_c, 0, 4, True)
        start_all(store_u)
        gg_ref[...] = jnp.sum(dh * n, 0, keepdims=True)
        dm_ref[...] = dy_ref[...] + norm_back(n, root, dh * gain)
        total = m_ref[...]
        for t in range(4):
            total = total + mat(a_ref[:, t * width : (t + 1) * width], wd[t].reshape(width, width))
        y_ref[...] = total
        wait_all(store_d)
        wait_all(store_u)

    return call(
        body,
        [meta, m, dy, gain, *pieces],
        (
            shape((length, width), F32),
            shape((length, width), F32),
            shape((1, width), F32),
            whole_shape(),
        ),
        [SMEM] + [VMEM] * 3 + [HBM] * count,
        (VMEM, VMEM, VMEM, HBM),
        [
            pltpu.VMEM((4, 4, width // 16, wide), BF),
            pltpu.VMEM((4, 4, width // 4, width), BF),
            pltpu.VMEM((length, wide), BF),
            pltpu.VMEM((length, wide), F32),
            pltpu.VMEM((4, 4, width // 16, wide), BF),
            pltpu.VMEM((4, 4, width // 4, width), BF),
            pltpu.SemaphoreType.DMA((32,)),
            pltpu.SemaphoreType.DMA((8,)),
            pltpu.SemaphoreType.DMA((32,)),
            pltpu.SemaphoreType.DMA((8,)),
        ],
        2 * length * width * wide * 6,
        60_000_000,
    )


def gain_place(pieces, half, i):
    array, at = place_in(len(pieces), half, i)
    return pieces[array].at[at, :, pl.ds(DEEP // 2, GAIN_ROWS), :]


def gain_rows(stage, one, two):
    width = one.shape[1]
    share = width // 16
    row = lax.broadcasted_iota(jnp.int32, (GAIN_ROWS, width), 0)
    both = jnp.where(row == 0, one, jnp.where(row == 1, two, 0.0))
    tall = jnp.broadcast_to(both[None], (16, GAIN_ROWS, width)).reshape(16 * GAIN_ROWS, width)
    chip = lax.broadcasted_iota(jnp.int32, tall.shape, 0) // GAIN_ROWS
    feature = lax.broadcasted_iota(jnp.int32, tall.shape, 1)
    tall = jnp.where(feature // share == chip, tall, 0.0).astype(BF)
    feature = lax.broadcasted_iota(jnp.int32, (width, 128), 0)
    lane = lax.broadcasted_iota(jnp.int32, (width, 128), 1)
    pick = jnp.where(feature % share == lane, 1.0, 0.0).astype(BF)
    stage[...] = jnp.zeros(stage.shape, BF)
    stage[:, :, :, :128] = mat(tall, pick).astype(BF).reshape(4, 4, GAIN_ROWS, 128)


def attend_backward(meta, dm, x, qkv, o, gain, gg_two, pieces):
    count = len(pieces)
    length, width = x.shape
    pairs = width // (2 * HEAD_DIM)
    scale = HEAD_DIM ** (-0.5)

    def body(meta, dm_ref, x_ref, qkv_ref, o_ref, gain_ref, gg_two_ref, *refs):
        src = pieces_of_refs(refs[:count])
        dx_ref = refs[count]
        outs = refs[count + 1 : count + 2], refs[count + 2 : count + 5]
        wqkv, wo, stage, stage_o, stage_g, do_ref, dqkv, sems_a, sems_b, sems_c = refs[count + 5 :]
        load_b = chunked(meta, src, wo, sems_b, width * 3 // 16, 1)
        load_a = chunked(meta, src, wqkv, sems_a, 0, 3)
        start_all(load_b)
        start_all(load_a)
        bias = attention_bias(meta[3], length)
        low = dm_ref[...].astype(BF)
        stage_o[...] = t_mat(o_ref[...], low).astype(BF).reshape(4, 4, width // 16, width)
        wait_all(load_b)
        do_ref[...] = mat_t(low, tile(wo, 0, width)).astype(BF)
        store_b = chunked(meta, outs, stage_o, sems_b, width * 3 // 16, 1, True)
        start_all(store_b)
        lanes = head_lanes()

        def pair(p, _):
            at = lambda part: pl.ds(
                pl.multiple_of(part * width + p * 2 * HEAD_DIM, 128), 2 * HEAD_DIM
            )
            q, k, v = qkv_ref[:, at(0)], qkv_ref[:, at(1)], qkv_ref[:, at(2)]
            d = do_ref[:, at(0)]
            dq, dk, dv = [], [], []
            for j in range(2):
                soft = probabilities(only(lanes, j, q), k, bias)
                dp = mat_t(only(lanes, j, d), v)
                ds = (soft * (dp - jnp.sum(dp * soft, -1, keepdims=True))).astype(BF)
                dv.append(t_mat(soft.astype(BF), d))
                dq.append(mat(ds, k) * scale)
                dk.append(t_mat(ds, q) * scale)
            for part, two in enumerate((dq, dk, dv)):
                dqkv[:, at(part)] = jnp.where(lanes == 0, two[0], two[1]).astype(BF)
            return 0

        lax.fori_loop(0, pairs, pair, 0, unroll=2)
        n, root = normed(x_ref[...])
        gain = gain_ref[...]
        hidden_t = (n * gain).astype(BF).T
        wait_all(load_a)
        dh = jnp.zeros((length, width), F32)
        for t in range(3):
            d = dqkv[:, t * width : (t + 1) * width]
            stage[:, :, :, t * width : (t + 1) * width] = (
                mat(hidden_t, d).astype(BF).reshape(4, 4, width // 16, width)
            )
            dh = dh + mat_t(d, tile(wqkv, t, width))
        store_a = chunked(meta, outs, stage, sems_a, 0, 3, True)
        start_all(store_a)
        gain_rows(stage_g, jnp.sum(dh * n, 0, keepdims=True), gg_two_ref[...])
        store_c = [
            pltpu.make_async_copy(
                stage_g.at[:, chip_row(meta, i)],
                gain_place(outs[side], half, i),
                sems_c.at[8 * half + 4 * side + i],
            )
            for half in range(2)
            for side in range(2)
            for i in range(4)
        ]
        start_all(store_c)
        dx_ref[...] = dm_ref[...] + norm_back(n, root, dh * gain)
        wait_all(store_a)
        wait_all(store_b)
        wait_all(store_c)

    return call(
        body,
        [meta, dm, x, qkv, o, gain, gg_two, *pieces],
        (shape((length, width), F32),) + piece_shapes(DEEP // 2 + GAIN_ROWS, 3),
        [SMEM] + [VMEM] * 6 + [HBM] * count,
        (VMEM,) + (HBM,) * 4,
        [
            pltpu.VMEM((4, 4, width // 16, 3 * width), BF),
            pltpu.VMEM((4, 4, width // 16, width), BF),
            pltpu.VMEM((4, 4, width // 16, 3 * width), BF),
            pltpu.VMEM((4, 4, width // 16, width), BF),
            pltpu.VMEM((4, 4, GAIN_ROWS, WIDE), BF),
            pltpu.VMEM((length, width), BF),
            pltpu.VMEM((length, 3 * width), BF),
            pltpu.SemaphoreType.DMA((24,)),
            pltpu.SemaphoreType.DMA((8,)),
            pltpu.SemaphoreType.DMA((16,)),
        ],
        2 * length * width * width * 8 + 2 * length * length * width * 10,
        52_000_000,
    )


def index_of(v, i):
    return lax.dynamic_index_in_dim(v, i, 0, keepdims=False)


class Grid:
    def __init__(self):
        dp, seq = lax.axis_index("dp"), lax.axis_index("seq")
        self.z, self.x, self.y, self.c = dp // 2, dp % 2, seq // 2, seq % 2
        places = [(z, x, y, c) for z in range(4) for x in range(2) for y in range(2) for c in range(2)]
        flat = lambda z, x, y, c: (z * 2 + x) * 4 + y * 2 + c
        to = lambda move: [(flat(*p), flat(*move(*p))) for p in places]
        self.perm_c = to(lambda z, x, y, c: (z, x, y, 1 - c))
        self.perm_x = to(lambda z, x, y, c: (z, 1 - x, y, c))
        self.perm_y = to(lambda z, x, y, c: (z, x, 1 - y, c))
        self.perm_z = [to(lambda z, x, y, c, k=k: (z ^ k, x, y, c)) for k in range(4)]

    def over_c(self, v):
        return lax.ppermute(v, LINES, self.perm_c)

    def over_x(self, v):
        return lax.ppermute(v, LINES, self.perm_x)

    def over_y(self, v):
        return lax.ppermute(v, LINES, self.perm_y)

    def over_z(self, v, k):
        return lax.ppermute(v, LINES, self.perm_z[k])

    def planes(self, block, before=(), after=()):
        block = tie(block, *before)
        parts = [tie(block, *after)] + [self.over_z(block, k) for k in (1, 2, 3)]
        order = jnp.stack([self.z ^ k for k in range(4)]).astype(jnp.int32)
        return place(parts, order, [(0, block.shape[0])])[0]


class Gathering:
    def __init__(self, grid, own, cut):
        self.grid, self.own, self.cut = grid, own, cut

    def first(self, *after):
        own = tie(self.own, *after)
        self.by_x, self.by_y = self.grid.over_x(own), self.grid.over_y(own)
        return [self.by_x, self.by_y]

    def second(self, *after):
        a, b = tie(self.by_x, *after), tie(self.by_y, *after)
        self.both = [self.grid.over_y(a[:, : self.cut]), self.grid.over_x(b[:, self.cut :])]
        return self.both

    def pieces(self, *after):
        here = [self.own, self.by_x, self.by_y, *(tie(v, *after) for v in self.both)]
        return here + [self.grid.over_c(v) for v in here]


class Reduction:
    def __init__(self, grid, *pieces):
        flat = lambda v: v.reshape(v.shape[0], -1, WIDE)
        self.mine = flat(pieces[0])
        self.came = [flat(grid.over_c(v)) for v in pieces[1:]]
        self.rows = self.mine.shape[1]

    def other(self, i, half, *rest):
        array, at = place_in(len(self.came), half, i)
        return self.came[array], lambda meta, ref: ref.at[(at, *[f(meta) for f in rest])]

    def part(self, i, half):
        return (self.mine, lambda meta, ref: ref.at[4 * half + i]), self.other(i, half)

    def at_plane(self, half, plane, count):
        rows = self.rows // 4

        def inside(first):
            return lambda meta, ref: ref.at[pl.ds(pl.multiple_of(first + plane(meta) * rows, 16), count)]

        def at(meta):
            return pl.ds(pl.multiple_of(plane(meta) * rows, 16), count)

        def own(meta, ref):
            return ref.at[4 * half, at(meta)]

        cells = [self.straight[half], self.last[half]]
        return [(self.mine, own), self.other(0, half, at)] + [(v, inside(first)) for v, first in cells]

    def counts(self):
        return DEEP // 2, self.rows // 4


def cell(v, first, rows):
    return v, lambda meta, ref: ref.at[pl.ds(first, rows)]


def step(grid, meta, after, seconds, firsts):
    tasks = Tasks(2)
    ends = []
    for r in seconds:
        for half in (0, 1):
            terms = r.part(1 + half, half) + (cell(*r.diagonal[half], r.rows),)
            ends.append((r, half, "last", 1 - half, tasks.add(1 - half, r.rows, *terms)))
    for r in firsts:
        for half in (0, 1):
            rows = r.rows
            ends.append((r, half, "diagonal", half, tasks.add(half, rows, *r.part(3, half))))
            ends.append((r, half, "straight", half, tasks.add(half, rows, *r.part(2 - half, half))))
    sent = tasks.run(meta, after)
    came = [grid.over_y(sent[0]), grid.over_x(sent[1])]
    for r, half, name, way, first in ends:
        if not hasattr(r, name):
            setattr(r, name, [None, None])
        getattr(r, name)[half] = (came[way], first)
    return sent, came


class Planes:
    def __init__(self, grid, meta, *reductions, at_once=False, after=()):
        self.grid, self.meta = grid, meta
        self.depth = sum(sum(r.counts()) for r in reductions)
        z = lambda meta: meta[4]
        if at_once:
            planes = [[lambda meta, k=k: z(meta) ^ k] for k in range(4)]
        else:
            planes = [[lambda meta, k=k, q=q: (z(meta) // 2 ^ k) * 2 + q for q in range(2)] for k in range(2)]
        tasks = Tasks(len(planes))
        tasks.kinds[0] = F32
        for out, group in enumerate(planes):
            for plane in group:
                for r in reductions:
                    for half in (0, 1):
                        tasks.add(out, r.counts()[half], *r.at_plane(half, plane, r.counts()[half]))
        self.kept, *sent = tasks.run(meta, after)
        self.sent = sent
        self.came = [grid.over_z(v, k) for v, k in zip(sent, (1, 2, 3) if at_once else (2,))]

    def second(self, *after):
        rows = self.depth
        tasks = Tasks(2)
        tasks.kinds[0] = F32
        for out in (0, 1):
            view = lambda meta, ref, out=out: ref.at[
                pl.ds(pl.multiple_of((meta[4] % 2 ^ out) * rows, 16), rows)
            ]
            tasks.add(out, rows, (self.kept, view), (self.came[0], view))
        self.kept, sent = tasks.run(self.meta, after)
        self.came = [self.grid.over_z(sent, 1)]

    def sums(self, layout, *after):
        return own_and_other(self.grid, self.meta, layout, tie(self.kept, *after), *self.came)


def own_and_other(grid, meta, layout, kept, *came):
    leave = sum(chunks * rows // 2 for _, chunks, rows in layout)
    count = len(came)

    def body(meta, kept, *refs):
        came, total, out = refs[:count], refs[count], refs[count + 1]
        total[...] = sum((v[...].astype(F32) for v in came), kept[...].astype(F32))
        at = 0
        for first, chunks, rows in layout:
            half = rows // 2
            for q in range(chunks):
                start = first + rows * q + half * (1 - meta[2])
                out[at : at + half] = total[pl.ds(pl.multiple_of(start, 8), half)]
                at += half

    total, out = call(
        body,
        [meta, kept, *came],
        [shape(kept.shape, F32), shape((leave, WIDE), F32)],
        [SMEM] + [VMEM] * (1 + count),
        [VMEM] * 2,
        [],
        0,
        5_000_000,
        limit=16,
    )
    return total, grid.over_c(out)


def tie(v, *after):
    return lax.optimization_barrier((v, *after))[0] if after else v


def seq_swaps(pieces_of, cuts):
    me, count = lax.axis_index("seq"), lax.axis_size("seq")
    kept = [pieces_of(me)]
    for r in range(1, count):
        kept.append(lax.ppermute(pieces_of(me ^ r), "seq", [(s, s ^ r) for s in range(count)]))
    order = jnp.stack([me ^ r for r in range(count)]).astype(jnp.int32)
    return lambda *after: place([tie(kept[0], *after), *kept[1:]], order, cuts)


def swap_all(grid, v, cuts):
    y, c = grid.y, grid.c
    pairs = v.reshape(2, 2, *v.shape[1:])
    stay = index_of(pairs, y)
    came = grid.over_y(index_of(pairs, 1 - y))
    other = grid.over_c(jnp.stack([index_of(stay, 1 - c), index_of(came, 1 - c)]))
    order = jnp.stack([y * 2 + c, (1 - y) * 2 + c, y * 2 + 1 - c, (1 - y) * 2 + 1 - c]).astype(jnp.int32)
    own = index_of(stay, c)
    return lambda *after: place(
        [tie(own, *after), index_of(came, c), other[0], other[1]], order, cuts
    )


def to_blocks(*arrays):
    quarter, width = arrays[0].shape[1:]
    cuts = [(quarter * k, quarter) for k in range(len(arrays))]
    end = seq_swaps(lambda s: jnp.concatenate([index_of(v, s) for v in arrays]), cuts)
    return lambda *after: [v.reshape(-1, width) for v in end(*after)]


def from_block(v, quarter):
    parts = v.reshape(-1, quarter, v.shape[-1])
    end = seq_swaps(lambda s: index_of(parts, s), [(0, quarter)])
    return lambda *after: end(*after)[0]


def both_halves(matrix):
    rows, wide = matrix.shape
    return matrix.reshape(rows, 2, wide // 2 // WIDE, WIDE).transpose(1, 2, 0, 3)


def lower_gains(ln1_gain, ln2_gain):
    return jnp.stack([ln1_gain, ln2_gain]).astype(BF)


def own_chunks(masters, core):
    views = []
    for l in range(masters[0].shape[0]):
        for ref, chunks in zip(masters, (3, 1, 4, 1)):
            for q in range(chunks):
                start = core * (ref.shape[2] // 2) + WIDE * q
                views.append(ref[l, :, pl.ds(pl.multiple_of(start, 128), WIDE)])
    return views


def chip_blocks(grid, meta, ln1_gain, ln2_gain, masters):
    layers, rows = masters[0].shape[:2]
    total = layers * 4 * 4 * rows * 3 // 4

    def leave(meta, one, two, *refs):
        ins, out = refs[:4], refs[4]
        start = 0
        for v in own_chunks(ins, 1 - meta[2]):
            out[start : start + v.shape[0]] = v
            start += v.shape[0]
        out[start : start + 8] = jnp.zeros((8, WIDE), F32)
        out[start : start + layers, :rows] = one[...]
        out[start + layers : start + 2 * layers, :rows] = two[...]

    size = sum(v.size for v in masters) * 8
    sent = call(
        leave,
        [meta, ln1_gain, ln2_gain, *masters],
        shape((total + 8, WIDE), F32),
        [SMEM] + [VMEM] * 6,
        VMEM,
        [],
        0,
        size,
        limit=16,
    )
    came = grid.over_c(sent)

    def merge(meta, sent, came, *refs):
        ins, outs, stage = refs[:4], refs[4:-1], refs[-1]
        core = meta[2]
        start = 0
        for v in own_chunks(ins, core):
            depth = v.shape[0]
            stage[pl.ds(pl.multiple_of(2 * start + core * depth, 8), depth)] = v
            stage[pl.ds(pl.multiple_of(2 * start + (1 - core) * depth, 8), depth)] = came[start : start + depth]
            start += depth
        stage[pl.ds(pl.multiple_of(2 * start + core * 8, 8), 8)] = sent[start : start + 8]
        stage[pl.ds(pl.multiple_of(2 * start + (1 - core) * 8, 8), 8)] = came[start : start + 8]
        first = 0
        for j, out in enumerate(outs):
            depth = DEEP * (1 + j % 2)
            out[:depth] = stage[first : first + depth].astype(BF)
            first += depth
        outs[0][DEEP:] = stage[first:].astype(BF)

    outs = [
        shape((DEEP * (1 + j % 2) + (GAIN_ROWS if j == 0 else 0), WIDE), BF) for j in range(2 * layers)
    ]
    return call(
        merge,
        [meta, sent, came, *masters],
        outs,
        [SMEM] + [VMEM] * 6,
        [VMEM] * len(outs),
        [pltpu.VMEM((2 * total + GAIN_ROWS, WIDE), F32)],
        0,
        size,
        limit=20,
    )


def finish(meta, sums, rows, width):
    layers = len(sums)

    def body(meta, *refs):
        count = 4 * layers
        ins, (one, two, *outs) = refs[:count], refs[count:]
        core = meta[2]
        for l in range(layers):
            feed, came, attn, came_attn = ins[4 * l : 4 * l + 4]

            def put(out, q, total, first, depth, came, at):
                half = out.shape[2] // 2
                columns = lambda c: pl.ds(pl.multiple_of(c * half + WIDE * q, 128), WIDE)
                out[l, :, columns(core)] = total[pl.ds(pl.multiple_of(first + core * depth, 8), depth)]
                out[l, :, columns(1 - core)] = came[at : at + depth]

            put(outs[3], 0, feed, DEEP, 4 * rows, came, 4 * rows)
            for q in range(4):
                put(outs[2], q, feed, 2 * rows * q, rows, came, q * rows)
            for q in range(3):
                put(outs[0], q, attn, 2 * rows * q, rows, came_attn, q * rows)
            put(outs[1], 0, attn, 6 * rows, rows, came_attn, 3 * rows)
            for g, out in enumerate((one, two)):
                both = attn[DEEP + g : DEEP + g + 1, : 2 * rows]
                out[l : l + 1] = jnp.where(core == 0, both[:, :rows], both[:, rows:])

    gain = shape((layers, rows), F32)
    outs = [gain, gain] + [
        shape((layers, r, w), F32)
        for r, w in ((rows, 3 * width), (rows, width), (rows, 4 * width), (4 * rows, width))
    ]
    flat = [v for l in range(layers) for v in sums[l]]
    one, two, qkv, out, up, down = call(
        body,
        [meta, *flat],
        outs,
        [SMEM] + [VMEM] * len(flat),
        [VMEM] * len(outs),
        [],
        0,
        8 * sum(v.size for v in flat),
        limit=20,
    )
    return one, qkv, out, two, up, down


def whole_gains(grid, gathering, layers, rows):
    g = gathering
    diagonal = g.both[1][:, -GAIN_ROWS:]
    tails = jnp.stack([v[:, -GAIN_ROWS:, :rows] for v in (g.own, g.by_x, g.by_y, diagonal)])
    tails = tails.reshape(2, 2, 4, 2, 8, rows)[:, :, :, :, : 2 * layers]
    tails = jnp.where(grid.y == 0, tails, tails[::-1])
    tails = jnp.where(grid.x == 0, tails, tails[:, ::-1])
    return tails.transpose(4, 2, 1, 0, 3, 5).reshape(2, layers, -1)


def pieces_of_whole(matrices):
    parts = []
    for whole in matrices:
        rows, wide = whole.shape
        parts.append(
            whole.reshape(4, 4, rows // 16, 2, wide // 2 // WIDE, WIDE).transpose(3, 1, 0, 4, 2, 5)
            .reshape(2, 4, 4, -1, WIDE)
        )
    stacked = jnp.concatenate(parts, 3)
    order = [(i & 1) * 2 + (i >> 1) for i in range(4)]
    return [stacked[side, order[i]] for side in range(2) for i in range(4)]


def whole_of_pieces(*pieces, widths):
    cut = DEEP // 2
    sides = []
    for arrays in (pieces[:1], pieces[1:]):
        places = [[place_in(len(arrays), half, i) for i in range(4)] for half in (0, 1)]
        sides.append([jnp.stack([arrays[array][at] for array, at in row]) for row in places])
    both = [jnp.concatenate([a[:, :, :cut], b[:, :, :cut]], 2) for a, b in sides]
    stacked = jnp.stack(both)
    stacked = jnp.stack([stacked[:, i] for i in (0, 2, 1, 3)], 1)
    outs, start = [], 0
    for rows, wide in widths:
        depth, chunks = rows // 16, wide // 2 // WIDE
        part = stacked[:, :, :, start : start + depth * chunks]
        start += depth * chunks
        outs.append(
            part.reshape(2, 4, 4, chunks, depth, WIDE).transpose(2, 1, 4, 0, 3, 5).reshape(rows, wide)
        )
    return outs


def per_device(
    states,
    item_halves,
    ln1_gain,
    qkv_weight,
    out_weight,
    ln2_gain,
    up_weight,
    down_weight,
    cotangent,
):
    masters = (qkv_weight, out_weight, up_weight, down_weight)
    layers, gain_shard = ln1_gain.shape
    quarter, width = states.shape[1:]
    near = lax.axis_size("dp") == 8 and lax.axis_size("seq") == 4 and layers == 2
    gains = lower_gains(ln1_gain, ln2_gain)
    flag = index_of(item_halves, lax.axis_index("seq"))
    if near:
        return by_permutes(states, flag, ln1_gain, ln2_gain, masters, cotangent, quarter)
    zero = jnp.zeros((), jnp.int32)
    meta = jnp.stack([zero, zero, zero, flag]).astype(jnp.int32)
    x, grad = to_blocks(states, cotangent)()
    gains = lax.all_gather(gains, LINES, axis=2, tiled=True).astype(F32)
    kept = []
    for l in range(layers):
        qkv, out, up, down = (
            lax.all_gather(v[l].astype(BF), LINES, axis=0, tiled=True) for v in masters
        )
        attn, feed = pieces_of_whole([qkv, out]), pieces_of_whole([up, down])
        qkv, o, m = attend_forward(meta, x, gains[0, l][None], attn)
        u, a, y = feed_forward(meta, m, gains[1, l][None], feed)
        kept.append((x, qkv, o, m, u, a, attn, feed))
        x = y
    outputs = x
    results = [None] * layers
    for l in reversed(range(layers)):
        x, qkv, o, m, u, a, attn, feed = kept[l]
        down_pieces = down_backward(meta, grad, a)
        dm, gg_two, *up_pieces = feed_backward(meta, grad, m, u, gains[1, l][None], feed)
        grad, *attn_pieces = attend_backward(meta, dm, x, qkv, o, gains[0, l][None], gg_two, attn)
        wholes = (
            whole_of_pieces(*attn_pieces, widths=((width, 3 * width), (width, width)))
            + whole_of_pieces(*up_pieces, widths=((width, 4 * width),))
            + whole_of_pieces(*down_pieces, widths=((4 * width, width),))
        )
        gain_sums = attn_pieces[0][:4, :, DEEP // 2 :, : width // 16]
        gain_sums = jnp.stack([gain_sums[i] for i in (0, 2, 1, 3)]).transpose(2, 1, 0, 3).reshape(GAIN_ROWS, width)
        sums = [
            lax.psum_scatter(v.astype(F32), LINES, scatter_dimension=0, tiled=True) for v in wholes
        ]
        gain_sums = lax.psum(gain_sums[:2].astype(F32), LINES)
        owner = lax.axis_index(LINES) * gain_shard
        results[l] = (lax.dynamic_slice_in_dim(gain_sums, owner, gain_shard, 1), *sums)
    return collect(from_block(outputs, quarter)(), from_block(grad, quarter)(), results)


def collect(outputs, grad_states, results):
    gains, qkv, out, up, down = (jnp.stack([r[k] for r in results]) for k in range(5))
    return outputs, grad_states, gains[:, 0], qkv, out, gains[:, 1], up, down


def by_permutes(states, flag, ln1_gain, ln2_gain, masters, cotangent, quarter):
    grid = Grid()
    meta = jnp.stack([grid.x, grid.y, grid.c, flag, grid.z]).astype(jnp.int32)
    layers, rows = masters[0].shape[:2]
    width = states.shape[2]
    blocks = chip_blocks(grid, meta, ln1_gain, ln2_gain, masters)
    come = swap_all(
        grid,
        jnp.concatenate([tie(states, blocks[0]), cotangent], 1),
        [(0, quarter), (quarter, quarter)],
    )
    feed1 = lax.all_gather(blocks[3], LINES, axis=0, tiled=True)
    feed1 = [feed1.reshape(4, 4, 2, 2 * DEEP, WIDE)]
    own = grid.planes(blocks[0])
    attn0 = Gathering(grid, own, DEEP // 2)
    attn0.first()
    own = grid.planes(blocks[1], (own,), (attn0.by_x, attn0.by_y))
    attn0.second()
    x, grad = (v.reshape(-1, width) for v in come(*attn0.both))
    feed0 = Gathering(grid, own, DEEP)
    feed0.first(*attn0.both)
    gains = whole_gains(grid, attn0, layers, rows).astype(F32)
    attn0 = attn0.pieces()
    qkv0, o0, m0 = attend_forward(meta, x, gains[0, 0][None], attn0)
    own = grid.planes(blocks[2], (own,), (m0,))
    feed0.second(m0, own)
    attn1 = Gathering(grid, own, DEEP // 2)
    attn1.first(feed0.by_x, feed0.by_y)
    attn1.second()
    feed0 = feed0.pieces()
    u0, a0, x1 = feed_forward(meta, tie(m0, attn1.by_x, attn1.by_y), gains[1, 0][None], feed0)
    attn1 = attn1.pieces(x1)
    qkv1, o1, m1 = attend_forward(meta, x1, gains[0, 1][None], attn1)
    y, dm, gg_two, whole = feed_both(meta, m1, grad, gains[1, 1][None], feed1)
    whole = lax.psum_scatter(whole.reshape(-1, WIDE), LINES, scatter_dimension=0, tiled=True)
    grad, *pieces = attend_backward(meta, dm, x1, qkv1, o1, gains[0, 1][None], gg_two, attn1)
    attn1 = Reduction(grid, *pieces)
    down_pieces = down_backward(meta, grad, a0)
    down0 = Reduction(grid, *down_pieces)
    ready, came1 = step(grid, meta, (down_pieces[0],), (), (attn1,))
    dm, gg_two, *pieces = feed_backward(
        meta, tie(grad, down_pieces[0], *ready), m0, u0, gains[1, 0][None], feed0
    )
    up0 = Reduction(grid, *pieces)
    ready, came2 = step(grid, meta, (dm, *down0.came, *came1), (attn1,), (down0,))
    dm = tie(dm, *ready)
    grad, *pieces = attend_backward(meta, dm, x, qkv0, o0, gains[0, 0][None], gg_two, attn0)
    attn0 = Reduction(grid, *pieces)
    sent, came3 = step(grid, meta, (grad, *attn0.came[:2], up0.came[0], *came2), (down0,), (up0, attn0))
    planes_attn1 = Planes(grid, meta, attn1, at_once=True, after=sent)
    sent, came4 = step(grid, meta, (*planes_attn1.came, *came3), (up0, attn0), ())
    feed = ((0, 4, 2 * rows), (DEEP, 1, DEEP))
    attend = ((0, 4, 2 * rows),)
    both = (feed[0], (DEEP, 4, 2 * rows))
    sums_attn1 = planes_attn1.sums(attend, *sent)
    planes_down0 = Planes(grid, meta, down0, at_once=True, after=sent)
    planes0 = Planes(grid, meta, up0, attn0, at_once=True, after=planes_down0.came)
    results = jnp.concatenate([v.reshape(4, quarter, width) for v in (tie(y, *planes0.sent), grad)], 1)
    results = swap_all(grid, results, [(0, quarter), (quarter, quarter)])
    outputs, grad_states = results(*planes0.came)
    sums1 = own_and_other(grid, meta, feed, tie(whole, *planes0.sent))
    total_down, came_down = planes_down0.sums(((0, 1, DEEP),), *planes0.sent)
    total, came = planes0.sums(both)
    cut = DEEP // 2
    sums0 = (
        jnp.concatenate([total[:DEEP], total_down]),
        jnp.concatenate([came[:cut], came_down]),
        total[DEEP:],
        came[cut:],
    )
    return outputs, grad_states, *finish(meta, (sums0, (*sums1, *sums_attn1)), rows, width)


def solution(mesh):
    rows = P(None, LINES, None)
    tokens = P("dp", "seq", None)
    gain = P(None, LINES)
    return jax.shard_map(
        per_device,
        mesh=mesh,
        in_specs=(tokens, P("dp"), gain, rows, rows, gain, rows, rows, tokens),
        out_specs=(tokens, tokens, gain, rows, rows, gain, rows, rows),
        check_vma=False,
    )
```

```python
import jax
import jax.numpy as jnp
from jax import lax
from jax.experimental import pallas as pl
from jax.experimental.pallas import tpu as pltpu
from jax.sharding import PartitionSpec as P

HEAD_DIM = 64
EPSILON = 1e-05
BF = jnp.bfloat16
F32 = jnp.float32
LINES = ("dp", "seq")
WIDE = 384
DEEP = 192
GAIN_ROWS = 16
VMEM = pl.BlockSpec(memory_space=pltpu.VMEM)
SMEM = pl.BlockSpec(memory_space=pltpu.SMEM)
HBM = pl.BlockSpec(memory_space=pl.ANY)


def call(body, ins, outs, specs, out_specs, scratch, flops, size, limit=58):
    return pl.pallas_call(
        body,
        out_shape=outs,
        in_specs=specs,
        out_specs=out_specs,
        scratch_shapes=scratch,
        cost_estimate=pl.CostEstimate(
            flops=flops, bytes_accessed=6 * size, transcendentals=0
        ),
        compiler_params=pltpu.CompilerParams(vmem_limit_bytes=limit * 1024 * 1024),
    )(*ins)


def shape(dims, dtype):
    return jax.ShapeDtypeStruct(dims, dtype)


def mat(a, b):
    return jnp.dot(a, b, preferred_element_type=F32)


def mat_t(a, b):
    return lax.dot_general(a, b, (((1,), (1,)), ((), ())), preferred_element_type=F32)


def t_mat(a, b):
    return lax.dot_general(a, b, (((0,), (0,)), ((), ())), preferred_element_type=F32)


def normed(v):
    average = jnp.mean(v, -1, keepdims=True)
    centered = v - average
    variance = jnp.mean(centered * centered, -1, keepdims=True)
    root = lax.rsqrt(variance + EPSILON)
    return centered * root, root


def norm_back(n, root, g):
    return root * (
        g - jnp.mean(g, -1, keepdims=True) - n * jnp.mean(g * n, -1, keepdims=True)
    )


def bell(u):
    return 0.5 * (1.0 + lax.erf(u * 0.7071067811865476))


def place(pieces, where_to, cuts):
    count = len(pieces)

    def body(to, *refs):
        for k in range(count):
            for (start, rows), out in zip(cuts, refs[count:]):
                out[to[k]] = refs[k][start : start + rows]

    one = pieces[0]
    return call(
        body,
        [where_to, *pieces],
        [shape((count, rows, one.shape[1]), one.dtype) for _, rows in cuts],
        [SMEM] + [VMEM] * count,
        [VMEM] * len(cuts),
        [],
        0,
        2 * count * one.size * one.dtype.itemsize,
        limit=16,
    )


def combine(meta, arrays, outs, tasks, after=()):
    count = len(arrays)
    terms = [(rows, term) for _, _, rows, sources in tasks for term in sources]

    def body(meta, *refs):
        ins, results, held = refs[:count], refs[count : count + len(outs)], refs[count + len(outs) : -1]
        sems = refs[-1]
        copies = [
            pltpu.make_async_copy(view(meta, ins[place_of]), held[k], sems.at[k])
            for k, (_, (place_of, view)) in enumerate(terms)
        ]
        start_all(copies)
        k = 0
        for result, first, rows, sources in tasks:
            wait_all(copies[k : k + len(sources)])
            step = 64 if rows % 64 == 0 else 16

            def some(r, _, k=k, result=result, first=first, step=step, sources=sources):
                at = pl.multiple_of(r * step, 16)
                total = sum(held[k + j][pl.ds(at, step)].astype(F32) for j in range(len(sources)))
                to = pl.multiple_of(first + at, 16)
                results[result][pl.ds(to, step)] = total.astype(results[result].dtype)
                return 0

            lax.fori_loop(0, rows // step, some, 0)
            k += len(sources)

    arrays = [tie(arrays[0], *after), *arrays[1:]]
    return call(
        body,
        [meta, *arrays],
        [shape((rows, WIDE), kind) for rows, kind in outs],
        [SMEM] + [HBM] * count,
        [VMEM] * len(outs),
        [pltpu.VMEM((rows, WIDE), arrays[term[0]].dtype) for rows, term in terms]
        + [pltpu.SemaphoreType.DMA((len(terms),))],
        0,
        60_000_000,
    )


class Tasks:
    def __init__(self, outs):
        self.arrays, self.tasks, self.rows, self.kinds = [], [], [0] * outs, [BF] * outs

    def add(self, out, rows, *terms):
        sources = []
        for array, view in terms:
            known = [k for k, v in enumerate(self.arrays) if v is array]
            if not known:
                self.arrays.append(array)
            sources.append((known[0] if known else len(self.arrays) - 1, view))
        first = self.rows[out]
        self.tasks.append((out, first, rows, sources))
        self.rows[out] += rows
        return first

    def run(self, meta, after=()):
        return combine(meta, self.arrays, list(zip(self.rows, self.kinds)), self.tasks, after)


def chip_row(meta, i):
    return (meta[0] ^ (i & 1)) * 2 + (meta[1] ^ (i >> 1))


def columns(meta, side, half, q):
    start = (meta[2] ^ side) * half + WIDE * q
    return pl.ds(pl.multiple_of(start, 128), WIDE)


def place_in(count, half, i):
    if count == 1:
        return 0, 4 * half + i
    if count == 2:
        return (0, 2 * half + (0 if i == 3 else 1)) if i in (3, 2 - half) else (1, 2 * half + (1 if i == 0 else 0))
    if i == 3 or i == 2 - half:
        return half, 0 if i == 3 else 1
    return 2, 2 * half + (1 if i == 0 else 0)


def piece_at(pieces, i, start, rows):
    if len(pieces) < 4:
        half = start // (DEEP // 2)
        array, at = place_in(len(pieces), half, i)
        return pieces[array].at[at, :, pl.ds(start - half * (DEEP // 2), rows), :]
    if i == 3 and len(pieces) == 5:
        cut = pieces[3].shape[1]
        if start >= cut:
            return pieces[4].at[:, pl.ds(start - cut, rows), :]
    return pieces[i].at[:, pl.ds(start, rows), :]


def chunked(meta, sides, target, sems, first, chunks, to_pieces=False, split=1):
    half = target.shape[-1] // 2
    rows = target.shape[2]
    step = rows // split
    whole = not isinstance(sides, (list, tuple))
    copies = []
    for side in range(2):
        for i in range(4):
            for q in range(chunks):
                for k in range(split):
                    start = first + rows * q + step * k
                    if whole:
                        a = sides.at[:, i, side, pl.ds(start, step), :]
                        place_of, lanes = i, pl.ds(side * half + WIDE * q, WIDE)
                    else:
                        a = piece_at(sides[side], i, start, step)
                        place_of, lanes = chip_row(meta, i), columns(meta, side, half, q)
                    b = target.at[:, place_of, pl.ds(step * k, step), lanes]
                    pair = (b, a) if to_pieces else (a, b)
                    copies.append(pltpu.make_async_copy(*pair, sems.at[len(copies)]))
    return copies


def pieces_of_refs(refs):
    count = len(refs)
    return refs[0] if count == 1 else (refs[: count // 2], refs[count // 2 :])


def start_all(copies):
    for copy in copies:
        copy.start()


def wait_all(copies):
    for copy in copies:
        copy.wait()


def attention_bias(flag, length):
    row = lax.broadcasted_iota(jnp.int32, (length, length), 0) // (length // 2)
    column = lax.broadcasted_iota(jnp.int32, (length, length), 1) // (length // 2)
    return jnp.where(jnp.logical_or(row == column, flag == 0), 0.0, -1e30)


def probabilities(queries, keys, bias):
    s = mat_t(queries, keys) * HEAD_DIM ** (-0.5) + bias
    e = jnp.exp(s - jnp.max(s, -1, keepdims=True))
    return e * (1.0 / jnp.sum(e, -1, keepdims=True))


def head_lanes():
    return lax.broadcasted_iota(jnp.int32, (1, 2 * HEAD_DIM), 1) // HEAD_DIM


def only(lanes, j, v):
    return jnp.where(lanes == j, v, jnp.zeros_like(v))


def tile(ref, t, width):
    z, xy, rows, _ = ref.shape
    return ref[:, :, :, t * width : (t + 1) * width].reshape(z * xy * rows, width)


def attend_forward(meta, x, gain, pieces):
    count = len(pieces)
    length, width = x.shape
    pairs = width // (2 * HEAD_DIM)

    def body(meta, x_ref, gain_ref, *refs):
        src = pieces_of_refs(refs[:count])
        qkv_ref, o_ref, m_ref, wqkv, wo, sems_a, sems_b = refs[count:]
        load_a = chunked(meta, src, wqkv, sems_a, 0, 3)
        load_b = chunked(meta, src, wo, sems_b, width * 3 // 16, 1)
        start_all(load_a)
        start_all(load_b)
        bias = attention_bias(meta[3], length)
        n, _ = normed(x_ref[...])
        hidden = (n * gain_ref[...]).astype(BF)
        wait_all(load_a)
        for t in range(3):
            qkv_ref[:, t * width : (t + 1) * width] = mat(hidden, tile(wqkv, t, width)).astype(BF)
        lanes = head_lanes()

        def pair(p, _):
            take = lambda part: qkv_ref[
                :, pl.ds(pl.multiple_of(part * width + p * 2 * HEAD_DIM, 128), 2 * HEAD_DIM)
            ]
            q, k, v = take(0), take(1), take(2)
            outs = [
                mat(probabilities(only(lanes, j, q), k, bias).astype(BF), v) for j in range(2)
            ]
            o_ref[:, pl.ds(pl.multiple_of(p * 2 * HEAD_DIM, 128), 2 * HEAD_DIM)] = jnp.where(
                lanes == 0, outs[0], outs[1]
            ).astype(BF)
            return 0

        lax.fori_loop(0, pairs, pair, 0, unroll=True)
        wait_all(load_b)
        m_ref[...] = x_ref[...] + mat(o_ref[...], tile(wo, 0, width))

    return call(
        body,
        [meta, x, gain, *pieces],
        (shape((length, 3 * width), BF), shape((length, width), BF), shape((length, width), F32)),
        [SMEM, VMEM, VMEM] + [HBM] * count,
        (VMEM,) * 3,
        [
            pltpu.VMEM((4, 4, width // 16, 3 * width), BF),
            pltpu.VMEM((4, 4, width // 16, width), BF),
            pltpu.SemaphoreType.DMA((24,)),
            pltpu.SemaphoreType.DMA((8,)),
        ],
        2 * length * width * width * 4 + 4 * length * length * width * 2,
        36_000_000,
    )


def feed_forward(meta, m, gain, pieces):
    count = len(pieces)
    length, width = m.shape
    wide = 4 * width

    def body(meta, m_ref, gain_ref, *refs):
        src = pieces_of_refs(refs[:count])
        u_ref, a_ref, y_ref, wu, wd, sems_a, sems_b = refs[count:]
        load_a = chunked(meta, src, wu, sems_a, 0, 4)
        load_b = chunked(meta, src, wd, sems_b, width // 4, 1)
        start_all(load_a)
        start_all(load_b)
        n, _ = normed(m_ref[...])
        hidden = (n * gain_ref[...]).astype(BF)
        wait_all(load_a)
        wait_all(load_b)
        total = m_ref[...]
        for t in range(4):
            u = mat(hidden, tile(wu, t, width))
            u_ref[:, t * width : (t + 1) * width] = u
            a = (u * bell(u)).astype(BF)
            a_ref[:, t * width : (t + 1) * width] = a
            total = total + mat(a, wd[t].reshape(width, width))
        y_ref[...] = total

    return call(
        body,
        [meta, m, gain, *pieces],
        (shape((length, wide), F32), shape((length, wide), BF), shape((length, width), F32)),
        [SMEM, VMEM, VMEM] + [HBM] * count,
        (VMEM,) * 3,
        [
            pltpu.VMEM((4, 4, width // 16, wide), BF),
            pltpu.VMEM((4, 4, width // 4, width), BF),
            pltpu.SemaphoreType.DMA((32,)),
            pltpu.SemaphoreType.DMA((8,)),
        ],
        2 * length * width * wide * 2,
        26_000_000,
    )


def piece_shapes(rows, parts):
    part = lambda count: shape((count, 4, rows, WIDE), BF)
    others = {1: (part(8),), 2: (part(4), part(4)), 3: (part(2), part(2), part(4))}
    return (part(8),) + others[parts]


def whole_shape():
    return shape((4, 4, 2, 2 * DEEP, WIDE), BF)


def down_backward(meta, dy, a):
    length, width = dy.shape

    def body(meta, dy_ref, a_ref, *refs):
        *outs, stage, sems = refs
        low = dy_ref[...].astype(BF)
        for t in range(4):
            stage[t] = (
                t_mat(a_ref[:, t * width : (t + 1) * width], low)
                .astype(BF)
                .reshape(4, width // 4, width)
            )
        copies = chunked(meta, (outs[:1], outs[1:]), stage, sems, 0, 1, True, 2)
        start_all(copies)
        wait_all(copies)

    outs = piece_shapes(DEEP // 2, 2)
    return call(
        body,
        [meta, dy, a],
        outs,
        [SMEM, VMEM, VMEM],
        (HBM,) * 3,
        [pltpu.VMEM((4, 4, width // 4, width), BF), pltpu.SemaphoreType.DMA((16,))],
        8 * length * width * width,
        13_000_000,
    )


def feed_backward(meta, dy, m, u, gain, pieces):
    count = len(pieces)
    length, width = m.shape
    wide = 4 * width

    def body(meta, dy_ref, m_ref, u_ref, gain_ref, *refs):
        src = pieces_of_refs(refs[:count])
        dm_ref, gg_ref, *outs = refs[count:-5]
        wu, wd, stage, sems_a, sems_b = refs[-5:]
        outs = outs[:1], outs[1:]
        load_a = chunked(meta, src, wu, sems_a, 0, 4)
        load_b = chunked(meta, src, wd, sems_b, width // 4, 1)
        start_all(load_b)
        start_all(load_a)
        n, root = normed(m_ref[...])
        gain = gain_ref[...]
        hidden_t = (n * gain).astype(BF).T
        low = dy_ref[...].astype(BF)
        wait_all(load_b)
        wait_all(load_a)
        dh = jnp.zeros((length, width), F32)
        for t in range(4):
            da = mat_t(low, wd[t].reshape(width, width))
            u = u_ref[:, t * width : (t + 1) * width]
            slope = bell(u) + u * (jnp.exp(-0.5 * u * u) * 0.3989422804014327)
            du = (da * slope).astype(BF)
            stage[:, :, :, t * width : (t + 1) * width] = (
                mat(hidden_t, du).astype(BF).reshape(4, 4, width // 16, width)
            )
            dh = dh + mat_t(du, tile(wu, t, width))
        store = chunked(meta, outs, stage, sems_a, 0, 4, True)
        start_all(store)
        gg_ref[...] = jnp.sum(dh * n, 0, keepdims=True)
        dm_ref[...] = dy_ref[...] + norm_back(n, root, dh * gain)
        wait_all(store)

    return call(
        body,
        [meta, dy, m, u, gain, *pieces],
        (shape((length, width), F32), shape((1, width), F32)) + piece_shapes(DEEP // 2, 2),
        [SMEM] + [VMEM] * 4 + [HBM] * count,
        (VMEM, VMEM) + (HBM,) * 3,
        [
            pltpu.VMEM((4, 4, width // 16, wide), BF),
            pltpu.VMEM((4, 4, width // 4, width), BF),
            pltpu.VMEM((4, 4, width // 16, wide), BF),
            pltpu.SemaphoreType.DMA((32,)),
            pltpu.SemaphoreType.DMA((8,)),
        ],
        2 * length * width * wide * 3,
        40_000_000,
    )


def feed_both(meta, m, dy, gain, pieces):
    length, width = m.shape
    wide = 4 * width
    count = len(pieces)

    def body(meta, m_ref, dy_ref, gain_ref, *refs):
        src = pieces_of_refs(refs[:count])
        y_ref, dm_ref, gg_ref, whole = refs[count : count + 4]
        wu, wd, a_ref, slope_ref, stage_u, stage_d, sems_a, sems_b, sems_c, sems_d = refs[count + 4 :]
        load_a = chunked(meta, src, wu, sems_a, DEEP, 4)
        load_b = chunked(meta, src, wd, sems_b, 2 * DEEP, 1)
        start_all(load_a)
        start_all(load_b)
        n, root = normed(m_ref[...])
        gain = gain_ref[...]
        hidden = (n * gain).astype(BF)
        hidden_t = (n * gain).astype(BF).T
        low = dy_ref[...].astype(BF)
        wait_all(load_a)
        for t in range(4):
            u = mat(hidden, tile(wu, t, width))
            share = bell(u)
            a = (u * share).astype(BF)
            a_ref[:, t * width : (t + 1) * width] = a
            slope_ref[:, t * width : (t + 1) * width] = share + u * (
                jnp.exp(-0.5 * u * u) * 0.3989422804014327
            )
            stage_d[t] = t_mat(a, low).astype(BF).reshape(4, width // 4, width)
        store_d = chunked(meta, whole, stage_d, sems_d, DEEP, 1, True)
        start_all(store_d)
        wait_all(load_b)
        dh = jnp.zeros((length, width), F32)
        for t in range(4):
            da = mat_t(low, wd[t].reshape(width, width))
            du = (da * slope_ref[:, t * width : (t + 1) * width]).astype(BF)
            stage_u[:, :, :, t * width : (t + 1) * width] = (
                mat(hidden_t, du).astype(BF).reshape(4, 4, width // 16, width)
            )
            dh = dh + mat_t(du, tile(wu, t, width))
        store_u = chunked(meta, whole, stage_u, sems_c, 0, 4, True)
        start_all(store_u)
        gg_ref[...] = jnp.sum(dh * n, 0, keepdims=True)
        dm_ref[...] = dy_ref[...] + norm_back(n, root, dh * gain)
        total = m_ref[...]
        for t in range(4):
            total = total + mat(a_ref[:, t * width : (t + 1) * width], wd[t].reshape(width, width))
        y_ref[...] = total
        wait_all(store_d)
        wait_all(store_u)

    return call(
        body,
        [meta, m, dy, gain, *pieces],
        (
            shape((length, width), F32),
            shape((length, width), F32),
            shape((1, width), F32),
            whole_shape(),
        ),
        [SMEM] + [VMEM] * 3 + [HBM] * count,
        (VMEM, VMEM, VMEM, HBM),
        [
            pltpu.VMEM((4, 4, width // 16, wide), BF),
            pltpu.VMEM((4, 4, width // 4, width), BF),
            pltpu.VMEM((length, wide), BF),
            pltpu.VMEM((length, wide), F32),
            pltpu.VMEM((4, 4, width // 16, wide), BF),
            pltpu.VMEM((4, 4, width // 4, width), BF),
            pltpu.SemaphoreType.DMA((32,)),
            pltpu.SemaphoreType.DMA((8,)),
            pltpu.SemaphoreType.DMA((32,)),
            pltpu.SemaphoreType.DMA((8,)),
        ],
        2 * length * width * wide * 6,
        60_000_000,
    )


def gain_place(pieces, half, i):
    array, at = place_in(len(pieces), half, i)
    return pieces[array].at[at, :, pl.ds(DEEP // 2, GAIN_ROWS), :]


def gain_rows(stage, one, two):
    width = one.shape[1]
    share = width // 16
    row = lax.broadcasted_iota(jnp.int32, (GAIN_ROWS, width), 0)
    both = jnp.where(row == 0, one, jnp.where(row == 1, two, 0.0))
    tall = jnp.broadcast_to(both[None], (16, GAIN_ROWS, width)).reshape(16 * GAIN_ROWS, width)
    chip = lax.broadcasted_iota(jnp.int32, tall.shape, 0) // GAIN_ROWS
    feature = lax.broadcasted_iota(jnp.int32, tall.shape, 1)
    tall = jnp.where(feature // share == chip, tall, 0.0).astype(BF)
    feature = lax.broadcasted_iota(jnp.int32, (width, 128), 0)
    lane = lax.broadcasted_iota(jnp.int32, (width, 128), 1)
    pick = jnp.where(feature % share == lane, 1.0, 0.0).astype(BF)
    stage[...] = jnp.zeros(stage.shape, BF)
    stage[:, :, :, :128] = mat(tall, pick).astype(BF).reshape(4, 4, GAIN_ROWS, 128)


def attend_backward(meta, dm, x, qkv, o, gain, gg_two, pieces):
    count = len(pieces)
    length, width = x.shape
    pairs = width // (2 * HEAD_DIM)
    scale = HEAD_DIM ** (-0.5)

    def body(meta, dm_ref, x_ref, qkv_ref, o_ref, gain_ref, gg_two_ref, *refs):
        src = pieces_of_refs(refs[:count])
        dx_ref = refs[count]
        outs = refs[count + 1 : count + 2], refs[count + 2 : count + 5]
        wqkv, wo, stage, stage_o, stage_g, do_ref, dqkv, sems_a, sems_b, sems_c = refs[count + 5 :]
        load_b = chunked(meta, src, wo, sems_b, width * 3 // 16, 1)
        load_a = chunked(meta, src, wqkv, sems_a, 0, 3)
        start_all(load_b)
        start_all(load_a)
        bias = attention_bias(meta[3], length)
        low = dm_ref[...].astype(BF)
        stage_o[...] = t_mat(o_ref[...], low).astype(BF).reshape(4, 4, width // 16, width)
        wait_all(load_b)
        do_ref[...] = mat_t(low, tile(wo, 0, width)).astype(BF)
        store_b = chunked(meta, outs, stage_o, sems_b, width * 3 // 16, 1, True)
        start_all(store_b)
        lanes = head_lanes()

        def pair(p, _):
            at = lambda part: pl.ds(
                pl.multiple_of(part * width + p * 2 * HEAD_DIM, 128), 2 * HEAD_DIM
            )
            q, k, v = qkv_ref[:, at(0)], qkv_ref[:, at(1)], qkv_ref[:, at(2)]
            d = do_ref[:, at(0)]
            dq, dk, dv = [], [], []
            for j in range(2):
                soft = probabilities(only(lanes, j, q), k, bias)
                dp = mat_t(only(lanes, j, d), v)
                ds = (soft * (dp - jnp.sum(dp * soft, -1, keepdims=True))).astype(BF)
                dv.append(t_mat(soft.astype(BF), d))
                dq.append(mat(ds, k) * scale)
                dk.append(t_mat(ds, q) * scale)
            for part, two in enumerate((dq, dk, dv)):
                dqkv[:, at(part)] = jnp.where(lanes == 0, two[0], two[1]).astype(BF)
            return 0

        lax.fori_loop(0, pairs, pair, 0, unroll=2)
        n, root = normed(x_ref[...])
        gain = gain_ref[...]
        hidden_t = (n * gain).astype(BF).T
        wait_all(load_a)
        dh = jnp.zeros((length, width), F32)
        for t in range(3):
            d = dqkv[:, t * width : (t + 1) * width]
            stage[:, :, :, t * width : (t + 1) * width] = (
                mat(hidden_t, d).astype(BF).reshape(4, 4, width // 16, width)
            )
            dh = dh + mat_t(d, tile(wqkv, t, width))
        store_a = chunked(meta, outs, stage, sems_a, 0, 3, True)
        start_all(store_a)
        gain_rows(stage_g, jnp.sum(dh * n, 0, keepdims=True), gg_two_ref[...])
        store_c = [
            pltpu.make_async_copy(
                stage_g.at[:, chip_row(meta, i)],
                gain_place(outs[side], half, i),
                sems_c.at[8 * half + 4 * side + i],
            )
            for half in range(2)
            for side in range(2)
            for i in range(4)
        ]
        start_all(store_c)
        dx_ref[...] = dm_ref[...] + norm_back(n, root, dh * gain)
        wait_all(store_a)
        wait_all(store_b)
        wait_all(store_c)

    return call(
        body,
        [meta, dm, x, qkv, o, gain, gg_two, *pieces],
        (shape((length, width), F32),) + piece_shapes(DEEP // 2 + GAIN_ROWS, 3),
        [SMEM] + [VMEM] * 6 + [HBM] * count,
        (VMEM,) + (HBM,) * 4,
        [
            pltpu.VMEM((4, 4, width // 16, 3 * width), BF),
            pltpu.VMEM((4, 4, width // 16, width), BF),
            pltpu.VMEM((4, 4, width // 16, 3 * width), BF),
            pltpu.VMEM((4, 4, width // 16, width), BF),
            pltpu.VMEM((4, 4, GAIN_ROWS, WIDE), BF),
            pltpu.VMEM((length, width), BF),
            pltpu.VMEM((length, 3 * width), BF),
            pltpu.SemaphoreType.DMA((24,)),
            pltpu.SemaphoreType.DMA((8,)),
            pltpu.SemaphoreType.DMA((16,)),
        ],
        2 * length * width * width * 8 + 2 * length * length * width * 10,
        52_000_000,
    )


def index_of(v, i):
    return lax.dynamic_index_in_dim(v, i, 0, keepdims=False)


class Grid:
    def __init__(self):
        dp, seq = lax.axis_index("dp"), lax.axis_index("seq")
        self.z, self.x, self.y, self.c = dp // 2, dp % 2, seq // 2, seq % 2
        places = [(z, x, y, c) for z in range(4) for x in range(2) for y in range(2) for c in range(2)]
        flat = lambda z, x, y, c: (z * 2 + x) * 4 + y * 2 + c
        to = lambda move: [(flat(*p), flat(*move(*p))) for p in places]
        self.perm_c = to(lambda z, x, y, c: (z, x, y, 1 - c))
        self.perm_x = to(lambda z, x, y, c: (z, 1 - x, y, c))
        self.perm_y = to(lambda z, x, y, c: (z, x, 1 - y, c))
        self.perm_z = [to(lambda z, x, y, c, k=k: (z ^ k, x, y, c)) for k in range(4)]

    def over_c(self, v):
        return lax.ppermute(v, LINES, self.perm_c)

    def over_x(self, v):
        return lax.ppermute(v, LINES, self.perm_x)

    def over_y(self, v):
        return lax.ppermute(v, LINES, self.perm_y)

    def over_z(self, v, k):
        return lax.ppermute(v, LINES, self.perm_z[k])

    def planes(self, block, before=(), after=()):
        block = tie(block, *before)
        parts = [tie(block, *after)] + [self.over_z(block, k) for k in (1, 2, 3)]
        order = jnp.stack([self.z ^ k for k in range(4)]).astype(jnp.int32)
        return place(parts, order, [(0, block.shape[0])])[0]


class Gathering:
    def __init__(self, grid, own, cut):
        self.grid, self.own, self.cut = grid, own, cut

    def first(self, *after):
        own = tie(self.own, *after)
        self.by_x, self.by_y = self.grid.over_x(own), self.grid.over_y(own)
        return [self.by_x, self.by_y]

    def second(self, *after):
        a, b = tie(self.by_x, *after), tie(self.by_y, *after)
        self.both = [self.grid.over_y(a[:, : self.cut]), self.grid.over_x(b[:, self.cut :])]
        return self.both

    def pieces(self, *after):
        here = [self.own, self.by_x, self.by_y, *(tie(v, *after) for v in self.both)]
        return here + [self.grid.over_c(v) for v in here]


class Reduction:
    def __init__(self, grid, *pieces):
        flat = lambda v: v.reshape(v.shape[0], -1, WIDE)
        self.mine = flat(pieces[0])
        self.came = [flat(grid.over_c(v)) for v in pieces[1:]]
        self.rows = self.mine.shape[1]

    def other(self, i, half, *rest):
        array, at = place_in(len(self.came), half, i)
        return self.came[array], lambda meta, ref: ref.at[(at, *[f(meta) for f in rest])]

    def part(self, i, half):
        return (self.mine, lambda meta, ref: ref.at[4 * half + i]), self.other(i, half)

    def at_plane(self, half, plane, count):
        rows = self.rows // 4

        def inside(first):
            return lambda meta, ref: ref.at[pl.ds(pl.multiple_of(first + plane(meta) * rows, 16), count)]

        def at(meta):
            return pl.ds(pl.multiple_of(plane(meta) * rows, 16), count)

        def own(meta, ref):
            return ref.at[4 * half, at(meta)]

        cells = [self.straight[half], self.last[half]]
        return [(self.mine, own), self.other(0, half, at)] + [(v, inside(first)) for v, first in cells]

    def counts(self):
        return DEEP // 2, self.rows // 4


def cell(v, first, rows):
    return v, lambda meta, ref: ref.at[pl.ds(first, rows)]


def step(grid, meta, after, seconds, firsts):
    tasks = Tasks(2)
    ends = []
    for r in seconds:
        for half in (0, 1):
            terms = r.part(1 + half, half) + (cell(*r.diagonal[half], r.rows),)
            ends.append((r, half, "last", 1 - half, tasks.add(1 - half, r.rows, *terms)))
    for r in firsts:
        for half in (0, 1):
            rows = r.rows
            ends.append((r, half, "diagonal", half, tasks.add(half, rows, *r.part(3, half))))
            ends.append((r, half, "straight", half, tasks.add(half, rows, *r.part(2 - half, half))))
    sent = tasks.run(meta, after)
    came = [grid.over_y(sent[0]), grid.over_x(sent[1])]
    for r, half, name, way, first in ends:
        if not hasattr(r, name):
            setattr(r, name, [None, None])
        getattr(r, name)[half] = (came[way], first)
    return sent, came


class Planes:
    def __init__(self, grid, meta, *reductions, at_once=False, after=()):
        self.grid, self.meta = grid, meta
        self.depth = sum(sum(r.counts()) for r in reductions)
        z = lambda meta: meta[4]
        if at_once:
            planes = [[lambda meta, k=k: z(meta) ^ k] for k in range(4)]
        else:
            planes = [[lambda meta, k=k, q=q: (z(meta) // 2 ^ k) * 2 + q for q in range(2)] for k in range(2)]
        tasks = Tasks(len(planes))
        tasks.kinds[0] = F32
        for out, group in enumerate(planes):
            for plane in group:
                for r in reductions:
                    for half in (0, 1):
                        tasks.add(out, r.counts()[half], *r.at_plane(half, plane, r.counts()[half]))
        self.kept, *sent = tasks.run(meta, after)
        self.sent = sent
        self.came = [grid.over_z(v, k) for v, k in zip(sent, (1, 2, 3) if at_once else (2,))]

    def second(self, *after):
        rows = self.depth
        tasks = Tasks(2)
        tasks.kinds[0] = F32
        for out in (0, 1):
            view = lambda meta, ref, out=out: ref.at[
                pl.ds(pl.multiple_of((meta[4] % 2 ^ out) * rows, 16), rows)
            ]
            tasks.add(out, rows, (self.kept, view), (self.came[0], view))
        self.kept, sent = tasks.run(self.meta, after)
        self.came = [self.grid.over_z(sent, 1)]

    def sums(self, layout, *after):
        return own_and_other(self.grid, self.meta, layout, tie(self.kept, *after), *self.came)


def own_and_other(grid, meta, layout, kept, *came):
    leave = sum(chunks * rows // 2 for _, chunks, rows in layout)
    count = len(came)

    def body(meta, kept, *refs):
        came, total, out = refs[:count], refs[count], refs[count + 1]
        total[...] = sum((v[...].astype(F32) for v in came), kept[...].astype(F32))
        at = 0
        for first, chunks, rows in layout:
            half = rows // 2
            for q in range(chunks):
                start = first + rows * q + half * (1 - meta[2])
                out[at : at + half] = total[pl.ds(pl.multiple_of(start, 8), half)]
                at += half

    total, out = call(
        body,
        [meta, kept, *came],
        [shape(kept.shape, F32), shape((leave, WIDE), F32)],
        [SMEM] + [VMEM] * (1 + count),
        [VMEM] * 2,
        [],
        0,
        5_000_000,
        limit=16,
    )
    return total, grid.over_c(out)


def tie(v, *after):
    return lax.optimization_barrier((v, *after))[0] if after else v


def seq_swaps(pieces_of, cuts):
    me, count = lax.axis_index("seq"), lax.axis_size("seq")
    kept = [pieces_of(me)]
    for r in range(1, count):
        kept.append(lax.ppermute(pieces_of(me ^ r), "seq", [(s, s ^ r) for s in range(count)]))
    order = jnp.stack([me ^ r for r in range(count)]).astype(jnp.int32)
    return lambda *after: place([tie(kept[0], *after), *kept[1:]], order, cuts)


def swap_all(grid, v, cuts):
    y, c = grid.y, grid.c
    pairs = v.reshape(2, 2, *v.shape[1:])
    stay = index_of(pairs, y)
    came = grid.over_y(index_of(pairs, 1 - y))
    other = grid.over_c(jnp.stack([index_of(stay, 1 - c), index_of(came, 1 - c)]))
    order = jnp.stack([y * 2 + c, (1 - y) * 2 + c, y * 2 + 1 - c, (1 - y) * 2 + 1 - c]).astype(jnp.int32)
    own = index_of(stay, c)
    return lambda *after: place(
        [tie(own, *after), index_of(came, c), other[0], other[1]], order, cuts
    )


def to_blocks(*arrays):
    quarter, width = arrays[0].shape[1:]
    cuts = [(quarter * k, quarter) for k in range(len(arrays))]
    end = seq_swaps(lambda s: jnp.concatenate([index_of(v, s) for v in arrays]), cuts)
    return lambda *after: [v.reshape(-1, width) for v in end(*after)]


def from_block(v, quarter):
    parts = v.reshape(-1, quarter, v.shape[-1])
    end = seq_swaps(lambda s: index_of(parts, s), [(0, quarter)])
    return lambda *after: end(*after)[0]


def both_halves(matrix):
    rows, wide = matrix.shape
    return matrix.reshape(rows, 2, wide // 2 // WIDE, WIDE).transpose(1, 2, 0, 3)


def lower_gains(ln1_gain, ln2_gain):
    return jnp.stack([ln1_gain, ln2_gain]).astype(BF)


def own_chunks(masters, core):
    views = []
    for l in range(masters[0].shape[0]):
        for ref, chunks in zip(masters, (3, 1, 4, 1)):
            for q in range(chunks):
                start = core * (ref.shape[2] // 2) + WIDE * q
                views.append(ref[l, :, pl.ds(pl.multiple_of(start, 128), WIDE)])
    return views


def chip_blocks(grid, meta, ln1_gain, ln2_gain, masters):
    layers, rows = masters[0].shape[:2]
    total = layers * 4 * 4 * rows * 3 // 4

    def leave(meta, one, two, *refs):
        ins, out = refs[:4], refs[4]
        start = 0
        for v in own_chunks(ins, 1 - meta[2]):
            out[start : start + v.shape[0]] = v
            start += v.shape[0]
        out[start : start + 8] = jnp.zeros((8, WIDE), F32)
        out[start : start + layers, :rows] = one[...]
        out[start + layers : start + 2 * layers, :rows] = two[...]

    size = sum(v.size for v in masters) * 8
    sent = call(
        leave,
        [meta, ln1_gain, ln2_gain, *masters],
        shape((total + 8, WIDE), F32),
        [SMEM] + [VMEM] * 6,
        VMEM,
        [],
        0,
        size,
        limit=16,
    )
    came = grid.over_c(sent)

    def merge(meta, sent, came, *refs):
        ins, outs, stage = refs[:4], refs[4:-1], refs[-1]
        core = meta[2]
        start = 0
        for v in own_chunks(ins, core):
            depth = v.shape[0]
            stage[pl.ds(pl.multiple_of(2 * start + core * depth, 8), depth)] = v
            stage[pl.ds(pl.multiple_of(2 * start + (1 - core) * depth, 8), depth)] = came[start : start + depth]
            start += depth
        stage[pl.ds(pl.multiple_of(2 * start + core * 8, 8), 8)] = sent[start : start + 8]
        stage[pl.ds(pl.multiple_of(2 * start + (1 - core) * 8, 8), 8)] = came[start : start + 8]
        first = 0
        for j, out in enumerate(outs):
            depth = DEEP * (1 + j % 2)
            out[:depth] = stage[first : first + depth].astype(BF)
            first += depth
        outs[0][DEEP:] = stage[first:].astype(BF)

    outs = [
        shape((DEEP * (1 + j % 2) + (GAIN_ROWS if j == 0 else 0), WIDE), BF) for j in range(2 * layers)
    ]
    return call(
        merge,
        [meta, sent, came, *masters],
        outs,
        [SMEM] + [VMEM] * 6,
        [VMEM] * len(outs),
        [pltpu.VMEM((2 * total + GAIN_ROWS, WIDE), F32)],
        0,
        size,
        limit=20,
    )


def finish(meta, sums, rows, width):
    layers = len(sums)

    def body(meta, *refs):
        count = 4 * layers
        ins, (one, two, *outs) = refs[:count], refs[count:]
        core = meta[2]
        for l in range(layers):
            feed, came, attn, came_attn = ins[4 * l : 4 * l + 4]

            def put(out, q, total, first, depth, came, at):
                half = out.shape[2] // 2
                columns = lambda c: pl.ds(pl.multiple_of(c * half + WIDE * q, 128), WIDE)
                out[l, :, columns(core)] = total[pl.ds(pl.multiple_of(first + core * depth, 8), depth)]
                out[l, :, columns(1 - core)] = came[at : at + depth]

            put(outs[3], 0, feed, DEEP, 4 * rows, came, 4 * rows)
            for q in range(4):
                put(outs[2], q, feed, 2 * rows * q, rows, came, q * rows)
            for q in range(3):
                put(outs[0], q, attn, 2 * rows * q, rows, came_attn, q * rows)
            put(outs[1], 0, attn, 6 * rows, rows, came_attn, 3 * rows)
            for g, out in enumerate((one, two)):
                both = attn[DEEP + g : DEEP + g + 1, : 2 * rows]
                out[l : l + 1] = jnp.where(core == 0, both[:, :rows], both[:, rows:])

    gain = shape((layers, rows), F32)
    outs = [gain, gain] + [
        shape((layers, r, w), F32)
        for r, w in ((rows, 3 * width), (rows, width), (rows, 4 * width), (4 * rows, width))
    ]
    flat = [v for l in range(layers) for v in sums[l]]
    one, two, qkv, out, up, down = call(
        body,
        [meta, *flat],
        outs,
        [SMEM] + [VMEM] * len(flat),
        [VMEM] * len(outs),
        [],
        0,
        8 * sum(v.size for v in flat),
        limit=20,
    )
    return one, qkv, out, two, up, down


def whole_gains(grid, gathering, layers, rows):
    g = gathering
    diagonal = g.both[1][:, -GAIN_ROWS:]
    tails = jnp.stack([v[:, -GAIN_ROWS:, :rows] for v in (g.own, g.by_x, g.by_y, diagonal)])
    tails = tails.reshape(2, 2, 4, 2, 8, rows)[:, :, :, :, : 2 * layers]
    tails = jnp.where(grid.y == 0, tails, tails[::-1])
    tails = jnp.where(grid.x == 0, tails, tails[:, ::-1])
    return tails.transpose(4, 2, 1, 0, 3, 5).reshape(2, layers, -1)


def pieces_of_whole(matrices):
    parts = []
    for whole in matrices:
        rows, wide = whole.shape
        parts.append(
            whole.reshape(4, 4, rows // 16, 2, wide // 2 // WIDE, WIDE).transpose(3, 1, 0, 4, 2, 5)
            .reshape(2, 4, 4, -1, WIDE)
        )
    stacked = jnp.concatenate(parts, 3)
    order = [(i & 1) * 2 + (i >> 1) for i in range(4)]
    return [stacked[side, order[i]] for side in range(2) for i in range(4)]


def whole_of_pieces(*pieces, widths):
    cut = DEEP // 2
    sides = []
    for arrays in (pieces[:1], pieces[1:]):
        places = [[place_in(len(arrays), half, i) for i in range(4)] for half in (0, 1)]
        sides.append([jnp.stack([arrays[array][at] for array, at in row]) for row in places])
    both = [jnp.concatenate([a[:, :, :cut], b[:, :, :cut]], 2) for a, b in sides]
    stacked = jnp.stack(both)
    stacked = jnp.stack([stacked[:, i] for i in (0, 2, 1, 3)], 1)
    outs, start = [], 0
    for rows, wide in widths:
        depth, chunks = rows // 16, wide // 2 // WIDE
        part = stacked[:, :, :, start : start + depth * chunks]
        start += depth * chunks
        outs.append(
            part.reshape(2, 4, 4, chunks, depth, WIDE).transpose(2, 1, 4, 0, 3, 5).reshape(rows, wide)
        )
    return outs


def per_device(
    states,
    item_halves,
    ln1_gain,
    qkv_weight,
    out_weight,
    ln2_gain,
    up_weight,
    down_weight,
    cotangent,
):
    masters = (qkv_weight, out_weight, up_weight, down_weight)
    layers, gain_shard = ln1_gain.shape
    quarter, width = states.shape[1:]
    near = lax.axis_size("dp") == 8 and lax.axis_size("seq") == 4 and layers == 2
    gains = lower_gains(ln1_gain, ln2_gain)
    flag = index_of(item_halves, lax.axis_index("seq"))
    if near:
        return by_permutes(states, flag, ln1_gain, ln2_gain, masters, cotangent, quarter)
    zero = jnp.zeros((), jnp.int32)
    meta = jnp.stack([zero, zero, zero, flag]).astype(jnp.int32)
    x, grad = to_blocks(states, cotangent)()
    gains = lax.all_gather(gains, LINES, axis=2, tiled=True).astype(F32)
    kept = []
    for l in range(layers):
        qkv, out, up, down = (
            lax.all_gather(v[l].astype(BF), LINES, axis=0, tiled=True) for v in masters
        )
        attn, feed = pieces_of_whole([qkv, out]), pieces_of_whole([up, down])
        qkv, o, m = attend_forward(meta, x, gains[0, l][None], attn)
        u, a, y = feed_forward(meta, m, gains[1, l][None], feed)
        kept.append((x, qkv, o, m, u, a, attn, feed))
        x = y
    outputs = x
    results = [None] * layers
    for l in reversed(range(layers)):
        x, qkv, o, m, u, a, attn, feed = kept[l]
        down_pieces = down_backward(meta, grad, a)
        dm, gg_two, *up_pieces = feed_backward(meta, grad, m, u, gains[1, l][None], feed)
        grad, *attn_pieces = attend_backward(meta, dm, x, qkv, o, gains[0, l][None], gg_two, attn)
        wholes = (
            whole_of_pieces(*attn_pieces, widths=((width, 3 * width), (width, width)))
            + whole_of_pieces(*up_pieces, widths=((width, 4 * width),))
            + whole_of_pieces(*down_pieces, widths=((4 * width, width),))
        )
        gain_sums = attn_pieces[0][:4, :, DEEP // 2 :, : width // 16]
        gain_sums = jnp.stack([gain_sums[i] for i in (0, 2, 1, 3)]).transpose(2, 1, 0, 3).reshape(GAIN_ROWS, width)
        sums = [
            lax.psum_scatter(v.astype(F32), LINES, scatter_dimension=0, tiled=True) for v in wholes
        ]
        gain_sums = lax.psum(gain_sums[:2].astype(F32), LINES)
        owner = lax.axis_index(LINES) * gain_shard
        results[l] = (lax.dynamic_slice_in_dim(gain_sums, owner, gain_shard, 1), *sums)
    return collect(from_block(outputs, quarter)(), from_block(grad, quarter)(), results)


def collect(outputs, grad_states, results):
    gains, qkv, out, up, down = (jnp.stack([r[k] for r in results]) for k in range(5))
    return outputs, grad_states, gains[:, 0], qkv, out, gains[:, 1], up, down


def by_permutes(states, flag, ln1_gain, ln2_gain, masters, cotangent, quarter):
    grid = Grid()
    meta = jnp.stack([grid.x, grid.y, grid.c, flag, grid.z]).astype(jnp.int32)
    layers, rows = masters[0].shape[:2]
    width = states.shape[2]
    blocks = chip_blocks(grid, meta, ln1_gain, ln2_gain, masters)
    come = swap_all(
        grid,
        jnp.concatenate([tie(states, blocks[0]), cotangent], 1),
        [(0, quarter), (quarter, quarter)],
    )
    layer1 = lax.all_gather(jnp.concatenate(blocks[2:]), LINES, axis=0, tiled=True)
    layer1 = [layer1.reshape(4, 4, 2, 3 * DEEP, WIDE)]
    own = grid.planes(blocks[0])
    attn0 = Gathering(grid, own, DEEP // 2)
    attn0.first()
    own = grid.planes(blocks[1], (own,), (attn0.by_x, attn0.by_y))
    attn0.second()
    x, grad = (v.reshape(-1, width) for v in come(*attn0.both))
    feed0 = Gathering(grid, own, DEEP)
    feed0.first(*attn0.both)
    gains = whole_gains(grid, attn0, layers, rows).astype(F32)
    attn0 = attn0.pieces()
    qkv0, o0, m0 = attend_forward(meta, x, gains[0, 0][None], attn0)
    feed0.second(m0)
    feed0 = feed0.pieces()
    u0, a0, x1 = feed_forward(meta, m0, gains[1, 0][None], feed0)
    qkv1, o1, m1 = attend_forward(meta, x1, gains[0, 1][None], layer1)
    y, dm, gg_two, whole = feed_both(meta, m1, grad, gains[1, 1][None], layer1)
    whole = lax.psum_scatter(whole.reshape(-1, WIDE), LINES, scatter_dimension=0, tiled=True)
    grad, *pieces = attend_backward(meta, dm, x1, qkv1, o1, gains[0, 1][None], gg_two, layer1)
    attn1 = Reduction(grid, *pieces)
    down_pieces = down_backward(meta, grad, a0)
    down0 = Reduction(grid, *down_pieces)
    ready, came1 = step(grid, meta, (down_pieces[0],), (), (attn1,))
    dm, gg_two, *pieces = feed_backward(
        meta, tie(grad, down_pieces[0], *ready), m0, u0, gains[1, 0][None], feed0
    )
    up0 = Reduction(grid, *pieces)
    ready, came2 = step(grid, meta, (dm, *down0.came, *came1), (attn1,), (down0,))
    dm = tie(dm, *ready)
    grad, *pieces = attend_backward(meta, dm, x, qkv0, o0, gains[0, 0][None], gg_two, attn0)
    attn0 = Reduction(grid, *pieces)
    sent, came3 = step(grid, meta, (grad, *attn0.came[:2], up0.came[0], *came2), (down0,), (up0, attn0))
    planes_attn1 = Planes(grid, meta, attn1, at_once=True, after=sent)
    sent, came4 = step(grid, meta, (*planes_attn1.came, *came3), (up0, attn0), ())
    feed = ((0, 4, 2 * rows), (DEEP, 1, DEEP))
    attend = ((0, 4, 2 * rows),)
    both = (feed[0], (DEEP, 4, 2 * rows))
    sums_attn1 = planes_attn1.sums(attend, *sent)
    planes_down0 = Planes(grid, meta, down0, at_once=True, after=sent)
    planes0 = Planes(grid, meta, up0, attn0, at_once=True, after=planes_down0.came)
    results = jnp.concatenate([v.reshape(4, quarter, width) for v in (tie(y, *planes0.sent), grad)], 1)
    results = swap_all(grid, results, [(0, quarter), (quarter, quarter)])
    outputs, grad_states = results(*planes0.came)
    sums1 = own_and_other(grid, meta, feed, tie(whole, *planes0.sent))
    total_down, came_down = planes_down0.sums(((0, 1, DEEP),), *planes0.sent)
    total, came = planes0.sums(both)
    cut = DEEP // 2
    sums0 = (
        jnp.concatenate([total[:DEEP], total_down]),
        jnp.concatenate([came[:cut], came_down]),
        total[DEEP:],
        came[cut:],
    )
    return outputs, grad_states, *finish(meta, (sums0, (*sums1, *sums_attn1)), rows, width)


def solution(mesh):
    rows = P(None, LINES, None)
    tokens = P("dp", "seq", None)
    gain = P(None, LINES)
    return jax.shard_map(
        per_device,
        mesh=mesh,
        in_specs=(tokens, P("dp"), gain, rows, rows, gain, rows, rows, tokens),
        out_specs=(tokens, tokens, gain, rows, rows, gain, rows, rows),
        check_vma=False,
    )
```
